32 devices in a mesh: ctx: 8 (over y, x, core), wt: 4 (over z).
Axes of the slice: x: 2, y: 2, z: 4, core: 2. Of those that a mesh axis runs over, the one named last changes fastest.
Arguments:
- tokens: bfloat16 [4, 2560, 1152], P('wt', 'ctx'), may hold values from -6 to 6
- assign: int32 [4, 8], P('wt'), may hold values from 0 to 7, each once within a row
- cotangent: bfloat16 [4, 2560, 1152], P('wt', 'ctx'), may hold values from -6 to 6
- attn_gain: bfloat16 [2, 1152], P(None, 'wt'), may hold values from 0.5 to 1.5
- w_query: bfloat16 [2, 1152, 1152], P(None, 'wt'), may hold values from -0.1875 to 0.1875
- w_key: bfloat16 [2, 1152, 384], P(None, 'wt'), may hold values from -0.1875 to 0.1875
- w_value: bfloat16 [2, 1152, 384], P(None, 'wt'), may hold values from -0.1875 to 0.1875
- w_out: bfloat16 [2, 1152, 1152], P(None, 'wt'), may hold values from -4 to 4
- mlp_gain: bfloat16 [2, 1152], P(None, 'wt'), may hold values from 0.5 to 1.5
- w_gate: bfloat16 [2, 1152, 3072], P(None, 'wt'), may hold values from -0.1875 to 0.1875
- w_up: bfloat16 [2, 1152, 3072], P(None, 'wt'), may hold values from -0.1875 to 0.1875
- w_down: bfloat16 [2, 3072, 1152], P(None, 'wt'), may hold values from -0.109375 to 0.109375
Outputs:
- layer_out: float32 [4, 2560, 1152], P('wt', 'ctx')
- token_grad: float32 [4, 2560, 1152], P('wt', 'ctx')
- attn_gain_grad: float32 [2, 1152], P(None, 'wt')
- w_query_grad: float32 [2, 1152, 1152], P(None, 'wt')
- w_key_grad: float32 [2, 1152, 384], P(None, 'wt')
- w_value_grad: float32 [2, 1152, 384], P(None, 'wt')
- w_out_grad: float32 [2, 1152, 1152], P(None, 'wt')
- mlp_gain_grad: float32 [2, 1152], P(None, 'wt')
- w_gate_grad: float32 [2, 1152, 3072], P(None, 'wt')
- w_up_grad: float32 [2, 1152, 3072], P(None, 'wt')
- w_down_grad: float32 [2, 3072, 1152], P(None, 'wt')
The draws below stay inside these ranges and needn't reach their ends.
Inputs may be any that keep to these rules, and one draw needn't show every extreme that they name: Each row names every index of ctx once; ctx index c of group g holds prompt blocks assign[g, c] and 15 - assign[g, c], block b being prompt positions b * 32 to (b + 1) * 32 - 1.
All inputs are finite; a program needn't handle non-finite values.
Results may differ from the reference program's by a relative error of at most 0.025.
Values may be sent and summed in bfloat16 or wider, within the bound.
No kernel may reach another device: no remote copies, remote signals or barrier semaphores. Data moves between devices by JAX's collectives and lax.ppermute only.
A program may use at most 448 MiB of HBM per device.

```python
import jax
import jax.numpy as jnp
from jax import lax

D = 1152
HEADS = 18
KV_HEADS = 6
HEAD_DIM = 64
FF = 3072
LAYERS = 2
HALF = 32
CONT = 256
GROUPS = 4
TOKENS_GROUP = 2560
Q = 1152
KV = 384
N_CTX = 8


def block_levels(stream_key, shape, cuts, low, largest):
    level, own = 1.0, jax.random.fold_in(stream_key, 6)
    for dim, parts in cuts:
        draws = jnp.exp(jax.random.uniform(jax.random.fold_in(own, dim), (parts,), jnp.float32, low / len(cuts), largest / len(cuts)))
        level = level * jnp.repeat(draws, shape[dim] // parts).reshape([-1 if axis == dim else 1 for axis in range(len(shape))])
    return level


def scatter_about(stream_key, shape, spread, reach, cuts=(), kind=jnp.bfloat16):
    factor_of = block_levels(stream_key, shape, cuts, -0.22, 0.18) if cuts else 1.0
    values = jax.random.normal(stream_key, shape, jnp.float32) * spread * factor_of
    return jnp.minimum(jnp.maximum(values, -reach), reach).astype(kind)


def setup_inputs(seed: int = 0) -> dict:
    seeds = jax.random.split(jax.random.key(seed), 13)
    return {
        "tokens": scatter_about(seeds[0], (GROUPS, TOKENS_GROUP, D), 1.0, 6.0, ((0, 4), (1, 8))),
        "assign": jax.vmap(lambda own: jax.random.permutation(own, N_CTX))(jax.random.split(seeds[1], GROUPS)).reshape((GROUPS, N_CTX)).astype(jnp.int32),
        "cotangent": scatter_about(seeds[2], (GROUPS, TOKENS_GROUP, D), 1.0, 6.0, ((0, 4), (1, 8))),
        "attn_gain": jnp.clip(1.0 + 0.1 * jax.random.normal(seeds[3], (LAYERS, D), jnp.float32), 0.5, 1.5).astype(jnp.bfloat16),
        "w_query": scatter_about(seeds[4], (LAYERS, D, Q), D ** -0.5, 0.1875, ((1, 4),)),
        "w_key": scatter_about(seeds[5], (LAYERS, D, KV), D ** -0.5, 0.1875, ((1, 4),)),
        "w_value": scatter_about(seeds[6], (LAYERS, D, KV), D ** -0.5, 0.1875, ((1, 4),)),
        "w_out": scatter_about(seeds[7], (LAYERS, Q, D), 2 ** -0.5, 4.0, ((1, 4),)),
        "mlp_gain": jnp.clip(1.0 + 0.1 * jax.random.normal(seeds[8], (LAYERS, D), jnp.float32), 0.5, 1.5).astype(jnp.bfloat16),
        "w_gate": scatter_about(seeds[9], (LAYERS, D, FF), D ** -0.5, 0.1875, ((1, 4),)),
        "w_up": scatter_about(seeds[10], (LAYERS, D, FF), D ** -0.5, 0.1875, ((1, 4),)),
        "w_down": scatter_about(seeds[11], (LAYERS, FF, D), FF ** -0.5, 0.109375, ((1, 4),)),
    }


EPSILON = 1e-05
SCORE_SCALE = 0.125
HIGHEST = lax.Precision.HIGHEST
MASKED = -1e+30

@jax.custom_vjp
def low(v):
    return lax.optimization_barrier(v.astype(jnp.bfloat16)).astype(jnp.float32)

@jax.custom_vjp
def low_back(v):
    return v

def low_keep(v):
    return (low(v), None)

def low_pass(kept, grad):
    return (grad,)

def back_keep(v):
    return (v, None)

def back_low(kept, grad):
    return (low(grad),)
low.defvjp(low_keep, low_pass)
low_back.defvjp(back_keep, back_low)

def matmul_high(left, right):
    return jnp.matmul(left, right, precision=HIGHEST)

def normed(value, gain_vec):
    return value * lax.rsqrt(lax.optimization_barrier(jnp.mean(value * value, axis=-1, keepdims=True)) + EPSILON) * gain_vec

def positions(deal_row, ctx_count):
    row_ids = jnp.arange(2 * HALF + CONT, dtype=jnp.int32)
    block_ids = deal_row[..., None].astype(jnp.int32)
    lower_block = block_ids * HALF + row_ids
    upper_block = (2 * ctx_count - 1 - block_ids) * HALF + row_ids - HALF
    continued = 2 * HALF * ctx_count + row_ids - 2 * HALF
    return jnp.where(row_ids < HALF, lower_block, jnp.where(row_ids < 2 * HALF, upper_block, continued)).astype(jnp.int32)

def angles(position):
    half_dim = HEAD_DIM // 2
    frequency = jnp.exp(jnp.arange(half_dim, dtype=jnp.float32) * (-jnp.log(10000.0) / half_dim))
    phase_angle = position.astype(jnp.float32)[..., None] * frequency
    return (jnp.cos(phase_angle), jnp.sin(phase_angle))

def rotate(value, cosine, sine):
    half_dim = value.shape[-1] // 2
    lower_half = value[..., :half_dim]
    upper_half = value[..., half_dim:]
    return jnp.concatenate([lower_half * cosine - upper_half * sine, upper_half * cosine + lower_half * sine], axis=-1)

def reference(tokens, assign, cotangent, attn_gain, w_query, w_key, w_value, w_out, mlp_gain, w_gate, w_up, w_down):
    ctx_count = N_CTX
    shared = HEADS // KV_HEADS
    tok_rows = 2 * HALF + CONT
    prompt_rows = 2 * HALF * ctx_count
    every_pos = positions(assign, ctx_count)
    prompt_pos = every_pos[:, :, :2 * HALF].reshape(GROUPS, prompt_rows)
    cos_t, sin_t = angles(every_pos)
    group_ids = (jnp.arange(GROUPS * ctx_count, dtype=jnp.int32) // ctx_count).astype(jnp.int32)
    flat_pos = every_pos.reshape(GROUPS * ctx_count, tok_rows)

    def layer_pass(residual, params):
        gain_attn, query_w, key_w, value_w, out_w, gain_mlp, gate_w, up_w, down_w = params
        normed_attn = low(normed(residual, gain_attn))
        query_pre = low_back(matmul_high(normed_attn, query_w)).reshape(GROUPS, ctx_count, tok_rows, KV_HEADS, shared, HEAD_DIM)
        key_pre = low_back(matmul_high(normed_attn, key_w)).reshape(GROUPS, ctx_count, tok_rows, KV_HEADS, HEAD_DIM)
        values = low(low_back(matmul_high(normed_attn, value_w))).reshape(GROUPS, ctx_count, tok_rows, KV_HEADS, HEAD_DIM)
        queries = low(rotate(query_pre, cos_t[:, :, :, None, None], sin_t[:, :, :, None, None]))
        keys = low(rotate(key_pre, cos_t[:, :, :, None], sin_t[:, :, :, None]))
        prompt_key = keys[:, :, :2 * HALF].reshape(GROUPS, prompt_rows, KV_HEADS, HEAD_DIM)
        prompt_value = values[:, :, :2 * HALF].reshape(GROUPS, prompt_rows, KV_HEADS, HEAD_DIM)

        def attend(block_item):
            query_block, cont_key, cont_value, query_pos, group_index = block_item
            all_keys = jnp.concatenate([lax.dynamic_index_in_dim(prompt_key, group_index, 0, keepdims=False), cont_key], axis=0)
            all_values = jnp.concatenate([lax.dynamic_index_in_dim(prompt_value, group_index, 0, keepdims=False), cont_value], axis=0)
            key_pos = jnp.concatenate([lax.dynamic_index_in_dim(prompt_pos, group_index, 0, keepdims=False), query_pos[2 * HALF:]], axis=0)
            scores = low_back(jnp.einsum('tkgd,skd->kgts', query_block, all_keys, precision=HIGHEST) * SCORE_SCALE)
            scores = jnp.where(key_pos[None, :] <= query_pos[:, None], scores, MASKED)
            row_max = lax.optimization_barrier(jnp.max(scores, axis=-1, keepdims=True))
            log_total = row_max + jnp.log(lax.optimization_barrier(jnp.sum(jnp.exp(scores - row_max), axis=-1, keepdims=True)))
            softmax_p = low(jnp.exp(scores - log_total))
            return jnp.einsum('kgts,skd->tkgd', softmax_p, all_values, precision=HIGHEST)
        attended = lax.map(jax.checkpoint(attend), (queries.reshape(GROUPS * ctx_count, tok_rows, KV_HEADS, shared, HEAD_DIM), keys[:, :, 2 * HALF:].reshape(GROUPS * ctx_count, CONT, KV_HEADS, HEAD_DIM), values[:, :, 2 * HALF:].reshape(GROUPS * ctx_count, CONT, KV_HEADS, HEAD_DIM), flat_pos, group_ids))
        attended = low(low_back(attended.reshape(GROUPS, ctx_count, tok_rows, HEADS * HEAD_DIM)))
        residual_mid = residual + low_back(matmul_high(attended, out_w))
        normed_mlp = low(normed(residual_mid, gain_mlp))
        gate_pre = low_back(matmul_high(normed_mlp, gate_w))
        up_pre = low_back(matmul_high(normed_mlp, up_w))
        swish_out = low(jax.nn.silu(gate_pre) * up_pre)
        return residual_mid + low_back(matmul_high(swish_out, down_w))

    def forward(inputs, *params):
        residual = inputs
        for layer_index in range(LAYERS):
            residual = layer_pass(residual, tuple((param[layer_index] for param in params)))
        return residual
    inputs = tokens.astype(jnp.float32).reshape(GROUPS, ctx_count, tok_rows, D)
    weights = tuple((weight_arg.astype(jnp.float32) for weight_arg in (attn_gain, w_query, w_key, w_value, w_out, mlp_gain, w_gate, w_up, w_down)))
    result, pullback = jax.vjp(forward, inputs, *weights)
    grads = pullback(cotangent.astype(jnp.float32).reshape(inputs.shape))
    whole = (GROUPS, ctx_count * tok_rows, D)
    return (result.reshape(whole), grads[0].reshape(whole), grads[1], grads[2], grads[3], grads[4], grads[5], grads[6], grads[7], grads[8], grads[9])
```

```python
import functools
import math

import jax
import jax.numpy as jnp
from jax import lax
from jax.experimental import pallas as pl
from jax.experimental.pallas import tpu as pltpu
from jax.sharding import PartitionSpec as P

HEADS = 18
KV_HEADS = 6
HEAD_DIM = 64
HALF = 32
CONT = 256
SHARED = HEADS // KV_HEADS
PAIR_KV = KV_HEADS // 2
PAIR_HEADS = HEADS // 2
RUN = 2 * HALF + CONT
ROWS = 2 * RUN
PROMPT = 4 * HALF
TAIL = 2 * CONT

EPSILON = 1e-05
SCORE_SCALE = 0.125
BASE_TWO = SCORE_SCALE * math.log2(math.e)
MASKED = -1e30

BF16 = jnp.bfloat16
F32 = jnp.float32

PAIR, SIDE, ROW = 1, 2, 4


def dot_nn(left, right):
    return lax.dot_general(left, right, (((1,), (0,)), ((), ())), preferred_element_type=F32)


def dot_nt(left, right):
    return lax.dot_general(left, right, (((1,), (1,)), ((), ())), preferred_element_type=F32)


def dot_tn(left, right):
    return lax.dot_general(left, right, (((0,), (0,)), ((), ())), preferred_element_type=F32)


def dot_tt(left, right):
    return lax.dot_general(left, right, (((0,), (1,)), ((), ())), preferred_element_type=F32)


def turned(value):
    return jnp.transpose(value.astype(F32))


def shaped(shape, dtype):
    return jax.ShapeDtypeStruct(shape, dtype)


WHOLE = pl.BlockSpec(memory_space=pltpu.VMEM)
FAR = pl.BlockSpec(memory_space=pl.ANY)
SCALARS = pl.BlockSpec(memory_space=pltpu.SMEM)


def call(kernel, outs, ins, flops, limit, out_specs=None, in_specs=None, **extra):
    moved = sum(math.prod(v.shape) * v.dtype.itemsize for v in (*ins, *outs))
    return pl.pallas_call(
        kernel,
        out_shape=outs,
        in_specs=in_specs or [WHOLE] * len(ins),
        out_specs=out_specs or [WHOLE] * len(outs),
        compiler_params=pltpu.CompilerParams(vmem_limit_bytes=limit << 20),
        cost_estimate=pl.CostEstimate(flops=flops, bytes_accessed=moved, transcendentals=0),
        **extra,
    )(*ins)


def add_norm_kernel(has_parts, *refs):
    if has_parts:
        held, mine, other, gain, total_ref, normed_ref = refs
        total = held[...] + (mine[...].astype(F32) + other[...].astype(F32))
        total_ref[...] = total
    else:
        held, gain, normed_ref = refs
        total = held[...]
    inverse = lax.rsqrt(jnp.mean(total * total, axis=-1, keepdims=True) + EPSILON)
    normed_ref[...] = (total * inverse * gain[...]).astype(BF16)


def add_norm(held, parts, gain):
    rows, width = held.shape
    step = 128
    block = pl.BlockSpec((step, width), lambda i: (i, 0))
    line = pl.BlockSpec((1, width), lambda i: (0, 0))
    ins = (held, *parts, gain)
    outs = ([shaped(held.shape, F32)] if parts else []) + [shaped(held.shape, BF16)]
    result = call(
        functools.partial(add_norm_kernel, bool(parts)),
        outs,
        ins,
        0,
        16,
        in_specs=[block] * (1 + len(parts)) + [line],
        out_specs=[block] * len(outs),
        grid=(rows // step,),
    )
    return result if parts else (held, result[0])


def norm_back_kernel(flow, mine, other, held, gain, flow_ref, low_ref, gain_ref):
    grad = mine[...].astype(F32) + other[...].astype(F32)
    value = held[...]
    inverse = lax.rsqrt(jnp.mean(value * value, axis=-1, keepdims=True) + EPSILON)
    plain = value * inverse
    scaled = grad * gain[...]
    tilt = jnp.mean(scaled * plain, axis=-1, keepdims=True)
    total = flow[...] + inverse * (scaled - plain * tilt)
    flow_ref[...] = total
    low_ref[...] = total.astype(BF16)

    @pl.when(pl.program_id(0) == 0)
    def _():
        gain_ref[...] = jnp.zeros_like(gain_ref)

    gain_ref[...] += jnp.sum(grad * plain, axis=0, keepdims=True)


def norm_back(flow, parts, held, gain):
    rows, width = held.shape
    step = 128
    block = pl.BlockSpec((step, width), lambda i: (i, 0))
    line = pl.BlockSpec((1, width), lambda i: (0, 0))
    return call(
        norm_back_kernel,
        [shaped(held.shape, F32), shaped(held.shape, BF16), shaped((1, width), F32)],
        (flow, *parts, held, gain),
        0,
        16,
        in_specs=[block] * 4 + [line],
        out_specs=[block, block, line],
        grid=(rows // step,),
    )


KEY_HALF = PAIR_KV * HEAD_DIM
QUERY_HALF = PAIR_HEADS * HEAD_DIM
QKV = 2 * KEY_HALF + QUERY_HALF


def rope_kernel(qkv_ref, cos_ref, sin_ref, query_ref, kv_ref, kv_turned_ref):
    cosine, sine = cos_ref[...], sin_ref[...]
    half = HEAD_DIM // 2

    def head(source, target_ref, target):
        low = qkv_ref[source : source + half, :]
        high = qkv_ref[source + half : source + 2 * half, :]
        target_ref[target : target + half, :] = (low * cosine - high * sine).astype(BF16)
        target_ref[target + half : target + 2 * half, :] = (high * cosine + low * sine).astype(
            BF16
        )

    for index in range(PAIR_KV):
        head(index * HEAD_DIM, kv_turned_ref, index * HEAD_DIM)
    kv_turned_ref[KEY_HALF:, :] = qkv_ref[KEY_HALF : 2 * KEY_HALF, :].astype(BF16)
    kv_ref[...] = turned(kv_turned_ref[...]).astype(BF16)
    for index in range(PAIR_HEADS):
        head(2 * KEY_HALF + index * HEAD_DIM, query_ref, index * HEAD_DIM)


def rope(qkv, cosine, sine):
    return call(
        rope_kernel,
        [
            shaped((QUERY_HALF, ROWS), BF16),
            shaped((ROWS, 2 * KEY_HALF), BF16),
            shaped((2 * KEY_HALF, ROWS), BF16),
        ],
        (qkv, cosine, sine),
        0,
        32,
    )


def later_mask():
    key = lax.broadcasted_iota(jnp.int32, (CONT, CONT), 0)
    query = lax.broadcasted_iota(jnp.int32, (CONT, CONT), 1)
    return key <= query


def attend_kernel(
    query_ref, kv_ref, kv_turned_ref, shared_ref, key_pos_ref, row_pos_ref, out_ref, lse_ref
):
    shared_values = turned(shared_ref[:, KEY_HALF:]).astype(BF16)
    for kv_head in range(PAIR_KV):
        low = kv_head * HEAD_DIM
        keys = shared_ref[:, low : low + HEAD_DIM]
        values = shared_values[low : low + HEAD_DIM, :]

        def head(index, carry, kv_head=kv_head, low=low, keys=keys, values=values):
            number = kv_head * SHARED + index
            base = pl.multiple_of(number * HEAD_DIM, HEAD_DIM)
            allowed = key_pos_ref[...] <= row_pos_ref[...]
            query = query_ref[pl.ds(base, HEAD_DIM), TAIL:]
            scores = jnp.where(allowed, dot_nn(keys, query) * BASE_TWO, MASKED)
            top = jnp.max(scores, axis=0, keepdims=True)
            weight = jnp.exp2(scores - top)
            total = jnp.sum(weight, axis=0, keepdims=True)
            out = dot_nn(values, weight.astype(BF16)) / total
            out_ref[pl.ds(base, HEAD_DIM), TAIL:] = out.astype(BF16)
            lse_ref[number, :, TAIL:] = top + jnp.log2(total)
            for run in range(2):
                cols = slice(run * CONT, (run + 1) * CONT)
                query = query_ref[pl.ds(base, HEAD_DIM), cols]
                own_keys = kv_ref[cols, low : low + HEAD_DIM]
                own_values = kv_turned_ref[KEY_HALF + low : KEY_HALF + low + HEAD_DIM, cols]
                first = dot_nn(keys, query) * BASE_TWO
                second = jnp.where(later_mask(), dot_nn(own_keys, query) * BASE_TWO, MASKED)
                top = jnp.maximum(
                    jnp.max(first, axis=0, keepdims=True), jnp.max(second, axis=0, keepdims=True)
                )
                first = jnp.exp2(first - top)
                second = jnp.exp2(second - top)
                total = jnp.sum(first, axis=0, keepdims=True) + jnp.sum(
                    second, axis=0, keepdims=True
                )
                out = dot_nn(values, first.astype(BF16)) + dot_nn(
                    own_values, second.astype(BF16)
                )
                out_ref[pl.ds(base, HEAD_DIM), cols] = (out / total).astype(BF16)
                lse_ref[number, :, cols] = top + jnp.log2(total)
            return carry

        lax.fori_loop(0, SHARED, head, 0)


def attend(query, key_value, key_value_turned, shared, key_pos, row_pos):
    flops = 4 * QUERY_HALF * ROWS * (shared.shape[0] + CONT)
    return call(
        attend_kernel,
        [shaped((QUERY_HALF, ROWS), BF16), shaped((PAIR_HEADS, 1, ROWS), F32)],
        (query, key_value, key_value_turned, shared, key_pos, row_pos),
        flops,
        48,
    )


def attend_back_kernel(
    query_ref,
    grad_ref,
    kv_ref,
    kv_turned_ref,
    shared_ref,
    key_pos_ref,
    row_pos_ref,
    lse_ref,
    cos_ref,
    sin_ref,
    query_grad_ref,
    own_grad_ref,
    shared_grad_ref,
    score_keep,
    weight_keep,
    own_score_keep,
    own_weight_keep,
):
    shared_turned = turned(shared_ref[:, :KEY_HALF]).astype(BF16)
    half = HEAD_DIM // 2
    for kv_head in range(PAIR_KV):
        low = kv_head * HEAD_DIM
        keys = shared_ref[:, low : low + HEAD_DIM]
        values = shared_ref[:, KEY_HALF + low : KEY_HALF + low + HEAD_DIM]
        keys_turned = shared_turned[low : low + HEAD_DIM, :]

        def head(index, carry, kv_head=kv_head, low=low, keys=keys, values=values, keys_turned=keys_turned):
            number = kv_head * SHARED + index
            base = pl.multiple_of(number * HEAD_DIM, HEAD_DIM)

            def put_query_grad(grad, cols):
                cosine, sine = cos_ref[:, cols], sin_ref[:, cols]
                first, second = grad[:half], grad[half:]
                query_grad_ref[pl.ds(base, half), cols] = (
                    (first * cosine + second * sine) * SCORE_SCALE
                ).astype(BF16)
                query_grad_ref[pl.ds(base + half, half), cols] = (
                    (second * cosine - first * sine) * SCORE_SCALE
                ).astype(BF16)

            cols = slice(TAIL, ROWS)
            query = query_ref[pl.ds(base, HEAD_DIM), cols]
            grad = grad_ref[pl.ds(base, HEAD_DIM), cols]
            lse = lse_ref[number, :, cols]
            allowed = key_pos_ref[...] <= row_pos_ref[...]
            scores = jnp.where(allowed, dot_nn(keys, query) * BASE_TWO, MASKED)
            weight = jnp.exp2(scores - lse)
            weight_keep[index, :, cols] = weight.astype(BF16)
            flow = weight * dot_nn(values, grad)
            delta = jnp.sum(flow, axis=0, keepdims=True)
            flow = (flow - weight * delta).astype(BF16)
            score_keep[index, :, cols] = flow
            put_query_grad(dot_nn(keys_turned, flow), cols)
            for run in range(2):
                cols = slice(run * CONT, (run + 1) * CONT)
                query = query_ref[pl.ds(base, HEAD_DIM), cols]
                grad = grad_ref[pl.ds(base, HEAD_DIM), cols]
                lse = lse_ref[number, :, cols]
                own_keys = kv_ref[cols, low : low + HEAD_DIM]
                own_values = kv_ref[cols, KEY_HALF + low : KEY_HALF + low + HEAD_DIM]
                own_turned = kv_turned_ref[low : low + HEAD_DIM, cols]
                first = jnp.exp2(dot_nn(keys, query) * BASE_TWO - lse)
                second = jnp.where(later_mask(), dot_nn(own_keys, query) * BASE_TWO, MASKED)
                second = jnp.exp2(second - lse)
                weight_keep[index, :, cols] = first.astype(BF16)
                own_weight_keep[index, :, cols] = second.astype(BF16)
                first_flow = first * dot_nn(values, grad)
                second_flow = second * dot_nn(own_values, grad)
                delta = jnp.sum(first_flow, axis=0, keepdims=True) + jnp.sum(
                    second_flow, axis=0, keepdims=True
                )
                first_flow = (first_flow - first * delta).astype(BF16)
                second_flow = (second_flow - second * delta).astype(BF16)
                score_keep[index, :, cols] = first_flow
                own_score_keep[index, :, cols] = second_flow
                put_query_grad(
                    dot_nn(keys_turned, first_flow) + dot_nn(own_turned, second_flow), cols
                )
            return carry

        lax.fori_loop(0, SHARED, head, 0)
        key_sum, value_sum = 0.0, 0.0
        own_key_sum, own_value_sum = [0.0, 0.0], [0.0, 0.0]
        for index in range(SHARED):
            base = (kv_head * SHARED + index) * HEAD_DIM
            query = query_ref[base : base + HEAD_DIM, :]
            grad = grad_ref[base : base + HEAD_DIM, :]
            key_sum = key_sum + dot_nt(score_keep[index], query)
            value_sum = value_sum + dot_nt(weight_keep[index], grad)
            for run in range(2):
                cols = slice(run * CONT, (run + 1) * CONT)
                own_key_sum[run] = own_key_sum[run] + dot_nt(
                    own_score_keep[index, :, cols], query[:, cols]
                )
                own_value_sum[run] = own_value_sum[run] + dot_nt(
                    own_weight_keep[index, :, cols], grad[:, cols]
                )
        shared_grad_ref[:, low : low + HEAD_DIM] = key_sum * SCORE_SCALE
        shared_grad_ref[:, KEY_HALF + low : KEY_HALF + low + HEAD_DIM] = value_sum
        for run in range(2):
            cols = slice(run * CONT, (run + 1) * CONT)
            own_grad_ref[cols, low : low + HEAD_DIM] = own_key_sum[run] * SCORE_SCALE
            own_grad_ref[cols, KEY_HALF + low : KEY_HALF + low + HEAD_DIM] = own_value_sum[run]


def attend_back(query, grad, key_value, key_value_turned, shared, key_pos, row_pos, lse, cosine, sine):
    count = shared.shape[0]
    flops = 10 * QUERY_HALF * ROWS * (count + CONT)
    return call(
        attend_back_kernel,
        [
            shaped((QUERY_HALF, ROWS), BF16),
            shaped((TAIL, 2 * KEY_HALF), F32),
            shaped((count, 2 * KEY_HALF), F32),
        ],
        (query, grad, key_value, key_value_turned, shared, key_pos, row_pos, lse, cosine, sine),
        flops,
        56,
        scratch_shapes=[
            pltpu.VMEM((SHARED, count, ROWS), BF16),
            pltpu.VMEM((SHARED, count, ROWS), BF16),
            pltpu.VMEM((SHARED, CONT, TAIL), BF16),
            pltpu.VMEM((SHARED, CONT, TAIL), BF16),
        ],
    )


def merge_kernel(query_grad_ref, own_ref, prompt_ref, cos_ref, sin_ref, out_ref):
    cosine, sine = cos_ref[...], sin_ref[...]
    half = HEAD_DIM // 2
    both = turned(jnp.concatenate([own_ref[...], prompt_ref[...]], axis=0))
    pieces = []
    for index in range(PAIR_KV):
        low = both[index * HEAD_DIM : index * HEAD_DIM + half]
        high = both[index * HEAD_DIM + half : (index + 1) * HEAD_DIM]
        pieces += [low * cosine + high * sine, high * cosine - low * sine]
    both = jnp.concatenate(pieces + [both[KEY_HALF:]], axis=0)
    out_ref[:, : 2 * KEY_HALF] = jnp.transpose(both).astype(BF16)
    out_ref[:, 2 * KEY_HALF :] = turned(query_grad_ref[...]).astype(BF16)


def merge(query_grad, own_grad, prompt_grad, cosine, sine):
    return call(
        merge_kernel,
        [shaped((ROWS, QKV), BF16)],
        (query_grad, own_grad, prompt_grad, cosine, sine),
        0,
        32,
    )[0]


def weight_copies(pieces, target, sems, block, depth):
    if block < 3:
        return [
            pltpu.make_async_copy(
                pieces[block].at[:, : 2 * block_of(target)], target.at[block], sems.at[block]
            )
        ]
    half = depth // 2
    return [
        pltpu.make_async_copy(
            pieces[3 + part].at[:, : 2 * block_of(target)],
            target.at[3, pl.ds(part * half, half)],
            sems.at[3 + part],
        )
        for part in range(2)
    ]


def block_of(target):
    return target.shape[2] // 2


def mlp_kernel(
    quarter_ref, normed_ref, *refs
):
    pieces = refs[:5]
    down_ref, slope_ref, scale_ref, unit_ref, out_ref = refs[5:10]
    held, sems, down_sem = refs[10:]
    rows, depth = normed_ref.shape
    width = depth
    block = block_of(held)
    shard = depth // 4
    lines = block // 4
    wide = width // 3
    quarter = quarter_ref[0]
    copies = [weight_copies(pieces, held, sems, part, depth) for part in range(4)]
    for part in range(4):
        for copy in copies[part]:
            copy.start()
    for place in range(4):
        plane = quarter ^ place
        for part in range(4):
            target_row = pl.multiple_of(place * block + lines * (quarter ^ part), lines)
            for column in range(3):
                target = down_ref.at[
                    pl.ds(target_row, lines), column * wide : (column + 1) * wide
                ]
                taken = slice(2 * block, 2 * block + wide)
                if part < 3:
                    start = pl.multiple_of(shard * plane + lines * column, lines)
                    pltpu.make_async_copy(
                        pieces[part].at[pl.ds(start, lines), taken], target, down_sem
                    ).start()
                else:
                    inner = plane % 2
                    start = pl.multiple_of(shard * inner + lines * column, lines)
                    for half in range(2):

                        @pl.when(plane // 2 == half)
                        def _(half=half, start=start, target=target, taken=taken):
                            pltpu.make_async_copy(
                                pieces[3 + half].at[pl.ds(start, lines), taken], target, down_sem
                            ).start()

    step = rows // 2
    for part in range(4):
        for copy in copies[part]:
            copy.wait()

        def tile(index, carry, part=part):
            at = pl.ds(pl.multiple_of(index * step, step), step)
            normed = normed_ref[at, :]
            gate = dot_nn(normed, held[part, :, :block])
            up = dot_nn(normed, held[part, :, block:])
            sigmoid = 1.0 / (1.0 + jnp.exp(-gate))
            scale = gate * sigmoid
            cols = slice(part * block, (part + 1) * block)
            slope_ref[at, cols] = (up * sigmoid * (1.0 + gate * (1.0 - sigmoid))).astype(BF16)
            scale_ref[at, cols] = scale.astype(BF16)
            unit_ref[at, cols] = (scale * up).astype(BF16)
            return carry

        lax.fori_loop(0, 2, tile, 0)
    pltpu.make_async_copy(down_ref, down_ref, down_sem).wait()

    def finish(index, carry):
        at = pl.ds(pl.multiple_of(index * step, step), step)
        out_ref[at, :] = dot_nn(unit_ref[at, :], down_ref[...]).astype(BF16)
        return carry

    lax.fori_loop(0, 2, finish, 0)


def mlp(quarter, normed, pieces, block):
    rows, depth = normed.shape
    units = 4 * block
    return call(
        mlp_kernel,
        [
            shaped((units, depth), BF16),
            shaped((rows, units), BF16),
            shaped((rows, units), BF16),
            shaped((rows, units), BF16),
            shaped((rows, depth), BF16),
        ],
        (quarter, normed, *pieces),
        6 * rows * depth * units,
        56,
        in_specs=[SCALARS, WHOLE] + [FAR] * 5,
        scratch_shapes=[
            pltpu.VMEM((4, depth, 2 * block), BF16),
            pltpu.SemaphoreType.DMA((5,)),
            pltpu.SemaphoreType.DMA,
        ],
    )


def down_grad_kernel(where_ref, unit_ref, flow_ref, keep_ref, send_ref):
    quarter, row = where_ref[0], where_ref[1]
    block = unit_ref.shape[1] // 4
    half = block // 2
    for place in range(4):
        plane = quarter ^ place
        total = dot_tn(unit_ref[:, place * block : (place + 1) * block], flow_ref[...]).astype(
            BF16
        )
        for index in range(2):
            part = total[index * half : (index + 1) * half]

            @pl.when(row == index)
            def _(part=part, plane=plane):
                keep_ref[plane] = part

            @pl.when(row != index)
            def _(part=part, plane=plane):
                send_ref[plane] = part


def down_grad(where, unit, flow):
    rows, units = unit.shape
    width = flow.shape[1]
    half = units // 8
    return call(
        down_grad_kernel,
        [shaped((4, half, width), BF16)] * 2,
        (where, unit, flow),
        2 * rows * units * width,
        48,
        in_specs=[SCALARS, WHOLE, WHOLE],
    )


def mlp_back_kernel(flow_ref, normed_ref, slope_ref, scale_ref, down_ref, *refs):
    pieces = refs[:5]
    keep_ref, send_ref, out_ref = refs[5:8]
    held, total, unit_grad, sems = refs[8:]
    rows, depth = normed_ref.shape
    block = block_of(held)
    order = (2, 3, 0, 1)
    copies = [weight_copies(pieces, held, sems, part, depth) for part in range(4)]
    for part in order:
        for copy in copies[part]:
            copy.start()
    step = rows // 2
    for part in order:
        cols = slice(part * block, (part + 1) * block)

        def tile(index, carry, cols=cols):
            at = pl.ds(pl.multiple_of(index * step, step), step)
            grad = dot_nt(flow_ref[at, :], down_ref[cols, :])
            unit_grad[at, :block] = (grad * slope_ref[at, cols].astype(F32)).astype(BF16)
            unit_grad[at, block:] = (grad * scale_ref[at, cols].astype(F32)).astype(BF16)
            return carry

        lax.fori_loop(0, 2, tile, 0)
        target = send_ref if part >= 2 else keep_ref
        side = slice((part % 2) * 2 * block, (part % 2 + 1) * 2 * block)
        target[:, side] = dot_tn(normed_ref[...], unit_grad[...]).astype(BF16)
        for copy in copies[part]:
            copy.wait()

        def gather(index, carry, part=part):
            at = pl.ds(pl.multiple_of(index * step, step), step)
            value = dot_nt(unit_grad[at, :], held[part])
            if part == order[0]:
                total[at, :] = value
            elif part == order[-1]:
                out_ref[at, :] = (total[at, :] + value).astype(BF16)
            else:
                total[at, :] += value
            return carry

        lax.fori_loop(0, 2, gather, 0)


def mlp_back(flow, normed, slope, scale, down, pieces):
    rows, depth = normed.shape
    block = down.shape[0] // 4
    return call(
        mlp_back_kernel,
        [
            shaped((depth, 4 * block), BF16),
            shaped((depth, 4 * block), BF16),
            shaped((rows, depth), BF16),
        ],
        (flow, normed, slope, scale, down, *pieces),
        10 * rows * depth * 4 * block,
        60,
        in_specs=[WHOLE] * 5 + [FAR] * 5,
        scratch_shapes=[
            pltpu.VMEM((4, depth, 2 * block), BF16),
            pltpu.VMEM((rows, depth), F32),
            pltpu.VMEM((rows, 2 * block), BF16),
            pltpu.SemaphoreType.DMA((5,)),
        ],
    )


def place_kernel(fresh, where_ref, *refs):
    parts = refs[:6]
    outs = refs[6:] if fresh else refs[13:]
    pair, quarter = where_ref[0], where_ref[1]
    ff_mine, ff_other, down_mine, down_other, attn_mine, attn_other = parts
    query_out, key_out, value_out, out_out, gate_out, up_out, down_out = outs
    block = ff_mine.shape[2] // 4
    side, row = quarter // 2, quarter % 2
    for where_from, owner in ((ff_mine, pair), (ff_other, 1 - pair)):
        for index in range(2):
            for inner in range(2):
                plane = 2 * (side ^ index) + (row ^ inner)
                col = pl.multiple_of((2 * plane + owner) * block, block)
                low = 2 * inner * block
                gate_out[0, :, pl.ds(col, block)] = where_from[
                    index, :, low : low + block
                ].astype(F32)
                up_out[0, :, pl.ds(col, block)] = where_from[
                    index, :, low + block : low + 2 * block
                ].astype(F32)
    down_rows = down_mine.shape[0]
    for where_from, owner in ((down_mine, pair), (down_other, 1 - pair)):
        down_out[0, pl.ds(pl.multiple_of(owner * down_rows, down_rows), down_rows), :] = (
            where_from[...].astype(F32)
        )
    first = jnp.where(pair == 0, attn_mine[...], attn_other[...]).astype(F32)
    second = jnp.where(pair == 0, attn_other[...], attn_mine[...]).astype(F32)
    low = 0
    for out, cols in (
        (key_out, KEY_HALF),
        (value_out, KEY_HALF),
        (query_out, QUERY_HALF),
        (out_out, first.shape[1] - QKV),
    ):
        out[0] = jnp.concatenate([first[:, low : low + cols], second[:, low : low + cols]], axis=1)
        low += cols


def place(layer, where, parts, outs, held):
    ins = (where, *parts, *(held or ()))
    specs = [SCALARS] + [WHOLE] * len(parts) + [FAR] * len(held or ())

    def layer_block(out):
        return pl.BlockSpec((1, *out.shape[1:]), lambda _: (layer, 0, 0))

    aliases = {} if held is None else {1 + len(parts) + i: i for i in range(len(outs))}
    return call(
        functools.partial(place_kernel, held is None),
        outs,
        ins,
        0,
        60,
        in_specs=specs,
        out_specs=[layer_block(out) for out in outs],
        input_output_aliases=aliases,
        grid=(1,),
    )


def positions(deal_row, ctx_count):
    row_ids = jnp.arange(RUN, dtype=jnp.int32)
    block_ids = deal_row[..., None]
    lower_block = block_ids * HALF + row_ids
    upper_block = (2 * ctx_count - 1 - block_ids) * HALF + row_ids - HALF
    continued = 2 * HALF * ctx_count + row_ids - 2 * HALF
    return jnp.where(
        row_ids < HALF, lower_block, jnp.where(row_ids < 2 * HALF, upper_block, continued)
    )


def per_device(
    tokens,
    assign,
    cotangent,
    attn_gain,
    w_query,
    w_key,
    w_value,
    w_out,
    mlp_gain,
    w_gate,
    w_up,
    w_down,
):
    ctx_count = lax.axis_size("ctx")
    wt_count = lax.axis_size("wt")
    ctx_index = lax.axis_index("ctx")
    pair = ctx_index % 2
    side = (ctx_index // SIDE) % 2
    row = (ctx_index // ROW) % 2
    quarter = 2 * side + row
    chip = ctx_index // 2
    chip_count = ctx_count // 2
    outer_bits = [bit for bit in (8, 16, 32, 64, 128) if bit < ctx_count]

    layer_count, depth = attn_gain.shape[0], w_query.shape[1]
    width = w_out.shape[2]
    half_width = width // 2
    ff_block = w_down.shape[1] // 2
    ff_piece = ff_block // 4
    half_depth = depth // 2

    def flip(value, bit, axis="ctx", count=None):
        count = ctx_count if count is None else count
        return lax.ppermute(value, axis, [(i, i ^ bit) for i in range(count)])

    def ordered(bit_value, mine, other):
        first = jnp.where(bit_value == 0, mine, other)
        second = jnp.where(bit_value == 0, other, mine)
        return first, second

    def pair_rows(own):
        first, second = ordered(pair, own, flip(own, PAIR))
        cut = 2 * HALF
        return jnp.concatenate([first[cut:], second[cut:], first[:cut], second[:cut]], axis=0)

    def own_rows(both):
        return jnp.concatenate(
            [
                lax.dynamic_slice(both, (TAIL + 2 * HALF * pair, 0), (2 * HALF, width)),
                lax.dynamic_slice(both, (CONT * pair, 0), (CONT, width)),
            ],
            axis=0,
        )

    every_pos = positions(assign[0], ctx_count).reshape(chip_count, 2, RUN)
    wanted = chip ^ jnp.arange(chip_count, dtype=jnp.int32)
    picked = wanted[:, None] == jnp.arange(chip_count, dtype=jnp.int32)[None, :]
    prompt_pos = jnp.sum(
        jnp.where(picked[:, :, None, None], every_pos[None, :, :, : 2 * HALF], 0), axis=1
    )
    key_pos = prompt_pos.reshape(-1, 1)
    row_pos = prompt_pos[0].reshape(1, -1)
    cont_pos = every_pos[0, 0, 2 * HALF :]
    own_pos = jnp.concatenate([cont_pos, cont_pos, row_pos[0]])
    half_dim = HEAD_DIM // 2
    frequency = jnp.exp(jnp.arange(half_dim, dtype=F32) * (-jnp.log(10000.0) / half_dim))
    phase = frequency[:, None] * own_pos.astype(F32)[None, :]
    cosine, sine = jnp.cos(phase), jnp.sin(phase)

    gain_line = jnp.concatenate([attn_gain, mlp_gain]).reshape(1, -1)
    columns = QKV + half_width

    def attn_piece(layer):
        piece = jnp.concatenate(
            [
                lax.dynamic_slice(
                    weight[layer], (half_depth * row, cols * pair), (half_depth, cols)
                )
                for weight, cols in (
                    (w_key, KEY_HALF),
                    (w_value, KEY_HALF),
                    (w_query, QUERY_HALF),
                    (w_out, half_width),
                )
            ],
            axis=1,
        )
        if layer == 0:
            line = jnp.pad(gain_line, ((0, 15), (0, columns - gain_line.shape[1])))
            piece = jnp.concatenate([piece, line], axis=0)
        return piece

    def attn_weights(mine):
        other = flip(mine, ROW)
        mine, other = mine[:, :half_depth], other[:, :half_depth]
        first, second = ordered(row, mine, other)
        both = jnp.stack([first, second], axis=1).reshape(wt_count * depth, columns)
        qkv_w = both[:, :QKV]
        out_cols = both[:, QKV:]
        keep = lax.dynamic_slice(out_cols, (QUERY_HALF * pair, 0), (QUERY_HALF, half_width))
        send = lax.dynamic_slice(out_cols, (QUERY_HALF * (1 - pair), 0), (QUERY_HALF, half_width))
        out_w = jnp.concatenate(ordered(pair, keep, flip(send, PAIR)), axis=1)
        return qkv_w, out_w

    def mlp_piece(layer):
        col = 2 * ff_block * quarter + ff_block * pair
        low = ff_block * pair + ff_piece * quarter
        down = lax.dynamic_slice(w_down[layer], (low, 0), (ff_piece, width))
        wide = width // 3
        down = jnp.concatenate([down[:, i * wide : (i + 1) * wide] for i in range(3)], axis=0)
        return jnp.concatenate(
            [
                lax.dynamic_slice(w_gate[layer], (0, col), (depth, ff_block)),
                lax.dynamic_slice(w_up[layer], (0, col), (depth, ff_block)),
                down,
            ],
            axis=1,
        )

    def mlp_pieces(mine):
        half_rows = mine.shape[0] // 2
        by_row = flip(mine, ROW)
        by_side = flip(mine, SIDE)
        return (
            mine,
            by_row,
            by_side,
            flip(by_row[:half_rows], SIDE),
            flip(by_side[half_rows:], ROW),
        )

    where = jnp.stack([pair, quarter])
    spot = jnp.stack([quarter, row])
    quarter_id = quarter[None]

    residual = pair_rows(tokens[0]).astype(F32)
    parts = ()
    saved_layers = []
    gains = None
    for layer in range(layer_count):
        gathered = lax.all_gather(attn_piece(layer), "wt", axis=0, tiled=False)
        if layer == 0:
            lines = gathered[:, half_depth, : gain_line.shape[1]].astype(F32)
            gains = (
                lines.reshape(wt_count, 2 * layer_count, depth)
                .transpose(1, 0, 2)
                .reshape(2 * layer_count, 1, wt_count * depth)
            )
        qkv_w, out_w = attn_weights(gathered)
        pieces = mlp_pieces(lax.all_gather(mlp_piece(layer), "wt", axis=0, tiled=True))
        gain_attn, gain_mlp = gains[layer], gains[layer_count + layer]
        residual, normed_attn = add_norm(residual, parts, gain_attn)
        query, key_value, key_value_turned = rope(dot_tt(qkv_w, normed_attn), cosine, sine)
        shared = key_value[TAIL:]
        for bit in [SIDE, ROW] + outer_bits:
            shared = jnp.concatenate([shared, flip(shared, bit)], axis=0)
        attended, lse = attend(query, key_value, key_value_turned, shared, key_pos, row_pos)
        part = dot_tn(attended, out_w).astype(BF16)
        residual_mid, normed_mlp = add_norm(residual, (part, flip(part, PAIR)), gain_mlp)
        down_w, slope, scale, unit, part = mlp(quarter_id, normed_mlp, pieces, ff_block)
        parts = (part, flip(part, PAIR))
        saved_layers.append(
            (
                qkv_w,
                out_w,
                pieces,
                down_w,
                gain_attn,
                gain_mlp,
                residual,
                normed_attn,
                query,
                key_value,
                key_value_turned,
                shared,
                lse,
                attended,
                residual_mid,
                normed_mlp,
                slope,
                scale,
                unit,
            )
        )
        residual = residual_mid
    residual = residual + (parts[0].astype(F32) + parts[1].astype(F32))
    layer_out = own_rows(residual)

    def outer_sum(total):
        for bit in outer_bits:
            total = total.astype(BF16)
            total = total.astype(F32) + flip(total, bit).astype(F32)
        return total.astype(BF16)

    flow = pair_rows(cotangent[0])
    flow, flow_low = flow.astype(F32), flow
    gain_grads = [None] * (2 * layer_count)
    outs = [
        shaped((layer_count, *weight.shape[1:]), F32)
        for weight in (w_query, w_key, w_value, w_out, w_gate, w_up, w_down)
    ]
    held = None
    for layer in reversed(range(layer_count)):
        (
            qkv_w,
            out_w,
            pieces,
            down_w,
            gain_attn,
            gain_mlp,
            residual,
            normed_attn,
            query,
            key_value,
            key_value_turned,
            shared,
            lse,
            attended,
            residual_mid,
            normed_mlp,
            slope,
            scale,
            unit,
        ) = saved_layers[layer]
        keep, send = down_grad(spot, unit, flow_low)
        down_sum = (keep.astype(F32) + flip(send, ROW).astype(F32)).astype(BF16)
        down_share = lax.psum_scatter(down_sum, "wt", scatter_dimension=0, tiled=False)
        keep, send, part = mlp_back(flow_low, normed_mlp, slope, scale, down_w, pieces)
        ff_sum = (keep.astype(F32) + flip(send, SIDE).astype(F32)).astype(BF16)
        ff_share = lax.psum_scatter(ff_sum, "wt", scatter_dimension=0, tiled=True)
        flow, flow_low, gain_grads[layer_count + layer] = norm_back(
            flow, (part, flip(part, PAIR)), residual_mid, gain_mlp
        )
        attended_grad = dot_nt(out_w, flow_low).astype(BF16)
        query_grad, own_grad, shared_grad = attend_back(
            query,
            attended_grad,
            key_value,
            key_value_turned,
            shared,
            key_pos,
            row_pos,
            lse,
            cosine,
            sine,
        )
        for bit in reversed([SIDE, ROW] + outer_bits):
            half = shared_grad.shape[0] // 2
            arrived = flip(shared_grad[half:].astype(BF16), bit)
            shared_grad = shared_grad[:half] + arrived.astype(F32)
        grad_qkv = merge(query_grad, own_grad, shared_grad, cosine, sine)
        part = dot_nt(grad_qkv, qkv_w).astype(BF16)
        flow, flow_low_next, gain_grads[layer] = norm_back(
            flow, (part, flip(part, PAIR)), residual, gain_attn
        )
        qkv_part = dot_tn(normed_attn, grad_qkv).astype(BF16)
        out_part = dot_nn(attended, flow_low).astype(BF16)
        flow_low = flow_low_next
        attn_sums = []
        for whole_part in (qkv_part, out_part):
            split = whole_part.reshape(-1, 2, half_depth, whole_part.shape[1])
            kept = lax.dynamic_index_in_dim(split, row, 1, keepdims=False)
            sent = lax.dynamic_index_in_dim(split, 1 - row, 1, keepdims=False)
            attn_sums.append((kept.astype(F32) + flip(sent, ROW).astype(F32)).astype(BF16))
        qkv_sum, out_sum = attn_sums
        kept = lax.dynamic_slice(
            out_sum, (0, 0, half_width * pair), (wt_count // 2, half_depth, half_width)
        )
        sent = lax.dynamic_slice(
            out_sum, (0, 0, half_width * (1 - pair)), (wt_count // 2, half_depth, half_width)
        )
        out_all = jnp.concatenate(ordered(pair, kept, flip(sent, PAIR)), axis=0)
        attn_share = lax.psum_scatter(
            jnp.concatenate([qkv_sum, out_all], axis=2), "wt", scatter_dimension=0, tiled=False
        )

        swapped = flip(ff_share, ROW)
        cut = 2 * ff_block
        swapped = jnp.concatenate([swapped[:, cut:], swapped[:, :cut]], axis=1)
        ff_total = outer_sum(ff_share.astype(F32) + swapped.astype(F32))
        ff_mine = jnp.stack([ff_total, flip(ff_total, SIDE)])
        ff_other = flip(ff_mine, PAIR)
        placed = [ff_mine, ff_other]
        for share in (down_share, attn_share):
            total = outer_sum(share.astype(F32) + flip(share, SIDE).astype(F32))
            joined = jnp.concatenate(ordered(row, total, flip(total, ROW)), axis=0)
            placed += [joined, flip(joined, PAIR)]
        held = place(layer, where, placed, outs, held)
    token_grad = own_rows(flow)

    gain_total = jnp.concatenate(gain_grads, axis=0)
    for bit in [SIDE, ROW] + outer_bits:
        gain_total = gain_total + flip(gain_total, bit)
    bit = 1
    while bit < wt_count:
        gain_total = gain_total + flip(gain_total, bit, "wt", wt_count)
        bit *= 2
    gain_share = lax.dynamic_slice(
        gain_total, (0, lax.axis_index("wt") * depth), (2 * layer_count, depth)
    )
    query_out, key_out, value_out, out_out, gate_out, up_out, down_out = held
    return (
        layer_out[None],
        token_grad[None],
        gain_share[:layer_count],
        query_out,
        key_out,
        value_out,
        out_out,
        gain_share[layer_count:],
        gate_out,
        up_out,
        down_out,
    )


def solution(mesh):
    weight = P(None, "wt", None)
    return jax.shard_map(
        per_device,
        mesh=mesh,
        in_specs=(
            P("wt", "ctx", None),
            P("wt", None),
            P("wt", "ctx", None),
            P(None, "wt"),
            weight,
            weight,
            weight,
            weight,
            P(None, "wt"),
            weight,
            weight,
            weight,
        ),
        out_specs=(
            P("wt", "ctx", None),
            P("wt", "ctx", None),
            P(None, "wt"),
            weight,
            weight,
            weight,
            weight,
            P(None, "wt"),
            weight,
            weight,
            weight,
        ),
        check_vma=False,
    )
```

```python
import functools
import math

import jax
import jax.numpy as jnp
from jax import lax
from jax.experimental import pallas as pl
from jax.experimental.pallas import tpu as pltpu
from jax.sharding import PartitionSpec as P

HEADS = 18
KV_HEADS = 6
HEAD_DIM = 64
HALF = 32
CONT = 256
SHARED = HEADS // KV_HEADS
PAIR_KV = KV_HEADS // 2
PAIR_HEADS = HEADS // 2
RUN = 2 * HALF + CONT
ROWS = 2 * RUN
PROMPT = 4 * HALF
TAIL = 2 * CONT

EPSILON = 1e-05
SCORE_SCALE = 0.125
BASE_TWO = SCORE_SCALE * math.log2(math.e)
MASKED = -1e30

BF16 = jnp.bfloat16
F32 = jnp.float32

PAIR, SIDE, ROW = 1, 2, 4


def dot_nn(left, right):
    return lax.dot_general(left, right, (((1,), (0,)), ((), ())), preferred_element_type=F32)


def dot_nt(left, right):
    return lax.dot_general(left, right, (((1,), (1,)), ((), ())), preferred_element_type=F32)


def dot_tn(left, right):
    return lax.dot_general(left, right, (((0,), (0,)), ((), ())), preferred_element_type=F32)


def dot_tt(left, right):
    return lax.dot_general(left, right, (((0,), (1,)), ((), ())), preferred_element_type=F32)


def turned(value):
    return jnp.transpose(value.astype(F32))


def shaped(shape, dtype):
    return jax.ShapeDtypeStruct(shape, dtype)


WHOLE = pl.BlockSpec(memory_space=pltpu.VMEM)
FAR = pl.BlockSpec(memory_space=pl.ANY)
SCALARS = pl.BlockSpec(memory_space=pltpu.SMEM)


def call(kernel, outs, ins, flops, limit, out_specs=None, in_specs=None, after=(), **extra):
    count, waited = len(ins), len(after)

    def body(*refs):
        kernel(*refs[:count], *refs[count + waited :])

    ins = (*ins, *after)
    return pl.pallas_call(
        body,
        out_shape=outs,
        in_specs=(in_specs or [WHOLE] * count) + [FAR] * waited,
        out_specs=out_specs or [WHOLE] * len(outs),
        compiler_params=pltpu.CompilerParams(vmem_limit_bytes=limit << 20),
        cost_estimate=pl.CostEstimate(flops=1, bytes_accessed=1, transcendentals=0),
        **extra,
    )(*ins)


def add_norm_kernel(has_parts, *refs):
    if has_parts:
        held, mine, other, gain, total_ref, normed_ref = refs
        total = held[...] + (mine[...].astype(F32) + other[...].astype(F32))
        total_ref[...] = total
    else:
        held, gain, normed_ref = refs
        total = held[...]
    inverse = lax.rsqrt(jnp.mean(total * total, axis=-1, keepdims=True) + EPSILON)
    normed_ref[...] = (total * inverse * gain[...]).astype(BF16)


def add_norm(held, parts, gain, after=()):
    rows, width = held.shape
    step = 128
    block = pl.BlockSpec((step, width), lambda i: (i, 0))
    line = pl.BlockSpec((1, width), lambda i: (0, 0))
    ins = (held, *parts, gain)
    outs = ([shaped(held.shape, F32)] if parts else []) + [shaped(held.shape, BF16)]
    result = call(
        functools.partial(add_norm_kernel, bool(parts)),
        outs,
        ins,
        0,
        16,
        in_specs=[block] * (1 + len(parts)) + [line],
        out_specs=[block] * len(outs),
        grid=(rows // step,),
        after=after,
    )
    return result if parts else (held, result[0])


def norm_back_kernel(flow, mine, other, held, gain, flow_ref, low_ref, gain_ref):
    grad = mine[...].astype(F32) + other[...].astype(F32)
    value = held[...]
    inverse = lax.rsqrt(jnp.mean(value * value, axis=-1, keepdims=True) + EPSILON)
    plain = value * inverse
    scaled = grad * gain[...]
    tilt = jnp.mean(scaled * plain, axis=-1, keepdims=True)
    total = flow[...] + inverse * (scaled - plain * tilt)
    flow_ref[...] = total
    low_ref[...] = total.astype(BF16)

    @pl.when(pl.program_id(0) == 0)
    def _():
        gain_ref[...] = jnp.zeros_like(gain_ref)

    gain_ref[...] += jnp.sum(grad * plain, axis=0, keepdims=True)


def norm_back(flow, parts, held, gain, after=()):
    rows, width = held.shape
    step = 128
    block = pl.BlockSpec((step, width), lambda i: (i, 0))
    line = pl.BlockSpec((1, width), lambda i: (0, 0))
    return call(
        norm_back_kernel,
        [shaped(held.shape, F32), shaped(held.shape, BF16), shaped((1, width), F32)],
        (flow, *parts, held, gain),
        0,
        16,
        in_specs=[block] * 4 + [line],
        out_specs=[block, block, line],
        grid=(rows // step,),
        after=after,
    )


def add_kernel(mine, other, out):
    out[...] = (mine[...].astype(F32) + other[...].astype(F32)).astype(BF16)


def add_two_kernel(first_mine, first_other, second_mine, second_other, *refs):
    out = refs[-1]
    if len(refs) == 3:
        refs[1][...] = refs[0][...]
    first = first_mine[...].astype(F32) + first_other[...].astype(F32)
    second = second_mine[...].astype(F32) + second_other[...].astype(F32)
    axis = len(out.shape) - 1
    out[...] = jnp.concatenate([first.astype(BF16), second.astype(BF16)], axis=axis)


def add_two(first, second, after=(), passed=None):
    ins = (*first, *second)
    lead = first[0].shape[:-1]
    steps = 4

    def block(*shape):
        shape = (shape[0] // steps, *shape[1:])
        return pl.BlockSpec(shape, lambda i: (i,) + (0,) * (len(shape) - 1))

    columns = first[0].shape[-1] + second[0].shape[-1]
    extra = () if passed is None else (passed,)
    result = call(
        add_two_kernel,
        [shaped(part.shape, part.dtype) for part in extra] + [shaped((*lead, columns), BF16)],
        (*ins, *extra),
        0,
        24,
        in_specs=[block(*part.shape) for part in (*ins, *extra)],
        out_specs=[block(*part.shape) for part in extra] + [block(*lead, columns)],
        grid=(steps,),
        after=after,
    )
    return result if extra else result[0]


def split_sum_kernel(share, row_other, side_other, row_out, side_out):
    cut = row_out.shape[1]
    row_out[...] = (share[:, :cut].astype(F32) + row_other[...].astype(F32)).astype(BF16)
    side_out[...] = (share[:, cut:].astype(F32) + side_other[...].astype(F32)).astype(BF16)


def split_sum(share, row_other, side_other, after=()):
    return call(
        split_sum_kernel,
        [shaped(row_other.shape, BF16), shaped(side_other.shape, BF16)],
        (share, row_other, side_other),
        0,
        16,
        after=after,
    )


def order_kernel(ids_ref, row_mine, row_other, side_mine, side_other, out):
    side, row = ids_ref[4], ids_ref[3]
    half, cut = row_mine.shape
    for value, mine, other, cols in (
        (row, row_mine, row_other, slice(0, cut)),
        (side, side_mine, side_other, slice(cut, None)),
    ):
        for index in range(2):
            chosen = jnp.where(value == index, mine[...], other[...])
            out[index * half : (index + 1) * half, cols] = chosen


def order(ids, parts):
    half, cut = parts[0].shape
    return call(
        order_kernel,
        [shaped((2 * half, cut + parts[2].shape[1]), BF16)],
        (ids, *parts),
        0,
        16,
        in_specs=[SCALARS] + [WHOLE] * 4,
    )[0]


def cross_kernel(share, gate_other, up_other, gate_out, up_out):
    block = gate_out.shape[1] // 2
    for out, other, low in ((gate_out, gate_other, 0), (up_out, up_other, 2 * block)):
        for index in range(2):
            mine = share[:, low + index * block : low + (index + 1) * block]
            theirs = other[:, (1 - index) * block : (2 - index) * block]
            out[:, index * block : (index + 1) * block] = (
                mine.astype(F32) + theirs.astype(F32)
            ).astype(BF16)


def cross(share, gate_other, up_other, after=()):
    shape = (share.shape[0], share.shape[1] // 2)
    return call(
        cross_kernel,
        [shaped(shape, BF16)] * 2,
        (share, gate_other, up_other),
        0,
        16,
        after=after,
    )


def add(mine, other, after=(), steps=4):
    shape = mine.shape
    block = pl.BlockSpec(
        (shape[0] // steps, *shape[1:]), lambda i: (i,) + (0,) * (len(shape) - 1)
    )
    return call(
        add_kernel,
        [shaped(shape, BF16)],
        (mine, other),
        0,
        24,
        in_specs=[block, block],
        out_specs=[block],
        grid=(steps,),
        after=after,
    )[0]


KEY_HALF = PAIR_KV * HEAD_DIM
QUERY_HALF = PAIR_HEADS * HEAD_DIM
QKV = 2 * KEY_HALF + QUERY_HALF


def rope_kernel(qkv_ref, cos_ref, sin_ref, query_ref, kv_ref, kv_turned_ref):
    cosine, sine = cos_ref[...], sin_ref[...]
    half = HEAD_DIM // 2

    def head(source, target_ref, target):
        low = qkv_ref[source : source + half, :]
        high = qkv_ref[source + half : source + 2 * half, :]
        target_ref[target : target + half, :] = (low * cosine - high * sine).astype(BF16)
        target_ref[target + half : target + 2 * half, :] = (high * cosine + low * sine).astype(
            BF16
        )

    for index in range(PAIR_KV):
        head(index * HEAD_DIM, kv_turned_ref, index * HEAD_DIM)
    kv_turned_ref[KEY_HALF:, :] = qkv_ref[KEY_HALF : 2 * KEY_HALF, :].astype(BF16)
    kv_ref[...] = turned(kv_turned_ref[...]).astype(BF16)
    for index in range(PAIR_HEADS):
        head(2 * KEY_HALF + index * HEAD_DIM, query_ref, index * HEAD_DIM)


def rope(qkv, cosine, sine, after=()):
    return call(
        rope_kernel,
        [
            shaped((QUERY_HALF, ROWS), BF16),
            shaped((ROWS, 2 * KEY_HALF), BF16),
            shaped((2 * KEY_HALF, ROWS), BF16),
        ],
        (qkv, cosine, sine),
        0,
        32,
        after=after,
    )


def later_mask():
    key = lax.broadcasted_iota(jnp.int32, (CONT, CONT), 0)
    query = lax.broadcasted_iota(jnp.int32, (CONT, CONT), 1)
    return key <= query


def attend_kernel(
    query_ref, kv_ref, kv_turned_ref, shared_ref, key_pos_ref, row_pos_ref, out_ref, lse_ref
):
    shared_values = turned(shared_ref[:, KEY_HALF:]).astype(BF16)
    for kv_head in range(PAIR_KV):
        low = kv_head * HEAD_DIM
        keys = shared_ref[:, low : low + HEAD_DIM]
        values = shared_values[low : low + HEAD_DIM, :]

        def head(index, carry, kv_head=kv_head, low=low, keys=keys, values=values):
            number = kv_head * SHARED + index
            base = pl.multiple_of(number * HEAD_DIM, HEAD_DIM)
            allowed = key_pos_ref[...] <= row_pos_ref[...]
            query = query_ref[pl.ds(base, HEAD_DIM), TAIL:]
            scores = jnp.where(allowed, dot_nn(keys, query) * BASE_TWO, MASKED)
            top = jnp.max(scores, axis=0, keepdims=True)
            weight = jnp.exp2(scores - top)
            total = jnp.sum(weight, axis=0, keepdims=True)
            out = dot_nn(values, weight.astype(BF16)) / total
            out_ref[pl.ds(base, HEAD_DIM), TAIL:] = out.astype(BF16)
            lse_ref[number, :, TAIL:] = top + jnp.log2(total)
            for run in range(2):
                cols = slice(run * CONT, (run + 1) * CONT)
                query = query_ref[pl.ds(base, HEAD_DIM), cols]
                own_keys = kv_ref[cols, low : low + HEAD_DIM]
                own_values = kv_turned_ref[KEY_HALF + low : KEY_HALF + low + HEAD_DIM, cols]
                first = dot_nn(keys, query) * BASE_TWO
                second = jnp.where(later_mask(), dot_nn(own_keys, query) * BASE_TWO, MASKED)
                top = jnp.maximum(
                    jnp.max(first, axis=0, keepdims=True), jnp.max(second, axis=0, keepdims=True)
                )
                first = jnp.exp2(first - top)
                second = jnp.exp2(second - top)
                total = jnp.sum(first, axis=0, keepdims=True) + jnp.sum(
                    second, axis=0, keepdims=True
                )
                out = dot_nn(values, first.astype(BF16)) + dot_nn(
                    own_values, second.astype(BF16)
                )
                out_ref[pl.ds(base, HEAD_DIM), cols] = (out / total).astype(BF16)
                lse_ref[number, :, cols] = top + jnp.log2(total)
            return carry

        lax.fori_loop(0, SHARED, head, 0)


def attend(query, key_value, key_value_turned, shared, key_pos, row_pos, after=()):
    flops = 4 * QUERY_HALF * ROWS * (shared.shape[0] + CONT)
    return call(
        attend_kernel,
        [shaped((QUERY_HALF, ROWS), BF16), shaped((PAIR_HEADS, 1, ROWS), F32)],
        (query, key_value, key_value_turned, shared, key_pos, row_pos),
        flops,
        48,
        after=after,
    )


def attend_back_kernel(
    query_ref,
    grad_ref,
    kv_ref,
    kv_turned_ref,
    shared_ref,
    key_pos_ref,
    row_pos_ref,
    lse_ref,
    cos_ref,
    sin_ref,
    query_grad_ref,
    own_grad_ref,
    shared_grad_ref,
    score_keep,
    weight_keep,
    own_score_keep,
    own_weight_keep,
):
    shared_turned = turned(shared_ref[:, :KEY_HALF]).astype(BF16)
    half = HEAD_DIM // 2
    for kv_head in range(PAIR_KV):
        low = kv_head * HEAD_DIM
        keys = shared_ref[:, low : low + HEAD_DIM]
        values = shared_ref[:, KEY_HALF + low : KEY_HALF + low + HEAD_DIM]
        keys_turned = shared_turned[low : low + HEAD_DIM, :]

        def head(index, carry, kv_head=kv_head, low=low, keys=keys, values=values, keys_turned=keys_turned):
            number = kv_head * SHARED + index
            base = pl.multiple_of(number * HEAD_DIM, HEAD_DIM)

            def put_query_grad(grad, cols):
                cosine, sine = cos_ref[:, cols], sin_ref[:, cols]
                first, second = grad[:half], grad[half:]
                query_grad_ref[pl.ds(base, half), cols] = (
                    (first * cosine + second * sine) * SCORE_SCALE
                ).astype(BF16)
                query_grad_ref[pl.ds(base + half, half), cols] = (
                    (second * cosine - first * sine) * SCORE_SCALE
                ).astype(BF16)

            cols = slice(TAIL, ROWS)
            query = query_ref[pl.ds(base, HEAD_DIM), cols]
            grad = grad_ref[pl.ds(base, HEAD_DIM), cols]
            lse = lse_ref[number, :, cols]
            allowed = key_pos_ref[...] <= row_pos_ref[...]
            scores = jnp.where(allowed, dot_nn(keys, query) * BASE_TWO, MASKED)
            weight = jnp.exp2(scores - lse)
            weight_keep[index, :, cols] = weight.astype(BF16)
            flow = weight * dot_nn(values, grad)
            delta = jnp.sum(flow, axis=0, keepdims=True)
            flow = (flow - weight * delta).astype(BF16)
            score_keep[index, :, cols] = flow
            put_query_grad(dot_nn(keys_turned, flow), cols)
            for run in range(2):
                cols = slice(run * CONT, (run + 1) * CONT)
                query = query_ref[pl.ds(base, HEAD_DIM), cols]
                grad = grad_ref[pl.ds(base, HEAD_DIM), cols]
                lse = lse_ref[number, :, cols]
                own_keys = kv_ref[cols, low : low + HEAD_DIM]
                own_values = kv_ref[cols, KEY_HALF + low : KEY_HALF + low + HEAD_DIM]
                own_turned = kv_turned_ref[low : low + HEAD_DIM, cols]
                first = jnp.exp2(dot_nn(keys, query) * BASE_TWO - lse)
                second = jnp.where(later_mask(), dot_nn(own_keys, query) * BASE_TWO, MASKED)
                second = jnp.exp2(second - lse)
                weight_keep[index, :, cols] = first.astype(BF16)
                own_weight_keep[index, :, cols] = second.astype(BF16)
                first_flow = first * dot_nn(values, grad)
                second_flow = second * dot_nn(own_values, grad)
                delta = jnp.sum(first_flow, axis=0, keepdims=True) + jnp.sum(
                    second_flow, axis=0, keepdims=True
                )
                first_flow = (first_flow - first * delta).astype(BF16)
                second_flow = (second_flow - second * delta).astype(BF16)
                score_keep[index, :, cols] = first_flow
                own_score_keep[index, :, cols] = second_flow
                put_query_grad(
                    dot_nn(keys_turned, first_flow) + dot_nn(own_turned, second_flow), cols
                )
            return carry

        lax.fori_loop(0, SHARED, head, 0)
        key_sum, value_sum = 0.0, 0.0
        own_key_sum, own_value_sum = [0.0, 0.0], [0.0, 0.0]
        for index in range(SHARED):
            base = (kv_head * SHARED + index) * HEAD_DIM
            query = query_ref[base : base + HEAD_DIM, :]
            grad = grad_ref[base : base + HEAD_DIM, :]
            key_sum = key_sum + dot_nt(score_keep[index], query)
            value_sum = value_sum + dot_nt(weight_keep[index], grad)
            for run in range(2):
                cols = slice(run * CONT, (run + 1) * CONT)
                own_key_sum[run] = own_key_sum[run] + dot_nt(
                    own_score_keep[index, :, cols], query[:, cols]
                )
                own_value_sum[run] = own_value_sum[run] + dot_nt(
                    own_weight_keep[index, :, cols], grad[:, cols]
                )
        shared_grad_ref[:, low : low + HEAD_DIM] = key_sum * SCORE_SCALE
        shared_grad_ref[:, KEY_HALF + low : KEY_HALF + low + HEAD_DIM] = value_sum
        for run in range(2):
            cols = slice(run * CONT, (run + 1) * CONT)
            own_grad_ref[cols, low : low + HEAD_DIM] = own_key_sum[run] * SCORE_SCALE
            own_grad_ref[cols, KEY_HALF + low : KEY_HALF + low + HEAD_DIM] = own_value_sum[run]


def attend_back(
    query, grad, key_value, key_value_turned, shared, key_pos, row_pos, lse, cosine, sine, after=()
):
    count = shared.shape[0]
    flops = 10 * QUERY_HALF * ROWS * (count + CONT)
    return call(
        attend_back_kernel,
        [
            shaped((QUERY_HALF, ROWS), BF16),
            shaped((TAIL, 2 * KEY_HALF), F32),
            shaped((count, 2 * KEY_HALF), F32),
        ],
        (query, grad, key_value, key_value_turned, shared, key_pos, row_pos, lse, cosine, sine),
        flops,
        56,
        scratch_shapes=[
            pltpu.VMEM((SHARED, count, ROWS), BF16),
            pltpu.VMEM((SHARED, count, ROWS), BF16),
            pltpu.VMEM((SHARED, CONT, TAIL), BF16),
            pltpu.VMEM((SHARED, CONT, TAIL), BF16),
        ],
        after=after,
    )


def merge_kernel(query_grad_ref, own_ref, prompt_ref, cos_ref, sin_ref, out_ref):
    cosine, sine = cos_ref[...], sin_ref[...]
    half = HEAD_DIM // 2
    both = turned(jnp.concatenate([own_ref[...], prompt_ref[...]], axis=0))
    pieces = []
    for index in range(PAIR_KV):
        low = both[index * HEAD_DIM : index * HEAD_DIM + half]
        high = both[index * HEAD_DIM + half : (index + 1) * HEAD_DIM]
        pieces += [low * cosine + high * sine, high * cosine - low * sine]
    both = jnp.concatenate(pieces + [both[KEY_HALF:]], axis=0)
    out_ref[:, : 2 * KEY_HALF] = jnp.transpose(both).astype(BF16)
    out_ref[:, 2 * KEY_HALF :] = turned(query_grad_ref[...]).astype(BF16)


def merge(query_grad, own_grad, prompt_grad, cosine, sine, after=()):
    return call(
        merge_kernel,
        [shaped((ROWS, QKV), BF16)],
        (query_grad, own_grad, prompt_grad, cosine, sine),
        0,
        32,
        after=after,
    )[0]


def mlp_kernel(layer, ids_ref, normed_ref, *refs):
    own = refs[0]
    from_row, from_side, from_across = refs[1:3], refs[3:5], refs[5:9]
    gate_ref, up_ref, down_shard = (ref.at[layer] for ref in refs[9:12])
    weight_ref, down_ref, slope_ref, scale_ref, unit_ref, out_ref = refs[12:18]
    held, sems, down_sem, keep_sem = refs[18:]
    rows, depth = normed_ref.shape
    block = held.shape[2] // 2
    shard = depth // 4
    lines = block // 4
    wide = depth // 3
    quarter, plane, pair = ids_ref[0], ids_ref[1], ids_ref[2]
    slots = line_slots(plane)

    def copy(source, target, sem):
        pltpu.make_async_copy(source, target, sem).start()

    def at(start, size):
        return pl.ds(pl.multiple_of(start, 16), size)

    def pieces(part):
        if part == 0:
            return [(own.at[owner], 0, shard, owner) for owner in (plane, *slots)]
        if part < 3:
            pair_of_slots, last = (from_row, from_side)[part - 1]
            arrived = (pair_of_slots.at[0], pair_of_slots.at[1], last.at[0])
            return [(arrived[slot], 0, shard, slots[slot]) for slot in range(3)]
        half = shard // 2
        return [
            (from_across[0], 0, shard, slots[0]),
            (from_across[1], 0, shard, slots[1]),
            (from_across[2], 0, half, slots[2]),
            (from_across[3], half, shard, slots[2]),
        ]

    for part in range(4):
        for source, low, high, owner in pieces(part):
            copy(
                source.at[:, : 2 * block],
                held.at[part, at(shard * owner + low, high - low)],
                sems.at[part],
            )
        if part == 0:
            continue
        col = pl.ds(pl.multiple_of((2 * (quarter ^ part) + pair) * block, block), block)
        for index, ref in enumerate((gate_ref, up_ref)):
            copy(
                ref.at[:, col],
                held.at[part, at(shard * plane, shard), pl.ds(index * block, block)],
                sems.at[part],
            )
    taken = pl.ds(2 * block, wide)

    def down_copies(source, low, high, place, piece):
        for column in range(3):
            first, last = max(low, lines * column), min(high, lines * (column + 1))
            if first < last:
                copy(
                    source.at[at(first - low, last - first), taken],
                    down_ref.at[
                        at(
                            block * place + lines * (quarter ^ piece) + first - lines * column,
                            last - first,
                        ),
                        pl.ds(wide * column, wide),
                    ],
                    down_sem,
                )

    for part in range(4):
        for source, low, high, owner in pieces(part):
            down_copies(source, low, high, quarter ^ owner, part)
        if part == 0:
            continue
        copy(
            down_shard.at[at(block * pair + lines * (quarter ^ part), lines)],
            down_ref.at[at(block * (quarter ^ plane) + lines * (quarter ^ part), lines)],
            down_sem,
        )

    step = rows // 2
    kept = []
    for part in range(4):
        pltpu.make_async_copy(held.at[part], held.at[part], sems.at[part]).wait()
        kept.append(pltpu.make_async_copy(held.at[part], weight_ref.at[part], keep_sem.at[part]))
        kept[-1].start()

        def tile(index, carry, part=part):
            some = pl.ds(pl.multiple_of(index * step, step), step)
            normed = normed_ref[some, :]
            gate = dot_nn(normed, held[part, :, :block])
            up = dot_nn(normed, held[part, :, block:])
            sigmoid = 1.0 / (1.0 + jnp.exp(-gate))
            scale = gate * sigmoid
            cols = slice(part * block, (part + 1) * block)
            slope_ref[some, cols] = (up * sigmoid * (1.0 + gate * (1.0 - sigmoid))).astype(BF16)
            scale_ref[some, cols] = scale.astype(BF16)
            unit_ref[some, cols] = (scale * up).astype(BF16)
            return carry

        lax.fori_loop(0, 2, tile, 0)
    pltpu.make_async_copy(down_ref, down_ref, down_sem).wait()

    def finish(index, carry):
        some = pl.ds(pl.multiple_of(index * step, step), step)
        out_ref[some, :] = dot_nn(unit_ref[some, :], down_ref[...]).astype(BF16)
        return carry

    lax.fori_loop(0, 2, finish, 0)
    for part in kept:
        part.wait()


def mlp(layer, ids, normed, pieces, weights, block, after=()):
    rows, depth = normed.shape
    units = 4 * block
    ins = (ids, normed, *pieces, *weights)
    return call(
        functools.partial(mlp_kernel, layer),
        [
            shaped((4, depth, 2 * block), BF16),
            shaped((units, depth), BF16),
            shaped((rows, units), BF16),
            shaped((rows, units), BF16),
            shaped((rows, units), BF16),
            shaped((rows, depth), BF16),
        ],
        ins,
        6 * rows * depth * units,
        56,
        in_specs=[SCALARS, WHOLE] + [FAR] * (len(ins) - 2),
        out_specs=[FAR] + [WHOLE] * 5,
        scratch_shapes=[
            pltpu.VMEM((4, depth, 2 * block), BF16),
            pltpu.SemaphoreType.DMA((4,)),
            pltpu.SemaphoreType.DMA,
            pltpu.SemaphoreType.DMA((4,)),
        ],
        after=after,
    )


def pack_kernel(layer, ids_ref, gate_ref, up_ref, down_ref, out, sem):
    quarter, pair = ids_ref[0], ids_ref[2]
    depth, columns = out.shape
    wide = columns // 3
    lines = depth // 3
    col = pl.ds(pl.multiple_of((2 * quarter + pair) * wide, wide), wide)
    for index, ref in enumerate((gate_ref, up_ref)):
        target = out.at[:, pl.ds(index * wide, wide)]
        pltpu.make_async_copy(ref.at[layer, :, col], target, sem).start()
    start = pl.multiple_of((4 * pair + quarter) * lines, lines)
    for index in range(3):
        pltpu.make_async_copy(
            down_ref.at[layer, pl.ds(start, lines), pl.ds(index * wide, wide)],
            out.at[pl.ds(index * lines, lines), pl.ds(2 * wide, wide)],
            sem,
        ).start()
    pltpu.make_async_copy(out, out, sem).wait()


def pack(layer, ids, weights, after=()):
    _, depth, units = weights[0].shape
    return call(
        functools.partial(pack_kernel, layer),
        [shaped((depth, 3 * units // 8), BF16)],
        (ids, *weights),
        0,
        16,
        in_specs=[SCALARS] + [FAR] * 3,
        out_specs=[FAR],
        scratch_shapes=[pltpu.SemaphoreType.DMA],
        after=after,
    )[0]


def deal(total, row, side, cut, place, row_keep, row_send, side_keep, side_send):
    half = total.shape[0] // 2
    for index in range(2):
        part = total[index * half : (index + 1) * half]
        for value, keep, send, cols in (
            (row, row_keep, row_send, slice(0, cut)),
            (side, side_keep, side_send, slice(cut, None)),
        ):

            @pl.when(value == index)
            def _(part=part, keep=keep, cols=cols):
                keep[place] = part[:, cols]

            @pl.when(value != index)
            def _(part=part, send=send, cols=cols):
                send[place] = part[:, cols]


def dealt(blocks, half, columns, cut):
    return [
        shaped((blocks, half, size), BF16) for size in (cut, cut, columns - cut, columns - cut)
    ]


def down_grad_kernel(cut, ids_ref, unit_ref, flow_ref, *outs):
    quarter, side, row = ids_ref[0], ids_ref[4], ids_ref[3]
    block = unit_ref.shape[1] // 4
    for place in range(4):
        total = dot_tn(unit_ref[:, place * block : (place + 1) * block], flow_ref[...])
        deal(total.astype(BF16), row, side, cut, quarter ^ place, *outs)


def down_grad(ids, unit, flow, cut, after=()):
    rows, units = unit.shape
    width = flow.shape[1]
    return call(
        functools.partial(down_grad_kernel, cut),
        dealt(4, units // 8, width, cut),
        (ids, unit, flow),
        2 * rows * units * width,
        48,
        in_specs=[SCALARS, WHOLE, WHOLE],
        after=after,
    )


def mlp_back_kernel(
    flow_ref,
    normed_ref,
    slope_ref,
    scale_ref,
    down_ref,
    weight_ref,
    gate_keep,
    gate_send,
    up_keep,
    up_send,
    out_ref,
    held,
    total,
    unit_grad,
    sems,
):
    rows, depth = normed_ref.shape
    block = held.shape[2] // 2
    order = (3, 2, 1, 0)
    copies = {
        part: pltpu.make_async_copy(weight_ref.at[part], held.at[part], sems.at[part])
        for part in order
    }
    for part in order:
        copies[part].start()
    step = rows // 2
    for part in order:
        cols = slice(part * block, (part + 1) * block)

        def tile(index, carry, cols=cols):
            at = pl.ds(pl.multiple_of(index * step, step), step)
            grad = dot_nt(flow_ref[at, :], down_ref[cols, :])
            unit_grad[at, :block] = (grad * slope_ref[at, cols].astype(F32)).astype(BF16)
            unit_grad[at, block:] = (grad * scale_ref[at, cols].astype(F32)).astype(BF16)
            return carry

        lax.fori_loop(0, 2, tile, 0)
        both = dot_tn(normed_ref[...], unit_grad[...]).astype(BF16)
        target = gate_send if part >= 2 else gate_keep
        target[:, (part % 2) * block : (part % 2 + 1) * block] = both[:, :block]
        target = up_send if part % 2 else up_keep
        target[:, (part // 2) * block : (part // 2 + 1) * block] = both[:, block:]
        copies[part].wait()

        def gather(index, carry, part=part):
            at = pl.ds(pl.multiple_of(index * step, step), step)
            value = dot_nt(unit_grad[at, :], held[part])
            if part == order[0]:
                total[at, :] = value
            elif part == order[-1]:
                out_ref[at, :] = (total[at, :] + value).astype(BF16)
            else:
                total[at, :] += value
            return carry

        lax.fori_loop(0, 2, gather, 0)


def mlp_back(flow, normed, slope, scale, down, weights, after=()):
    rows, depth = normed.shape
    block = down.shape[0] // 4
    return call(
        mlp_back_kernel,
        [shaped((depth, 2 * block), BF16)] * 4 + [shaped((rows, depth), BF16)],
        (flow, normed, slope, scale, down, weights),
        10 * rows * depth * 4 * block,
        60,
        in_specs=[WHOLE] * 5 + [FAR],
        scratch_shapes=[
            pltpu.VMEM((4, depth, 2 * block), BF16),
            pltpu.VMEM((rows, depth), F32),
            pltpu.VMEM((rows, 2 * block), BF16),
            pltpu.SemaphoreType.DMA((4,)),
        ],
        after=after,
    )


def join_kernel(ids_ref, local, mine, other, out, sem):
    plane, row = ids_ref[1], ids_ref[3]
    half = local.shape[0] // 2

    def copy(source, start):
        target = out.at[pl.ds(pl.multiple_of(start, 16), source.shape[0])]
        pltpu.make_async_copy(source, target, sem).start()

    copy(local, 2 * half * plane)
    for slot, owner in enumerate(line_slots(plane)):
        copy(mine.at[owner, pl.ds(0, half)], half * (2 * owner + row))
        copy(other.at[slot], half * (2 * owner + 1 - row))
    pltpu.make_async_copy(out, out, sem).wait()


def join(ids, local, mine, other, after=()):
    shape = (4 * local.shape[0], local.shape[1])
    return call(
        join_kernel,
        [shaped(shape, BF16)],
        (ids, local, mine, other),
        0,
        16,
        in_specs=[SCALARS] + [FAR] * 3,
        out_specs=[FAR],
        scratch_shapes=[pltpu.SemaphoreType.DMA],
        after=after,
    )[0]


def others_kernel(first, ids_ref, gathered, out, sem):
    count, rows, _ = out.shape
    for slot, owner in enumerate(line_slots(ids_ref[1])[first : first + count]):
        pltpu.make_async_copy(gathered.at[owner, pl.ds(0, rows)], out.at[slot], sem).start()
    pltpu.make_async_copy(out, out, sem).wait()


def others(ids, gathered, rows, first, last, after=()):
    return call(
        functools.partial(others_kernel, first),
        [shaped((last - first, rows, gathered.shape[2]), BF16)],
        (ids, gathered),
        0,
        16,
        in_specs=[SCALARS, FAR],
        out_specs=[FAR],
        scratch_shapes=[pltpu.SemaphoreType.DMA],
        after=after,
    )[0]


def line_slots(plane):
    return [plane ^ step for step in (1, 2, 3)]


def attn_grad_kernel(cut, ids_ref, normed, grad, attended, flow, *outs):
    side, row = ids_ref[4], ids_ref[3]
    blocks, half, _ = outs[0].shape
    out_cols = flow.shape[1] // 2
    out = dot_nn(attended[...], flow[...]).astype(BF16)
    for block in range(blocks):
        low, col = 2 * (block // 2) * half, (block % 2) * out_cols
        total = jnp.concatenate(
            [
                dot_tn(normed[:, 2 * block * half : 2 * (block + 1) * half], grad[...]).astype(
                    BF16
                ),
                out[low : low + 2 * half, col : col + out_cols],
            ],
            axis=1,
        )
        deal(total, row, side, cut, block, *outs)


def attn_grad(ids, normed, grad, attended, flow, cut, after=()):
    columns = grad.shape[1] + flow.shape[1] // 2
    return call(
        functools.partial(attn_grad_kernel, cut),
        dealt(4, normed.shape[1] // 8, columns, cut),
        (ids, normed, grad, attended, flow),
        0,
        40,
        in_specs=[SCALARS] + [WHOLE] * 4,
        after=after,
    )


def attn_sum_kernel(pair_ref, row_mine, row_other, side_mine, side_other, keep_ref, send_ref):
    pair = pair_ref[0]
    total = jnp.concatenate(
        [
            (mine[...].astype(F32) + other[...].astype(F32)).astype(BF16)
            for mine, other in ((row_mine, row_other), (side_mine, side_other))
        ],
        axis=2,
    )
    keep_ref[:, :, :QKV] = total[:, :, :QKV]
    for plane in range(4):
        for owner in range(2):

            @pl.when(pair == owner)
            def _(plane=plane, owner=owner):
                if plane // 2 == owner:
                    keep_ref[plane, :, QKV:] = total[2 * (plane % 2) + owner, :, QKV:]
                else:
                    send_ref[plane % 2] = total[2 * (plane % 2) + 1 - owner, :, QKV:]
                    keep_ref[plane, :, QKV:] = jnp.zeros_like(keep_ref[plane, :, QKV:])


def attn_sum(pair, parts, after=()):
    blocks, half, first = parts[0].shape
    columns = first + parts[2].shape[2]
    return call(
        attn_sum_kernel,
        [
            shaped((blocks, half, columns), BF16),
            shaped((blocks // 2, half, columns - QKV), BF16),
        ],
        (pair, *parts),
        0,
        32,
        in_specs=[SCALARS] + [WHOLE] * 4,
        after=after,
    )


def attn_join_kernel(pair_ref, mine, other, out):
    pair = pair_ref[0]
    out[:, :, :QKV] = mine[:, :, :QKV]
    for plane in range(4):
        for owner in range(2):

            @pl.when(pair == owner)
            def _(plane=plane, owner=owner):
                if plane // 2 == owner:
                    out[plane, :, QKV:] = mine[plane, :, QKV:]
                else:
                    out[plane, :, QKV:] = other[plane % 2]


def attn_join(pair, mine, other, after=()):
    return call(
        attn_join_kernel,
        [shaped(mine.shape, BF16)],
        (pair, mine, other),
        0,
        32,
        in_specs=[SCALARS, WHOLE, WHOLE],
        after=after,
    )[0]


def place_ff_kernel(where_ref, *refs):
    gates, ups, downs = refs[0:4], refs[4:8], refs[8:10]
    gate_out, up_out, down_out = refs[10:]
    pair, quarter = where_ref[0], where_ref[1]
    block = gates[0].shape[1] // 2
    for out, pieces, spread, inner in ((gate_out, gates, 2, 1), (up_out, ups, 1, 2)):
        for number, ref in enumerate(pieces):
            owner = pair ^ (number // 2)
            for index in range(2):
                plane = quarter ^ ((number % 2) * spread + index * inner)
                col = pl.multiple_of((2 * plane + owner) * block, block)
                out[0, :, pl.ds(col, block)] = ref[
                    :, index * block : (index + 1) * block
                ].astype(F32)
    down_rows = downs[0].shape[0]
    for where_from, owner in ((downs[0], pair), (downs[1], 1 - pair)):
        down_out[0, pl.ds(pl.multiple_of(owner * down_rows, down_rows), down_rows), :] = (
            where_from[...].astype(F32)
        )


def place_attn_kernel(where_ref, attn_mine, attn_other, *refs):
    query_out, key_out, value_out, out_out = refs
    pair = where_ref[0]
    first = jnp.where(pair == 0, attn_mine[...], attn_other[...]).astype(F32)
    second = jnp.where(pair == 0, attn_other[...], attn_mine[...]).astype(F32)
    low = 0
    for out, cols in (
        (key_out, KEY_HALF),
        (value_out, KEY_HALF),
        (query_out, QUERY_HALF),
        (out_out, first.shape[1] - QKV),
    ):
        out[0] = jnp.concatenate([first[:, low : low + cols], second[:, low : low + cols]], axis=1)
        low += cols


def place_kernel(kernel, fresh, parts, outs, *refs):
    here = refs[: 1 + parts]
    there = refs[1 + parts :] if fresh else refs[1 + parts + outs :]
    kernel(*here, *there[:outs])
    there[outs][...] = jnp.zeros_like(there[outs])


def place(kernel, layer, where, parts, outs, held, after=()):
    ins = (where, *parts, *(held or ()))
    specs = [SCALARS] + [WHOLE] * len(parts) + [FAR] * len(held or ())

    def layer_block(out):
        return pl.BlockSpec((1, *out.shape[1:]), lambda _: (layer, 0, 0))

    aliases = {} if held is None else {1 + len(parts) + i: i for i in range(len(outs))}
    return call(
        functools.partial(place_kernel, kernel, held is None, len(parts), len(outs)),
        [*outs, shaped((8, 128), F32)],
        ins,
        0,
        60,
        in_specs=specs,
        out_specs=[layer_block(out) for out in outs]
        + [pl.BlockSpec((8, 128), lambda _: (0, 0))],
        input_output_aliases=aliases,
        grid=(1,),
        after=after,
    )


def positions(deal_row, ctx_count):
    row_ids = jnp.arange(RUN, dtype=jnp.int32)
    block_ids = deal_row[..., None]
    lower_block = block_ids * HALF + row_ids
    upper_block = (2 * ctx_count - 1 - block_ids) * HALF + row_ids - HALF
    continued = 2 * HALF * ctx_count + row_ids - 2 * HALF
    return jnp.where(
        row_ids < HALF, lower_block, jnp.where(row_ids < 2 * HALF, upper_block, continued)
    )


def per_device(
    tokens,
    assign,
    cotangent,
    attn_gain,
    w_query,
    w_key,
    w_value,
    w_out,
    mlp_gain,
    w_gate,
    w_up,
    w_down,
):
    ctx_count = lax.axis_size("ctx")
    wt_count = lax.axis_size("wt")
    ctx_index = lax.axis_index("ctx")
    pair = ctx_index % 2
    side = (ctx_index // SIDE) % 2
    row = (ctx_index // ROW) % 2
    quarter = 2 * side + row
    chip = ctx_index // 2
    chip_count = ctx_count // 2
    outer_bits = [bit for bit in (8, 16, 32, 64, 128) if bit < ctx_count]

    layer_count, depth = attn_gain.shape[0], w_query.shape[1]
    width = w_out.shape[2]
    half_width = width // 2
    ff_block = w_down.shape[1] // 2
    ff_piece = ff_block // 4
    half_depth = depth // 2

    def flip(value, bit, axis="ctx", count=None):
        count = ctx_count if count is None else count
        return lax.ppermute(value, axis, [(i, i ^ bit) for i in range(count)])

    def ordered(bit_value, mine, other):
        first = jnp.where(bit_value == 0, mine, other)
        second = jnp.where(bit_value == 0, other, mine)
        return first, second

    def pair_rows(own):
        first, second = ordered(pair, own, flip(own, PAIR))
        cut = 2 * HALF
        return jnp.concatenate([first[cut:], second[cut:], first[:cut], second[:cut]], axis=0)

    def own_rows(both):
        return jnp.concatenate(
            [
                lax.dynamic_slice(both, (TAIL + 2 * HALF * pair, 0), (2 * HALF, width)),
                lax.dynamic_slice(both, (CONT * pair, 0), (CONT, width)),
            ],
            axis=0,
        )

    every_pos = positions(assign[0], ctx_count).reshape(chip_count, 2, RUN)
    key_bits = [ROW, SIDE] + outer_bits
    steps = [0]
    for bit in key_bits:
        steps += [step ^ (bit // 2) for step in steps]
    wanted = chip ^ jnp.array(steps, dtype=jnp.int32)
    picked = wanted[:, None] == jnp.arange(chip_count, dtype=jnp.int32)[None, :]
    prompt_pos = jnp.sum(
        jnp.where(picked[:, :, None, None], every_pos[None, :, :, : 2 * HALF], 0), axis=1
    )
    key_pos = prompt_pos.reshape(-1, 1)
    row_pos = prompt_pos[0].reshape(1, -1)
    cont_pos = every_pos[0, 0, 2 * HALF :]
    own_pos = jnp.concatenate([cont_pos, cont_pos, row_pos[0]])
    half_dim = HEAD_DIM // 2
    frequency = jnp.exp(jnp.arange(half_dim, dtype=F32) * (-jnp.log(10000.0) / half_dim))
    phase = frequency[:, None] * own_pos.astype(F32)[None, :]
    cosine, sine = jnp.cos(phase), jnp.sin(phase)

    gain_line = jnp.concatenate([attn_gain, mlp_gain]).reshape(1, -1)
    columns = QKV + half_width
    plane = lax.axis_index("wt")
    ids = jnp.stack([quarter, plane, pair, row, side])
    ff_weights = (w_gate, w_up, w_down)

    def attn_local(layer):
        return jnp.concatenate(
            [
                lax.dynamic_slice(weight[layer], (0, cols * pair), (depth, cols))
                for weight, cols in (
                    (w_key, KEY_HALF),
                    (w_value, KEY_HALF),
                    (w_query, QUERY_HALF),
                    (w_out, half_width),
                )
            ],
            axis=1,
        )

    def attn_gather(layer):
        local = attn_local(layer)
        piece = lax.dynamic_slice(local, (half_depth * row, 0), (half_depth, columns))
        if layer == 0:
            line = jnp.pad(gain_line, ((0, 15), (0, columns - gain_line.shape[1])))
            piece = jnp.concatenate([piece, line], axis=0)
        return local, lax.all_gather(piece, "wt", axis=0, tiled=False)

    def attn_weights(local, mine, other, after):
        both = join(ids, local, mine, other, after)
        keep = lax.dynamic_slice(both, (QUERY_HALF * pair, QKV), (QUERY_HALF, half_width))
        send = lax.dynamic_slice(both, (QUERY_HALF * (1 - pair), QKV), (QUERY_HALF, half_width))
        out_w = jnp.concatenate(ordered(pair, keep, flip(send, PAIR)), axis=1)
        return both[:, :QKV], out_w

    def mlp_gather(layer):
        piece = pack(layer, ids, ff_weights)
        return lax.all_gather(piece, "wt", axis=0, tiled=False)

    def mlp_spread(line, ahead, bit):
        first, last = line
        by_row, by_side = ahead or (flip(first, ROW), flip(first, SIDE))
        last_by_row, last_by_side = flip(last, ROW), flip(last, SIDE)
        across = (
            flip(by_row[0], SIDE),
            flip(by_row[1], SIDE) if bit == SIDE else flip(by_side[1], ROW),
            flip(last_by_row[0, :half_depth], SIDE),
            flip(last_by_side[0, half_depth:], ROW),
        )
        return by_row, last_by_row, by_side, last_by_side, *across

    where = jnp.stack([pair, quarter])

    residual = pair_rows(tokens[0]).astype(F32)
    parts = ()
    saved_layers = []
    attn_sets, ff_sets = [], []
    for layer in range(layer_count):
        attn_sets.append(attn_gather(layer))
        ff_sets.append(mlp_gather(layer))
    lines = attn_sets[0][1][:, half_depth, : gain_line.shape[1]].astype(F32)
    gains = (
        lines.reshape(wt_count, 2 * layer_count, depth)
        .transpose(1, 0, 2)
        .reshape(2 * layer_count, 1, wt_count * depth)
    )
    attn_other = flip(others(ids, attn_sets[0][1], half_depth, 0, 3), ROW)
    for layer in range(layer_count):
        last = layer + 1 == layer_count
        local, mine = attn_sets[layer]
        qkv_w, out_w = attn_weights(local, mine, attn_other, ())
        gain_attn, gain_mlp = gains[layer], gains[layer_count + layer]
        residual, normed_attn = add_norm(residual, parts, gain_attn)
        ahead = tuple(flip(early, bit) for bit in (ROW, SIDE)) if layer else ()
        query, key_value, key_value_turned = rope(
            dot_tt(qkv_w, normed_attn), cosine, sine, ahead
        )
        shared = key_value[TAIL:]
        for bit in key_bits:
            shared = jnp.concatenate([shared, flip(shared, bit)], axis=0)
        first = early if layer else others(ids, ff_sets[layer], depth, 0, 2, (shared,))
        line = (first, others(ids, ff_sets[layer], depth, 2, 3, (shared,)))
        spread = mlp_spread(line, ahead, ROW if layer else SIDE)
        attended, lse = attend(
            query, key_value, key_value_turned, shared, key_pos, row_pos, line
        )
        part = dot_tn(attended, out_w).astype(BF16)
        residual_mid, normed_mlp = add_norm(residual, (part, flip(part, PAIR)), gain_mlp)
        late = ()
        if layer + 1 < layer_count:
            next_attn = attn_sets[layer + 1][1]
            attn_other = flip(others(ids, next_attn, half_depth, 0, 3, (attended,)), ROW)
            late = (attn_other,)
        ff_w, down_w, slope, scale, unit, part = mlp(
            layer,
            ids,
            normed_mlp,
            (ff_sets[layer], *spread),
            ff_weights,
            ff_block,
            late,
        )
        parts = (part, flip(part, PAIR))
        if layer + 1 < layer_count:
            early = others(ids, ff_sets[layer + 1], depth, 0, 2, (part,))
        saved_layers.append(
            (
                qkv_w,
                out_w,
                ff_w,
                down_w,
                gain_attn,
                gain_mlp,
                residual,
                normed_attn,
                query,
                key_value,
                key_value_turned,
                shared,
                lse,
                attended,
                residual_mid,
                normed_mlp,
                slope,
                scale,
                unit,
            )
        )
        residual = residual_mid
    residual = residual + (parts[0].astype(F32) + parts[1].astype(F32))
    layer_out = own_rows(residual)

    def outer_sum(total):
        for bit in outer_bits:
            total = add(total, flip(total, bit), steps=1)
        return total

    def sum_ff(share, after=()):
        cut = 2 * ff_block
        totals = cross(share, flip(share[:, :cut], ROW), flip(share[:, cut:], SIDE), after)
        return [outer_sum(total) for total in totals]

    def spread_ff(totals):
        gate, up = totals
        gates, ups = [gate, flip(gate, SIDE)], [up, flip(up, ROW)]
        for group in (gates, ups):
            group += [flip(part, PAIR) for part in group]
        return gates + ups

    def sum_rows(share, cut, after=()):
        totals = split_sum(
            share, flip(share[:, :cut], SIDE), flip(share[:, cut:], ROW), after
        )
        return [outer_sum(total) for total in totals]

    def spread_rows(totals):
        by_row, by_side = totals
        joined = order(ids, (by_row, flip(by_row, ROW), by_side, flip(by_side, SIDE)))
        return [joined, flip(joined, PAIR)]

    down_cut, attn_cut = 640, 768

    def scatter(total):
        return lax.psum_scatter(total, "wt", scatter_dimension=0, tiled=total.ndim == 2)

    flow = pair_rows(cotangent[0])
    flow, flow_low = flow.astype(F32), flow
    gain_grads = [None] * (2 * layer_count)
    ff_outs, attn_outs = (
        [shaped((layer_count, *weight.shape[1:]), F32) for weight in group]
        for group in ((w_gate, w_up, w_down), (w_query, w_key, w_value, w_out))
    )
    ff_held = attn_held = None
    shares = {}
    for layer in reversed(range(layer_count)):
        (
            qkv_w,
            out_w,
            ff_w,
            down_w,
            gain_attn,
            gain_mlp,
            residual,
            normed_attn,
            query,
            key_value,
            key_value_turned,
            shared,
            lse,
            attended,
            residual_mid,
            normed_mlp,
            slope,
            scale,
            unit,
        ) = saved_layers[layer]
        older = shares.get(layer + 1)
        row_keep, row_send, side_keep, side_send = down_grad(ids, unit, flow_low, down_cut)
        down_parts = (row_keep, flip(row_send, ROW)), (side_keep, flip(side_send, SIDE))
        done = (row_keep,) if older is None else (row_keep, attn_all)
        gate_keep, gate_send, up_keep, up_send, part = mlp_back(
            flow_low, normed_mlp, slope, scale, down_w, ff_w, after=done
        )
        gate_got, up_got = flip(gate_send, SIDE), flip(up_send, ROW)
        done = () if older is None else (older["ff"],)
        part, down_sum = add_two(*down_parts, done, part)
        done = (down_sum,)
        flow, flow_low, gain_grads[layer_count + layer] = norm_back(
            flow, (part, flip(part, PAIR)), residual_mid, gain_mlp, after=done
        )
        attended_grad = dot_nt(out_w, flow_low).astype(BF16)
        query_grad, own_grad, shared_grad = attend_back(
            query,
            attended_grad,
            key_value,
            key_value_turned,
            shared,
            key_pos,
            row_pos,
            lse,
            cosine,
            sine,
        )
        for bit in reversed(key_bits):
            half = shared_grad.shape[0] // 2
            arrived = flip(shared_grad[half:].astype(BF16), bit)
            shared_grad = shared_grad[:half] + arrived.astype(F32)
            if bit == key_bits[-1]:
                started = shared_grad
        shares[layer] = {"down": scatter(down_sum)}
        done = (started, shares[layer]["down"])
        if older is not None:
            done = (*done, older["attn"])
        ff_sum = add_two((gate_keep, gate_got), (up_keep, up_got), done)
        shares[layer]["ff"] = scatter(ff_sum)
        down_totals = sum_rows(shares[layer]["down"], down_cut, (ff_sum,))
        done = (ff_sum, down_totals[0])
        if older is not None:
            ff_totals = sum_ff(older["ff"], (ff_sum,))
            attn_totals = sum_rows(older["attn"], attn_cut, (ff_sum,))
            done = (*done, ff_totals[0], attn_totals[0])
        grad_qkv = merge(query_grad, own_grad, shared_grad, cosine, sine, done)
        part = dot_nt(grad_qkv, qkv_w).astype(BF16)
        shares[layer]["down"] = spread_rows(down_totals)
        done = (shares[layer]["down"][0],)
        if older is not None:
            older["ff"] = spread_ff(ff_totals)
            older["attn"] = spread_rows(attn_totals)
            done = (*done, older["ff"][1], older["ff"][5], older["attn"][0])
        row_keep, row_send, side_keep, side_send = attn_grad(
            ids, normed_attn, grad_qkv, attended, flow_low, attn_cut, done
        )
        attn_mine, send = attn_sum(
            pair[None], (row_keep, flip(row_send, ROW), side_keep, flip(side_send, SIDE))
        )
        flow, flow_low, gain_grads[layer] = norm_back(
            flow, (part, flip(part, PAIR)), residual, gain_attn, after=(attn_mine,)
        )
        attn_all = attn_join(pair[None], attn_mine, flip(send, PAIR))
        shares[layer]["attn"] = scatter(attn_all)
    gain_total = jnp.concatenate(gain_grads, axis=0)
    for bit in [SIDE, ROW] + outer_bits:
        gain_total = gain_total + flip(gain_total, bit)
    bit = 1
    while bit < wt_count:
        gain_total = gain_total + flip(gain_total, bit, "wt", wt_count)
        bit *= 2
    for layer in reversed(range(layer_count)):
        share = shares[layer]
        if layer == 0:
            share["ff"] = spread_ff(sum_ff(share["ff"], (placed, attn_placed)))
        *ff_held, placed = place(
            place_ff_kernel, layer, where, share["ff"] + share["down"], ff_outs, ff_held, (flow_low,)
        )
        if layer == 0:
            totals = sum_rows(share["attn"], attn_cut, (placed, gain_total))
            share["attn"] = spread_rows(totals)
        *attn_held, attn_placed = place(
            place_attn_kernel, layer, where, share["attn"], attn_outs, attn_held, (flow_low,)
        )
    query_out, key_out, value_out, out_out = attn_held
    gate_out, up_out, down_out = ff_held
    token_grad = own_rows(flow)

    gain_share = lax.dynamic_slice(
        gain_total, (0, lax.axis_index("wt") * depth), (2 * layer_count, depth)
    )
    return (
        layer_out[None],
        token_grad[None],
        gain_share[:layer_count],
        query_out,
        key_out,
        value_out,
        out_out,
        gain_share[layer_count:],
        gate_out,
        up_out,
        down_out,
    )


def solution(mesh):
    weight = P(None, "wt", None)
    return jax.shard_map(
        per_device,
        mesh=mesh,
        in_specs=(
            P("wt", "ctx", None),
            P("wt", None),
            P("wt", "ctx", None),
            P(None, "wt"),
            weight,
            weight,
            weight,
            weight,
            P(None, "wt"),
            weight,
            weight,
            weight,
        ),
        out_specs=(
            P("wt", "ctx", None),
            P("wt", "ctx", None),
            P(None, "wt"),
            weight,
            weight,
            weight,
            weight,
            P(None, "wt"),
            weight,
            weight,
            weight,
        ),
        check_vma=False,
    )
```

```python
import functools
import math

import jax
import jax.numpy as jnp
from jax import lax
from jax.experimental import pallas as pl
from jax.experimental.pallas import tpu as pltpu
from jax.sharding import PartitionSpec as P

HEADS = 18
KV_HEADS = 6
HEAD_DIM = 64
HALF = 32
CONT = 256
SHARED = HEADS // KV_HEADS
PAIR_KV = KV_HEADS // 2
PAIR_HEADS = HEADS // 2
RUN = 2 * HALF + CONT
ROWS = 2 * RUN
PROMPT = 4 * HALF
TAIL = 2 * CONT

EPSILON = 1e-05
SCORE_SCALE = 0.125
BASE_TWO = SCORE_SCALE * math.log2(math.e)
MASKED = -1e30

BF16 = jnp.bfloat16
F32 = jnp.float32

PAIR, SIDE, ROW = 1, 2, 4


def dot_nn(left, right):
    return lax.dot_general(left, right, (((1,), (0,)), ((), ())), preferred_element_type=F32)


def dot_nt(left, right):
    return lax.dot_general(left, right, (((1,), (1,)), ((), ())), preferred_element_type=F32)


def dot_tn(left, right):
    return lax.dot_general(left, right, (((0,), (0,)), ((), ())), preferred_element_type=F32)


def dot_tt(left, right):
    return lax.dot_general(left, right, (((0,), (1,)), ((), ())), preferred_element_type=F32)


def turned(value):
    return jnp.transpose(value.astype(F32))


def shaped(shape, dtype):
    return jax.ShapeDtypeStruct(shape, dtype)


WHOLE = pl.BlockSpec(memory_space=pltpu.VMEM)
FAR = pl.BlockSpec(memory_space=pl.ANY)
SCALARS = pl.BlockSpec(memory_space=pltpu.SMEM)


def call(
    kernel, outs, ins, limit, out_specs=None, in_specs=None, after=(), far_in=0, far_out=0, **extra
):
    count, waited = len(ins), len(after)

    def body(*refs):
        kernel(*refs[:count], *refs[count + waited :])

    ins = [
        pltpu.with_memory_space_constraint(value, pltpu.HBM) if index < far_in else value
        for index, value in enumerate(ins)
    ]
    outs = [
        pltpu.HBM(out.shape, out.dtype) if index < far_out else out
        for index, out in enumerate(outs)
    ]
    return pl.pallas_call(
        body,
        out_shape=outs,
        in_specs=(in_specs or [WHOLE] * count) + [FAR] * waited,
        out_specs=out_specs or [WHOLE] * len(outs),
        compiler_params=pltpu.CompilerParams(vmem_limit_bytes=limit << 20),
        cost_estimate=pl.CostEstimate(flops=1, bytes_accessed=1, transcendentals=0),
        **extra,
    )(*ins, *after)


def add_norm_kernel(has_parts, *refs):
    if has_parts:
        held, mine, other, gain, total_ref, normed_ref = refs
        total = held[...] + (mine[...].astype(F32) + other[...].astype(F32))
        total_ref[...] = total
    else:
        held, gain, normed_ref = refs
        total = held[...]
    inverse = lax.rsqrt(jnp.mean(total * total, axis=-1, keepdims=True) + EPSILON)
    normed_ref[...] = (total * inverse * gain[...]).astype(BF16)


def add_norm(held, parts, gain, after=()):
    rows, width = held.shape
    step = 128
    block = pl.BlockSpec((step, width), lambda i: (i, 0))
    line = pl.BlockSpec((1, width), lambda i: (0, 0))
    ins = (held, *parts, gain)
    outs = ([shaped(held.shape, F32)] if parts else []) + [shaped(held.shape, BF16)]
    result = call(
        functools.partial(add_norm_kernel, bool(parts)),
        outs,
        ins,
        10,
        in_specs=[block] * (1 + len(parts)) + [line],
        out_specs=[block] * len(outs),
        grid=(rows // step,),
        after=after,
    )
    return result if parts else (held, result[0])


def norm_back_kernel(flow, mine, other, held, gain, flow_ref, low_ref, gain_ref):
    grad = mine[...].astype(F32) + other[...].astype(F32)
    value = held[...]
    inverse = lax.rsqrt(jnp.mean(value * value, axis=-1, keepdims=True) + EPSILON)
    plain = value * inverse
    scaled = grad * gain[...]
    tilt = jnp.mean(scaled * plain, axis=-1, keepdims=True)
    total = flow[...] + inverse * (scaled - plain * tilt)
    flow_ref[...] = total
    low_ref[...] = total.astype(BF16)

    @pl.when(pl.program_id(0) == 0)
    def _():
        gain_ref[...] = jnp.zeros_like(gain_ref)

    gain_ref[...] += jnp.sum(grad * plain, axis=0, keepdims=True)


def norm_back(flow, parts, held, gain, after=(), pinned=False):
    rows, width = held.shape
    step = 128
    block = pl.BlockSpec((step, width), lambda i: (i, 0))
    line = pl.BlockSpec((1, width), lambda i: (0, 0))
    return call(
        norm_back_kernel,
        [shaped(held.shape, F32), shaped(held.shape, BF16), shaped((1, width), F32)],
        (flow, *parts, held, gain),
        12,
        in_specs=[block] * 4 + [line],
        out_specs=[block, block, line],
        grid=(rows // step,),
        after=after,
        far_in=4 if pinned else 0,
    )


def add_kernel(mine, other, out):
    out[...] = (mine[...].astype(F32) + other[...].astype(F32)).astype(BF16)


def add_two_kernel(first_mine, first_other, second_mine, second_other, *refs):
    out = refs[-1]
    if len(refs) == 3:
        refs[1][...] = refs[0][...]
    first = first_mine[...].astype(F32) + first_other[...].astype(F32)
    second = second_mine[...].astype(F32) + second_other[...].astype(F32)
    axis = len(out.shape) - 1
    out[...] = jnp.concatenate([first.astype(BF16), second.astype(BF16)], axis=axis)


def add_two(first, second, after=(), passed=None):
    ins = (*first, *second)
    lead = first[0].shape[:-1]
    steps = 4

    def block(*shape):
        shape = (shape[0] // steps, *shape[1:])
        return pl.BlockSpec(shape, lambda i: (i,) + (0,) * (len(shape) - 1))

    columns = first[0].shape[-1] + second[0].shape[-1]
    extra = () if passed is None else (passed,)
    result = call(
        add_two_kernel,
        [shaped(part.shape, part.dtype) for part in extra] + [shaped((*lead, columns), BF16)],
        (*ins, *extra),
        12,
        in_specs=[block(*part.shape) for part in (*ins, *extra)],
        out_specs=[block(*part.shape) for part in extra] + [block(*lead, columns)],
        grid=(steps,),
        after=after,
        far_in=4,
    )
    return result if extra else result[0]


def split_sum_kernel(share, row_other, side_other, row_out, side_out):
    cut = row_out.shape[1]
    row_out[...] = (share[:, :cut].astype(F32) + row_other[...].astype(F32)).astype(BF16)
    side_out[...] = (share[:, cut:].astype(F32) + side_other[...].astype(F32)).astype(BF16)


def split_sum(share, row_other, side_other, after=()):
    return call(
        split_sum_kernel,
        [shaped(row_other.shape, BF16), shaped(side_other.shape, BF16)],
        (share, row_other, side_other),
        8,
        after=after,
    )


def order_kernel(ids_ref, row_mine, row_other, side_mine, side_other, out):
    side, row = ids_ref[4], ids_ref[3]
    half, cut = row_mine.shape
    for value, mine, other, cols in (
        (row, row_mine, row_other, slice(0, cut)),
        (side, side_mine, side_other, slice(cut, None)),
    ):
        for index in range(2):
            chosen = jnp.where(value == index, mine[...], other[...])
            out[index * half : (index + 1) * half, cols] = chosen


def order(ids, parts):
    half, cut = parts[0].shape
    return call(
        order_kernel,
        [shaped((2 * half, cut + parts[2].shape[1]), BF16)],
        (ids, *parts),
        8,
        in_specs=[SCALARS] + [WHOLE] * 4,
    )[0]


def cross_kernel(share, gate_other, up_other, gate_out, up_out):
    block = gate_out.shape[1] // 2
    for out, other, low in ((gate_out, gate_other, 0), (up_out, up_other, 2 * block)):
        for index in range(2):
            mine = share[:, low + index * block : low + (index + 1) * block]
            theirs = other[:, (1 - index) * block : (2 - index) * block]
            out[:, index * block : (index + 1) * block] = (
                mine.astype(F32) + theirs.astype(F32)
            ).astype(BF16)


def cross(share, gate_other, up_other, after=()):
    shape = (share.shape[0], share.shape[1] // 2)
    return call(
        cross_kernel,
        [shaped(shape, BF16)] * 2,
        (share, gate_other, up_other),
        8,
        after=after,
    )


def add(mine, other, after=(), steps=4):
    shape = mine.shape
    block = pl.BlockSpec(
        (shape[0] // steps, *shape[1:]), lambda i: (i,) + (0,) * (len(shape) - 1)
    )
    return call(
        add_kernel,
        [shaped(shape, BF16)],
        (mine, other),
        12,
        in_specs=[block, block],
        out_specs=[block],
        grid=(steps,),
        after=after,
    )[0]


KEY_HALF = PAIR_KV * HEAD_DIM
QUERY_HALF = PAIR_HEADS * HEAD_DIM
QKV = 2 * KEY_HALF + QUERY_HALF


def rope_kernel(qkv_ref, cos_ref, sin_ref, query_ref, kv_ref, kv_turned_ref):
    cosine, sine = cos_ref[...], sin_ref[...]
    half = HEAD_DIM // 2

    def head(source, target_ref, target):
        low = qkv_ref[source : source + half, :]
        high = qkv_ref[source + half : source + 2 * half, :]
        target_ref[target : target + half, :] = (low * cosine - high * sine).astype(BF16)
        target_ref[target + half : target + 2 * half, :] = (high * cosine + low * sine).astype(
            BF16
        )

    for index in range(PAIR_KV):
        head(index * HEAD_DIM, kv_turned_ref, index * HEAD_DIM)
    kv_turned_ref[KEY_HALF:, :] = qkv_ref[KEY_HALF : 2 * KEY_HALF, :].astype(BF16)
    kv_ref[...] = turned(kv_turned_ref[...]).astype(BF16)
    for index in range(PAIR_HEADS):
        head(2 * KEY_HALF + index * HEAD_DIM, query_ref, index * HEAD_DIM)


def rope(qkv, cosine, sine, after=()):
    return call(
        rope_kernel,
        [
            shaped((QUERY_HALF, ROWS), BF16),
            shaped((ROWS, 2 * KEY_HALF), BF16),
            shaped((2 * KEY_HALF, ROWS), BF16),
        ],
        (qkv, cosine, sine),
        14,
        after=after,
    )


def later_mask():
    key = lax.broadcasted_iota(jnp.int32, (CONT, CONT), 0)
    query = lax.broadcasted_iota(jnp.int32, (CONT, CONT), 1)
    return key <= query


def attend_kernel(
    query_ref, kv_ref, kv_turned_ref, shared_ref, key_pos_ref, row_pos_ref, out_ref, lse_ref
):
    shared_values = turned(shared_ref[:, KEY_HALF:]).astype(BF16)
    for kv_head in range(PAIR_KV):
        low = kv_head * HEAD_DIM
        keys = shared_ref[:, low : low + HEAD_DIM]
        values = shared_values[low : low + HEAD_DIM, :]

        def head(index, carry, kv_head=kv_head, low=low, keys=keys, values=values):
            number = kv_head * SHARED + index
            base = pl.multiple_of(number * HEAD_DIM, HEAD_DIM)
            allowed = key_pos_ref[...] <= row_pos_ref[...]
            query = query_ref[pl.ds(base, HEAD_DIM), TAIL:]
            scores = jnp.where(allowed, dot_nn(keys, query) * BASE_TWO, MASKED)
            top = jnp.max(scores, axis=0, keepdims=True)
            weight = jnp.exp2(scores - top)
            total = jnp.sum(weight, axis=0, keepdims=True)
            out = dot_nn(values, weight.astype(BF16)) / total
            out_ref[pl.ds(base, HEAD_DIM), TAIL:] = out.astype(BF16)
            lse_ref[number, :, TAIL:] = top + jnp.log2(total)
            for run in range(2):
                cols = slice(run * CONT, (run + 1) * CONT)
                query = query_ref[pl.ds(base, HEAD_DIM), cols]
                own_keys = kv_ref[cols, low : low + HEAD_DIM]
                own_values = kv_turned_ref[KEY_HALF + low : KEY_HALF + low + HEAD_DIM, cols]
                first = dot_nn(keys, query) * BASE_TWO
                second = jnp.where(later_mask(), dot_nn(own_keys, query) * BASE_TWO, MASKED)
                top = jnp.maximum(
                    jnp.max(first, axis=0, keepdims=True), jnp.max(second, axis=0, keepdims=True)
                )
                first = jnp.exp2(first - top)
                second = jnp.exp2(second - top)
                total = jnp.sum(first, axis=0, keepdims=True) + jnp.sum(
                    second, axis=0, keepdims=True
                )
                out = dot_nn(values, first.astype(BF16)) + dot_nn(
                    own_values, second.astype(BF16)
                )
                out_ref[pl.ds(base, HEAD_DIM), cols] = (out / total).astype(BF16)
                lse_ref[number, :, cols] = top + jnp.log2(total)
            return carry

        lax.fori_loop(0, SHARED, head, 0)


def attend(query, key_value, key_value_turned, shared, key_pos, row_pos, after=()):
    return call(
        attend_kernel,
        [shaped((QUERY_HALF, ROWS), BF16), shaped((PAIR_HEADS, 1, ROWS), F32)],
        (query, key_value, key_value_turned, shared, key_pos, row_pos),
        16 + shared.shape[0] // 64,
        after=after,
    )


def attend_back_kernel(
    query_ref,
    grad_ref,
    kv_ref,
    kv_turned_ref,
    shared_ref,
    key_pos_ref,
    row_pos_ref,
    lse_ref,
    cos_ref,
    sin_ref,
    query_grad_ref,
    own_grad_ref,
    shared_grad_ref,
    score_keep,
    weight_keep,
    own_score_keep,
    own_weight_keep,
):
    shared_turned = turned(shared_ref[:, :KEY_HALF]).astype(BF16)
    half = HEAD_DIM // 2
    for kv_head in range(PAIR_KV):
        low = kv_head * HEAD_DIM
        keys = shared_ref[:, low : low + HEAD_DIM]
        values = shared_ref[:, KEY_HALF + low : KEY_HALF + low + HEAD_DIM]
        keys_turned = shared_turned[low : low + HEAD_DIM, :]

        def head(index, carry, kv_head=kv_head, low=low, keys=keys, values=values, keys_turned=keys_turned):
            number = kv_head * SHARED + index
            base = pl.multiple_of(number * HEAD_DIM, HEAD_DIM)

            def put_query_grad(grad, cols):
                cosine, sine = cos_ref[:, cols], sin_ref[:, cols]
                first, second = grad[:half], grad[half:]
                query_grad_ref[pl.ds(base, half), cols] = (
                    (first * cosine + second * sine) * SCORE_SCALE
                ).astype(BF16)
                query_grad_ref[pl.ds(base + half, half), cols] = (
                    (second * cosine - first * sine) * SCORE_SCALE
                ).astype(BF16)

            cols = slice(TAIL, ROWS)
            query = query_ref[pl.ds(base, HEAD_DIM), cols]
            grad = grad_ref[pl.ds(base, HEAD_DIM), cols]
            lse = lse_ref[number, :, cols]
            allowed = key_pos_ref[...] <= row_pos_ref[...]
            scores = jnp.where(allowed, dot_nn(keys, query) * BASE_TWO, MASKED)
            weight = jnp.exp2(scores - lse)
            weight_keep[index, :, cols] = weight.astype(BF16)
            flow = weight * dot_nn(values, grad)
            delta = jnp.sum(flow, axis=0, keepdims=True)
            flow = (flow - weight * delta).astype(BF16)
            score_keep[index, :, cols] = flow
            put_query_grad(dot_nn(keys_turned, flow), cols)
            for run in range(2):
                cols = slice(run * CONT, (run + 1) * CONT)
                query = query_ref[pl.ds(base, HEAD_DIM), cols]
                grad = grad_ref[pl.ds(base, HEAD_DIM), cols]
                lse = lse_ref[number, :, cols]
                own_keys = kv_ref[cols, low : low + HEAD_DIM]
                own_values = kv_ref[cols, KEY_HALF + low : KEY_HALF + low + HEAD_DIM]
                own_turned = kv_turned_ref[low : low + HEAD_DIM, cols]
                first = jnp.exp2(dot_nn(keys, query) * BASE_TWO - lse)
                second = jnp.where(later_mask(), dot_nn(own_keys, query) * BASE_TWO, MASKED)
                second = jnp.exp2(second - lse)
                weight_keep[index, :, cols] = first.astype(BF16)
                own_weight_keep[index, :, cols] = second.astype(BF16)
                first_flow = first * dot_nn(values, grad)
                second_flow = second * dot_nn(own_values, grad)
                delta = jnp.sum(first_flow, axis=0, keepdims=True) + jnp.sum(
                    second_flow, axis=0, keepdims=True
                )
                first_flow = (first_flow - first * delta).astype(BF16)
                second_flow = (second_flow - second * delta).astype(BF16)
                score_keep[index, :, cols] = first_flow
                own_score_keep[index, :, cols] = second_flow
                put_query_grad(
                    dot_nn(keys_turned, first_flow) + dot_nn(own_turned, second_flow), cols
                )
            return carry

        lax.fori_loop(0, SHARED, head, 0)
        key_sum, value_sum = 0.0, 0.0
        own_key_sum, own_value_sum = [0.0, 0.0], [0.0, 0.0]
        for index in range(SHARED):
            base = (kv_head * SHARED + index) * HEAD_DIM
            query = query_ref[base : base + HEAD_DIM, :]
            grad = grad_ref[base : base + HEAD_DIM, :]
            key_sum = key_sum + dot_nt(score_keep[index], query)
            value_sum = value_sum + dot_nt(weight_keep[index], grad)
            for run in range(2):
                cols = slice(run * CONT, (run + 1) * CONT)
                own_key_sum[run] = own_key_sum[run] + dot_nt(
                    own_score_keep[index, :, cols], query[:, cols]
                )
                own_value_sum[run] = own_value_sum[run] + dot_nt(
                    own_weight_keep[index, :, cols], grad[:, cols]
                )
        shared_grad_ref[:, low : low + HEAD_DIM] = key_sum * SCORE_SCALE
        shared_grad_ref[:, KEY_HALF + low : KEY_HALF + low + HEAD_DIM] = value_sum
        for run in range(2):
            cols = slice(run * CONT, (run + 1) * CONT)
            own_grad_ref[cols, low : low + HEAD_DIM] = own_key_sum[run] * SCORE_SCALE
            own_grad_ref[cols, KEY_HALF + low : KEY_HALF + low + HEAD_DIM] = own_value_sum[run]


def attend_back(
    query, grad, key_value, key_value_turned, shared, key_pos, row_pos, lse, cosine, sine, after=()
):
    count = shared.shape[0]
    return call(
        attend_back_kernel,
        [
            shaped((QUERY_HALF, ROWS), BF16),
            shaped((TAIL, 2 * KEY_HALF), F32),
            shaped((count, 2 * KEY_HALF), F32),
        ],
        (query, grad, key_value, key_value_turned, shared, key_pos, row_pos, lse, cosine, sine),
        22 + count // 64,
        scratch_shapes=[
            pltpu.VMEM((SHARED, count, ROWS), BF16),
            pltpu.VMEM((SHARED, count, ROWS), BF16),
            pltpu.VMEM((SHARED, CONT, TAIL), BF16),
            pltpu.VMEM((SHARED, CONT, TAIL), BF16),
        ],
        after=after,
    )


def merge_kernel(query_grad_ref, own_ref, prompt_ref, cos_ref, sin_ref, out_ref):
    cosine, sine = cos_ref[...], sin_ref[...]
    half = HEAD_DIM // 2
    both = turned(jnp.concatenate([own_ref[...], prompt_ref[...]], axis=0))
    pieces = []
    for index in range(PAIR_KV):
        low = both[index * HEAD_DIM : index * HEAD_DIM + half]
        high = both[index * HEAD_DIM + half : (index + 1) * HEAD_DIM]
        pieces += [low * cosine + high * sine, high * cosine - low * sine]
    both = jnp.concatenate(pieces + [both[KEY_HALF:]], axis=0)
    out_ref[:, : 2 * KEY_HALF] = jnp.transpose(both).astype(BF16)
    out_ref[:, 2 * KEY_HALF :] = turned(query_grad_ref[...]).astype(BF16)


def merge(query_grad, own_grad, prompt_grad, cosine, sine, after=()):
    return call(
        merge_kernel,
        [shaped((ROWS, QKV), BF16)],
        (query_grad, own_grad, prompt_grad, cosine, sine),
        16,
        after=after,
    )[0]


def mlp_kernel(layer, ids_ref, normed_ref, *refs):
    own = refs[0]
    from_row, from_side, from_across = refs[1:3], refs[3:5], refs[5:9]
    gate_ref, up_ref, down_shard = (ref.at[layer] for ref in refs[9:12])
    weight_ref, down_ref, slope_ref, scale_ref, unit_ref, out_ref = refs[12:18]
    held, sems, down_sem, keep_sem = refs[18:]
    rows, depth = normed_ref.shape
    block = held.shape[2] // 2
    shard = depth // 4
    lines = block // 4
    wide = depth // 3
    quarter, plane, pair = ids_ref[0], ids_ref[1], ids_ref[2]
    slots = line_slots(plane)

    def copy(source, target, sem):
        pltpu.make_async_copy(source, target, sem).start()

    def at(start, size):
        return pl.ds(pl.multiple_of(start, 16), size)

    def pieces(part):
        if part == 0:
            return [(own.at[owner], 0, shard, owner) for owner in (plane, *slots)]
        if part < 3:
            pair_of_slots, last = (from_row, from_side)[part - 1]
            arrived = (pair_of_slots.at[0], pair_of_slots.at[1], last.at[0])
            return [(arrived[slot], 0, shard, slots[slot]) for slot in range(3)]
        half = shard // 2
        return [
            (from_across[0], 0, shard, slots[0]),
            (from_across[1], 0, shard, slots[1]),
            (from_across[2], 0, half, slots[2]),
            (from_across[3], half, shard, slots[2]),
        ]

    for part in range(4):
        for source, low, high, owner in pieces(part):
            copy(
                source.at[:, : 2 * block],
                held.at[part, at(shard * owner + low, high - low)],
                sems.at[part],
            )
        if part == 0:
            continue
        col = pl.ds(pl.multiple_of((2 * (quarter ^ part) + pair) * block, block), block)
        for index, ref in enumerate((gate_ref, up_ref)):
            copy(
                ref.at[:, col],
                held.at[part, at(shard * plane, shard), pl.ds(index * block, block)],
                sems.at[part],
            )
    taken = pl.ds(2 * block, wide)

    def down_copies(source, low, high, place, piece):
        for column in range(3):
            first, last = max(low, lines * column), min(high, lines * (column + 1))
            if first < last:
                copy(
                    source.at[at(first - low, last - first), taken],
                    down_ref.at[
                        at(
                            block * place + lines * (quarter ^ piece) + first - lines * column,
                            last - first,
                        ),
                        pl.ds(wide * column, wide),
                    ],
                    down_sem,
                )

    for part in range(4):
        for source, low, high, owner in pieces(part):
            down_copies(source, low, high, quarter ^ owner, part)
        if part == 0:
            continue
        copy(
            down_shard.at[at(block * pair + lines * (quarter ^ part), lines)],
            down_ref.at[at(block * (quarter ^ plane) + lines * (quarter ^ part), lines)],
            down_sem,
        )

    step = rows // 2
    kept = []
    for part in range(4):
        pltpu.make_async_copy(held.at[part], held.at[part], sems.at[part]).wait()
        kept.append(pltpu.make_async_copy(held.at[part], weight_ref.at[part], keep_sem.at[part]))
        kept[-1].start()

        def tile(index, carry, part=part):
            some = pl.ds(pl.multiple_of(index * step, step), step)
            normed = normed_ref[some, :]
            gate = dot_nn(normed, held[part, :, :block])
            up = dot_nn(normed, held[part, :, block:])
            sigmoid = 1.0 / (1.0 + jnp.exp(-gate))
            scale = gate * sigmoid
            cols = slice(part * block, (part + 1) * block)
            slope_ref[some, cols] = (up * sigmoid * (1.0 + gate * (1.0 - sigmoid))).astype(BF16)
            scale_ref[some, cols] = scale.astype(BF16)
            unit_ref[some, cols] = (scale * up).astype(BF16)
            return carry

        lax.fori_loop(0, 2, tile, 0)
    pltpu.make_async_copy(down_ref, down_ref, down_sem).wait()

    def finish(index, carry):
        some = pl.ds(pl.multiple_of(index * step, step), step)
        out_ref[some, :] = dot_nn(unit_ref[some, :], down_ref[...]).astype(BF16)
        return carry

    lax.fori_loop(0, 2, finish, 0)
    for part in kept:
        part.wait()


def mlp(layer, ids, normed, pieces, weights, block, after=()):
    rows, depth = normed.shape
    units = 4 * block
    ins = (ids, normed, *pieces, *weights)
    return call(
        functools.partial(mlp_kernel, layer),
        [
            shaped((4, depth, 2 * block), BF16),
            shaped((units, depth), BF16),
            shaped((rows, units), BF16),
            shaped((rows, units), BF16),
            shaped((rows, units), BF16),
            shaped((rows, depth), BF16),
        ],
        ins,
        32,
        in_specs=[SCALARS, WHOLE] + [FAR] * (len(ins) - 2),
        out_specs=[FAR] + [WHOLE] * 5,
        scratch_shapes=[
            pltpu.VMEM((4, depth, 2 * block), BF16),
            pltpu.SemaphoreType.DMA((4,)),
            pltpu.SemaphoreType.DMA,
            pltpu.SemaphoreType.DMA((4,)),
        ],
        after=after,
    )


def pack_kernel(layer, ids_ref, gate_ref, up_ref, down_ref, out, sem):
    quarter, pair = ids_ref[0], ids_ref[2]
    depth, columns = out.shape
    wide = columns // 3
    lines = depth // 3
    col = pl.ds(pl.multiple_of((2 * quarter + pair) * wide, wide), wide)
    for index, ref in enumerate((gate_ref, up_ref)):
        target = out.at[:, pl.ds(index * wide, wide)]
        pltpu.make_async_copy(ref.at[layer, :, col], target, sem).start()
    start = pl.multiple_of((4 * pair + quarter) * lines, lines)
    for index in range(3):
        pltpu.make_async_copy(
            down_ref.at[layer, pl.ds(start, lines), pl.ds(index * wide, wide)],
            out.at[pl.ds(index * lines, lines), pl.ds(2 * wide, wide)],
            sem,
        ).start()
    pltpu.make_async_copy(out, out, sem).wait()


def pack(layer, ids, weights, after=()):
    _, depth, units = weights[0].shape
    return call(
        functools.partial(pack_kernel, layer),
        [shaped((depth, 3 * units // 8), BF16)],
        (ids, *weights),
        16,
        in_specs=[SCALARS] + [FAR] * 3,
        scratch_shapes=[pltpu.SemaphoreType.DMA],
        after=after,
    )[0]


def deal(total, row, side, cut, place, row_keep, row_send, side_keep, side_send):
    half = total.shape[0] // 2
    for index in range(2):
        part = total[index * half : (index + 1) * half]
        for value, keep, send, cols in (
            (row, row_keep, row_send, slice(0, cut)),
            (side, side_keep, side_send, slice(cut, None)),
        ):

            @pl.when(value == index)
            def _(part=part, keep=keep, cols=cols):
                keep[place] = part[:, cols]

            @pl.when(value != index)
            def _(part=part, send=send, cols=cols):
                send[place] = part[:, cols]


def dealt(blocks, half, columns, cut):
    return [
        shaped((blocks, half, size), BF16) for size in (cut, cut, columns - cut, columns - cut)
    ]


def down_grad_kernel(cut, ids_ref, unit_ref, flow_ref, *outs):
    quarter, side, row = ids_ref[0], ids_ref[4], ids_ref[3]
    block = unit_ref.shape[1] // 4
    for place in range(4):
        total = dot_tn(unit_ref[:, place * block : (place + 1) * block], flow_ref[...])
        deal(total.astype(BF16), row, side, cut, quarter ^ place, *outs)


def down_grad(ids, unit, flow, cut, after=()):
    rows, units = unit.shape
    width = flow.shape[1]
    return call(
        functools.partial(down_grad_kernel, cut),
        dealt(4, units // 8, width, cut),
        (ids, unit, flow),
        16,
        in_specs=[SCALARS, WHOLE, WHOLE],
        after=after,
    )


def mlp_back_kernel(
    flow_ref,
    normed_ref,
    slope_ref,
    scale_ref,
    down_ref,
    weight_ref,
    gate_keep,
    gate_send,
    up_keep,
    up_send,
    out_ref,
    held,
    total,
    unit_grad,
    sems,
):
    rows, depth = normed_ref.shape
    block = held.shape[2] // 2
    order = (3, 2, 1, 0)
    copies = {
        part: pltpu.make_async_copy(weight_ref.at[part], held.at[part], sems.at[part])
        for part in order
    }
    for part in order:
        copies[part].start()
    step = rows // 2
    for part in order:
        cols = slice(part * block, (part + 1) * block)

        def tile(index, carry, cols=cols):
            at = pl.ds(pl.multiple_of(index * step, step), step)
            grad = dot_nt(flow_ref[at, :], down_ref[cols, :])
            unit_grad[at, :block] = (grad * slope_ref[at, cols].astype(F32)).astype(BF16)
            unit_grad[at, block:] = (grad * scale_ref[at, cols].astype(F32)).astype(BF16)
            return carry

        lax.fori_loop(0, 2, tile, 0)
        both = dot_tn(normed_ref[...], unit_grad[...]).astype(BF16)
        target = gate_send if part >= 2 else gate_keep
        target[:, (part % 2) * block : (part % 2 + 1) * block] = both[:, :block]
        target = up_send if part % 2 else up_keep
        target[:, (part // 2) * block : (part // 2 + 1) * block] = both[:, block:]
        copies[part].wait()

        def gather(index, carry, part=part):
            at = pl.ds(pl.multiple_of(index * step, step), step)
            value = dot_nt(unit_grad[at, :], held[part])
            if part == order[0]:
                total[at, :] = value
            elif part == order[-1]:
                out_ref[at, :] = (total[at, :] + value).astype(BF16)
            else:
                total[at, :] += value
            return carry

        lax.fori_loop(0, 2, gather, 0)


def mlp_back(flow, normed, slope, scale, down, weights, after=()):
    rows, depth = normed.shape
    block = down.shape[0] // 4
    return call(
        mlp_back_kernel,
        [shaped((depth, 2 * block), BF16)] * 4 + [shaped((rows, depth), BF16)],
        (flow, normed, slope, scale, down, weights),
        40,
        in_specs=[WHOLE] * 5 + [FAR],
        scratch_shapes=[
            pltpu.VMEM((4, depth, 2 * block), BF16),
            pltpu.VMEM((rows, depth), F32),
            pltpu.VMEM((rows, 2 * block), BF16),
            pltpu.SemaphoreType.DMA((4,)),
        ],
        after=after,
        far_out=4,
    )


def join_kernel(ids_ref, local, mine, other, out, sem):
    plane, row = ids_ref[1], ids_ref[3]
    half = local.shape[0] // 2

    def copy(source, start):
        target = out.at[pl.ds(pl.multiple_of(start, 16), source.shape[0])]
        pltpu.make_async_copy(source, target, sem).start()

    copy(local, 2 * half * plane)
    for slot, owner in enumerate(line_slots(plane)):
        copy(mine.at[owner, pl.ds(0, half)], half * (2 * owner + row))
        copy(other.at[slot], half * (2 * owner + 1 - row))
    pltpu.make_async_copy(out, out, sem).wait()


def join(ids, local, mine, other, after=()):
    shape = (4 * local.shape[0], local.shape[1])
    return call(
        join_kernel,
        [shaped(shape, BF16)],
        (ids, local, mine, other),
        16,
        in_specs=[SCALARS] + [FAR] * 3,
        scratch_shapes=[pltpu.SemaphoreType.DMA],
        after=after,
    )[0]


def others_kernel(first, ids_ref, gathered, out, sem):
    count, rows, _ = out.shape
    for slot, owner in enumerate(line_slots(ids_ref[1])[first : first + count]):
        pltpu.make_async_copy(gathered.at[owner, pl.ds(0, rows)], out.at[slot], sem).start()
    pltpu.make_async_copy(out, out, sem).wait()


def others(ids, gathered, rows, first, last, after=()):
    return call(
        functools.partial(others_kernel, first),
        [shaped((last - first, rows, gathered.shape[2]), BF16)],
        (ids, gathered),
        16,
        in_specs=[SCALARS, FAR],
        scratch_shapes=[pltpu.SemaphoreType.DMA],
        after=after,
    )[0]


def line_slots(plane):
    return [plane ^ step for step in (1, 2, 3)]


def attn_grad_kernel(cut, ids_ref, normed, grad, attended, flow, *outs):
    side, row = ids_ref[4], ids_ref[3]
    blocks, half, _ = outs[0].shape
    out_cols = flow.shape[1] // 2
    out = dot_nn(attended[...], flow[...]).astype(BF16)
    for block in range(blocks):
        low, col = 2 * (block // 2) * half, (block % 2) * out_cols
        total = jnp.concatenate(
            [
                dot_tn(normed[:, 2 * block * half : 2 * (block + 1) * half], grad[...]).astype(
                    BF16
                ),
                out[low : low + 2 * half, col : col + out_cols],
            ],
            axis=1,
        )
        deal(total, row, side, cut, block, *outs)


def attn_grad(ids, normed, grad, attended, flow, cut, after=()):
    columns = grad.shape[1] + flow.shape[1] // 2
    return call(
        functools.partial(attn_grad_kernel, cut),
        dealt(4, normed.shape[1] // 8, columns, cut),
        (ids, normed, grad, attended, flow),
        20,
        in_specs=[SCALARS] + [WHOLE] * 4,
        after=after,
    )


def attn_sum_kernel(pair_ref, row_mine, row_other, side_mine, side_other, keep_ref, send_ref):
    pair = pair_ref[0]
    total = jnp.concatenate(
        [
            (mine[...].astype(F32) + other[...].astype(F32)).astype(BF16)
            for mine, other in ((row_mine, row_other), (side_mine, side_other))
        ],
        axis=2,
    )
    keep_ref[:, :, :QKV] = total[:, :, :QKV]
    for plane in range(4):
        for owner in range(2):

            @pl.when(pair == owner)
            def _(plane=plane, owner=owner):
                if plane // 2 == owner:
                    keep_ref[plane, :, QKV:] = total[2 * (plane % 2) + owner, :, QKV:]
                else:
                    send_ref[plane % 2] = total[2 * (plane % 2) + 1 - owner, :, QKV:]
                    keep_ref[plane, :, QKV:] = jnp.zeros_like(keep_ref[plane, :, QKV:])


def attn_sum(pair, parts, after=()):
    blocks, half, first = parts[0].shape
    columns = first + parts[2].shape[2]
    return call(
        attn_sum_kernel,
        [
            shaped((blocks, half, columns), BF16),
            shaped((blocks // 2, half, columns - QKV), BF16),
        ],
        (pair, *parts),
        16,
        in_specs=[SCALARS] + [WHOLE] * 4,
        after=after,
    )


def attn_join_kernel(pair_ref, mine, other, out):
    pair = pair_ref[0]
    out[:, :, :QKV] = mine[:, :, :QKV]
    for plane in range(4):
        for owner in range(2):

            @pl.when(pair == owner)
            def _(plane=plane, owner=owner):
                if plane // 2 == owner:
                    out[plane, :, QKV:] = mine[plane, :, QKV:]
                else:
                    out[plane, :, QKV:] = other[plane % 2]


def attn_join(pair, mine, other, after=()):
    return call(
        attn_join_kernel,
        [shaped(mine.shape, BF16)],
        (pair, mine, other),
        12,
        in_specs=[SCALARS, WHOLE, WHOLE],
        after=after,
    )[0]


def place_ff_kernel(where_ref, *refs):
    gates, ups, downs = refs[0:4], refs[4:8], refs[8:10]
    gate_out, up_out, down_out = refs[10:]
    pair, quarter = where_ref[0], where_ref[1]
    block = gates[0].shape[1] // 2
    for out, pieces, spread, inner in ((gate_out, gates, 2, 1), (up_out, ups, 1, 2)):
        for number, ref in enumerate(pieces):
            owner = pair ^ (number // 2)
            for index in range(2):
                plane = quarter ^ ((number % 2) * spread + index * inner)
                col = pl.multiple_of((2 * plane + owner) * block, block)
                out[0, :, pl.ds(col, block)] = ref[
                    :, index * block : (index + 1) * block
                ].astype(F32)
    down_rows = downs[0].shape[0]
    for where_from, owner in ((downs[0], pair), (downs[1], 1 - pair)):
        down_out[0, pl.ds(pl.multiple_of(owner * down_rows, down_rows), down_rows), :] = (
            where_from[...].astype(F32)
        )


def place_attn_kernel(where_ref, attn_mine, attn_other, *refs):
    query_out, key_out, value_out, out_out = refs
    pair = where_ref[0]
    first = jnp.where(pair == 0, attn_mine[...], attn_other[...]).astype(F32)
    second = jnp.where(pair == 0, attn_other[...], attn_mine[...]).astype(F32)
    low = 0
    for out, cols in (
        (key_out, KEY_HALF),
        (value_out, KEY_HALF),
        (query_out, QUERY_HALF),
        (out_out, first.shape[1] - QKV),
    ):
        out[0] = jnp.concatenate([first[:, low : low + cols], second[:, low : low + cols]], axis=1)
        low += cols


def place_kernel(kernel, fresh, parts, outs, *refs):
    here = refs[: 1 + parts]
    there = refs[1 + parts :] if fresh else refs[1 + parts + outs :]
    kernel(*here, *there[:outs])
    there[outs][...] = jnp.zeros_like(there[outs])


def place(kernel, layer, where, parts, outs, held, after=()):
    ins = (where, *parts, *(held or ()))
    specs = [SCALARS] + [WHOLE] * len(parts) + [FAR] * len(held or ())

    def layer_block(out):
        return pl.BlockSpec((1, *out.shape[1:]), lambda _: (layer, 0, 0))

    aliases = {} if held is None else {1 + len(parts) + i: i for i in range(len(outs))}
    return call(
        functools.partial(place_kernel, kernel, held is None, len(parts), len(outs)),
        [*outs, shaped((8, 128), F32)],
        ins,
        48,
        in_specs=specs,
        out_specs=[layer_block(out) for out in outs]
        + [pl.BlockSpec((8, 128), lambda _: (0, 0))],
        input_output_aliases=aliases,
        grid=(1,),
        after=after,
    )


def positions(deal_row, ctx_count):
    row_ids = jnp.arange(RUN, dtype=jnp.int32)
    block_ids = deal_row[..., None]
    lower_block = block_ids * HALF + row_ids
    upper_block = (2 * ctx_count - 1 - block_ids) * HALF + row_ids - HALF
    continued = 2 * HALF * ctx_count + row_ids - 2 * HALF
    return jnp.where(
        row_ids < HALF, lower_block, jnp.where(row_ids < 2 * HALF, upper_block, continued)
    )


def per_device(
    tokens,
    assign,
    cotangent,
    attn_gain,
    w_query,
    w_key,
    w_value,
    w_out,
    mlp_gain,
    w_gate,
    w_up,
    w_down,
):
    ctx_count = lax.axis_size("ctx")
    wt_count = lax.axis_size("wt")
    ctx_index = lax.axis_index("ctx")
    pair = ctx_index % 2
    side = (ctx_index // SIDE) % 2
    row = (ctx_index // ROW) % 2
    quarter = 2 * side + row
    chip = ctx_index // 2
    chip_count = ctx_count // 2
    outer_bits = [bit for bit in (8, 16, 32, 64, 128) if bit < ctx_count]

    layer_count, depth = attn_gain.shape[0], w_query.shape[1]
    width = w_out.shape[2]
    half_width = width // 2
    ff_block = w_down.shape[1] // 2
    ff_piece = ff_block // 4
    half_depth = depth // 2

    def flip(value, bit, axis="ctx", count=None):
        count = ctx_count if count is None else count
        return lax.ppermute(value, axis, [(i, i ^ bit) for i in range(count)])

    def ordered(bit_value, mine, other):
        first = jnp.where(bit_value == 0, mine, other)
        second = jnp.where(bit_value == 0, other, mine)
        return first, second

    def pair_rows(own):
        first, second = ordered(pair, own, flip(own, PAIR))
        cut = 2 * HALF
        return jnp.concatenate([first[cut:], second[cut:], first[:cut], second[:cut]], axis=0)

    def own_rows(both):
        return jnp.concatenate(
            [
                lax.dynamic_slice(both, (TAIL + 2 * HALF * pair, 0), (2 * HALF, width)),
                lax.dynamic_slice(both, (CONT * pair, 0), (CONT, width)),
            ],
            axis=0,
        )

    every_pos = positions(assign[0], ctx_count).reshape(chip_count, 2, RUN)
    key_bits = [ROW, SIDE] + outer_bits
    steps = [0]
    for bit in key_bits:
        steps += [step ^ (bit // 2) for step in steps]
    wanted = chip ^ jnp.array(steps, dtype=jnp.int32)
    picked = wanted[:, None] == jnp.arange(chip_count, dtype=jnp.int32)[None, :]
    prompt_pos = jnp.sum(
        jnp.where(picked[:, :, None, None], every_pos[None, :, :, : 2 * HALF], 0), axis=1
    )
    key_pos = prompt_pos.reshape(-1, 1)
    row_pos = prompt_pos[0].reshape(1, -1)
    cont_pos = every_pos[0, 0, 2 * HALF :]
    own_pos = jnp.concatenate([cont_pos, cont_pos, row_pos[0]])
    half_dim = HEAD_DIM // 2
    frequency = jnp.exp(jnp.arange(half_dim, dtype=F32) * (-jnp.log(10000.0) / half_dim))
    phase = frequency[:, None] * own_pos.astype(F32)[None, :]
    cosine, sine = jnp.cos(phase), jnp.sin(phase)

    gain_line = jnp.concatenate([attn_gain, mlp_gain]).reshape(1, -1)
    columns = QKV + half_width
    plane = lax.axis_index("wt")
    ids = jnp.stack([quarter, plane, pair, row, side])
    ff_weights = (w_gate, w_up, w_down)

    def attn_local(layer):
        return jnp.concatenate(
            [
                lax.dynamic_slice(weight[layer], (0, cols * pair), (depth, cols))
                for weight, cols in (
                    (w_key, KEY_HALF),
                    (w_value, KEY_HALF),
                    (w_query, QUERY_HALF),
                    (w_out, half_width),
                )
            ],
            axis=1,
        )

    def attn_gather(layer):
        local = attn_local(layer)
        piece = lax.dynamic_slice(local, (half_depth * row, 0), (half_depth, columns))
        if layer == 0:
            line = jnp.pad(gain_line, ((0, 15), (0, columns - gain_line.shape[1])))
            piece = jnp.concatenate([piece, line], axis=0)
        return local, lax.all_gather(piece, "wt", axis=0, tiled=False)

    def attn_weights(local, mine, other, after):
        both = join(ids, local, mine, other, after)
        keep = lax.dynamic_slice(both, (QUERY_HALF * pair, QKV), (QUERY_HALF, half_width))
        send = lax.dynamic_slice(both, (QUERY_HALF * (1 - pair), QKV), (QUERY_HALF, half_width))
        out_w = jnp.concatenate(ordered(pair, keep, flip(send, PAIR)), axis=1)
        return both[:, :QKV], out_w

    def mlp_gather(layer):
        piece = pack(layer, ids, ff_weights)
        return lax.all_gather(piece, "wt", axis=0, tiled=False)

    def mlp_spread(line, ahead, bit):
        first, last = line
        by_row, by_side = ahead or (flip(first, ROW), flip(first, SIDE))
        last_by_row, last_by_side = flip(last, ROW), flip(last, SIDE)
        across = (
            flip(by_row[0], SIDE),
            flip(by_row[1], SIDE) if bit == SIDE else flip(by_side[1], ROW),
            flip(last_by_row[0, :half_depth], SIDE),
            flip(last_by_side[0, half_depth:], ROW),
        )
        return by_row, last_by_row, by_side, last_by_side, *across

    where = jnp.stack([pair, quarter])

    residual = pair_rows(tokens[0]).astype(F32)
    parts = ()
    saved_layers = []
    attn_sets, ff_sets = [], []
    for layer in range(layer_count):
        attn_sets.append(attn_gather(layer))
        ff_sets.append(mlp_gather(layer))
    lines = attn_sets[0][1][:, half_depth, : gain_line.shape[1]].astype(F32)
    gains = (
        lines.reshape(wt_count, 2 * layer_count, depth)
        .transpose(1, 0, 2)
        .reshape(2 * layer_count, 1, wt_count * depth)
    )
    attn_other = flip(others(ids, attn_sets[0][1], half_depth, 0, 3), ROW)
    for layer in range(layer_count):
        last = layer + 1 == layer_count
        local, mine = attn_sets[layer]
        qkv_w, out_w = attn_weights(local, mine, attn_other, ())
        gain_attn, gain_mlp = gains[layer], gains[layer_count + layer]
        residual, normed_attn = add_norm(residual, parts, gain_attn)
        ahead = tuple(flip(early, bit) for bit in (ROW, SIDE)) if layer else ()
        query, key_value, key_value_turned = rope(
            dot_tt(qkv_w, normed_attn), cosine, sine, ahead
        )
        shared = key_value[TAIL:]
        for bit in key_bits:
            shared = jnp.concatenate([shared, flip(shared, bit)], axis=0)
        first = early if layer else others(ids, ff_sets[layer], depth, 0, 2, (shared,))
        line = (first, others(ids, ff_sets[layer], depth, 2, 3, (shared,)))
        spread = mlp_spread(line, ahead, ROW if layer else SIDE)
        attended, lse = attend(
            query, key_value, key_value_turned, shared, key_pos, row_pos, line
        )
        part = dot_tn(attended, out_w).astype(BF16)
        residual_mid, normed_mlp = add_norm(residual, (part, flip(part, PAIR)), gain_mlp)
        late = ()
        if layer + 1 < layer_count:
            next_attn = attn_sets[layer + 1][1]
            attn_other = flip(others(ids, next_attn, half_depth, 0, 3, (attended,)), ROW)
            late = (attn_other,)
        ff_w, down_w, slope, scale, unit, part = mlp(
            layer,
            ids,
            normed_mlp,
            (ff_sets[layer], *spread),
            ff_weights,
            ff_block,
            late,
        )
        parts = (part, flip(part, PAIR))
        if layer + 1 < layer_count:
            early = others(ids, ff_sets[layer + 1], depth, 0, 2, (part,))
        saved_layers.append(
            (
                qkv_w,
                out_w,
                ff_w,
                down_w,
                gain_attn,
                gain_mlp,
                residual,
                normed_attn,
                query,
                key_value,
                key_value_turned,
                shared,
                lse,
                attended,
                residual_mid,
                normed_mlp,
                slope,
                scale,
                unit,
            )
        )
        residual = residual_mid
    residual = residual + (parts[0].astype(F32) + parts[1].astype(F32))
    layer_out = own_rows(residual)

    def outer_sum(total):
        for bit in outer_bits:
            total = add(total, flip(total, bit), steps=1)
        return total

    def sum_ff(share, after=()):
        cut = 2 * ff_block
        totals = cross(share, flip(share[:, :cut], ROW), flip(share[:, cut:], SIDE), after)
        return [outer_sum(total) for total in totals]

    def spread_ff(totals):
        gate, up = totals
        gates, ups = [gate, flip(gate, SIDE)], [up, flip(up, ROW)]
        for group in (gates, ups):
            group += [flip(part, PAIR) for part in group]
        return gates + ups

    def sum_rows(share, cut, after=()):
        totals = split_sum(
            share, flip(share[:, :cut], SIDE), flip(share[:, cut:], ROW), after
        )
        return [outer_sum(total) for total in totals]

    def spread_rows(totals):
        by_row, by_side = totals
        joined = order(ids, (by_row, flip(by_row, ROW), by_side, flip(by_side, SIDE)))
        return [joined, flip(joined, PAIR)]

    down_cut, attn_cut = 640, 768

    def scatter(total):
        return lax.psum_scatter(total, "wt", scatter_dimension=0, tiled=total.ndim == 2)

    flow = pair_rows(cotangent[0])
    flow, flow_low = flow.astype(F32), flow
    gain_grads = [None] * (2 * layer_count)
    ff_outs, attn_outs = (
        [shaped((layer_count, *weight.shape[1:]), F32) for weight in group]
        for group in ((w_gate, w_up, w_down), (w_query, w_key, w_value, w_out))
    )
    ff_held = attn_held = None
    shares = {}
    for layer in reversed(range(layer_count)):
        (
            qkv_w,
            out_w,
            ff_w,
            down_w,
            gain_attn,
            gain_mlp,
            residual,
            normed_attn,
            query,
            key_value,
            key_value_turned,
            shared,
            lse,
            attended,
            residual_mid,
            normed_mlp,
            slope,
            scale,
            unit,
        ) = saved_layers[layer]
        older = shares.get(layer + 1)
        row_keep, row_send, side_keep, side_send = down_grad(ids, unit, flow_low, down_cut)
        down_parts = (row_keep, flip(row_send, ROW)), (side_keep, flip(side_send, SIDE))
        done = (row_keep,) if older is None else (row_keep, attn_all)
        gate_keep, gate_send, up_keep, up_send, part = mlp_back(
            flow_low, normed_mlp, slope, scale, down_w, ff_w, after=done
        )
        gate_got, up_got = flip(gate_send, SIDE), flip(up_send, ROW)
        done = () if older is None else (older["ff"],)
        part, down_sum = add_two(*down_parts, done, part)
        done = (down_sum,)
        flow, flow_low, gain_grads[layer_count + layer] = norm_back(
            flow, (part, flip(part, PAIR)), residual_mid, gain_mlp, after=done, pinned=True
        )
        attended_grad = dot_nt(out_w, flow_low).astype(BF16)
        query_grad, own_grad, shared_grad = attend_back(
            query,
            attended_grad,
            key_value,
            key_value_turned,
            shared,
            key_pos,
            row_pos,
            lse,
            cosine,
            sine,
        )
        for bit in reversed(key_bits):
            half = shared_grad.shape[0] // 2
            arrived = flip(shared_grad[half:].astype(BF16), bit)
            shared_grad = shared_grad[:half] + arrived.astype(F32)
            if bit == key_bits[-1]:
                started = shared_grad
        shares[layer] = {"down": scatter(down_sum)}
        done = (started, shares[layer]["down"])
        if older is not None:
            done = (*done, older["attn"])
        ff_sum = add_two((gate_keep, gate_got), (up_keep, up_got), done)
        shares[layer]["ff"] = scatter(ff_sum)
        down_totals = sum_rows(shares[layer]["down"], down_cut, (ff_sum,))
        done = (ff_sum, down_totals[0])
        if older is not None:
            ff_totals = sum_ff(older["ff"], (ff_sum,))
            attn_totals = sum_rows(older["attn"], attn_cut, (ff_sum,))
            done = (*done, ff_totals[0], attn_totals[0])
        grad_qkv = merge(query_grad, own_grad, shared_grad, cosine, sine, done)
        part = dot_nt(grad_qkv, qkv_w).astype(BF16)
        shares[layer]["down"] = spread_rows(down_totals)
        done = (shares[layer]["down"][0],)
        if older is not None:
            older["ff"] = spread_ff(ff_totals)
            older["attn"] = spread_rows(attn_totals)
            done = (*done, older["ff"][1], older["ff"][5], older["attn"][0])
        row_keep, row_send, side_keep, side_send = attn_grad(
            ids, normed_attn, grad_qkv, attended, flow_low, attn_cut, done
        )
        attn_mine, send = attn_sum(
            pair[None], (row_keep, flip(row_send, ROW), side_keep, flip(side_send, SIDE))
        )
        flow, flow_low, gain_grads[layer] = norm_back(
            flow, (part, flip(part, PAIR)), residual, gain_attn, after=(attn_mine,)
        )
        attn_all = attn_join(pair[None], attn_mine, flip(send, PAIR))
        shares[layer]["attn"] = scatter(attn_all)
    gain_total = jnp.concatenate(gain_grads, axis=0)
    for bit in [SIDE, ROW] + outer_bits:
        gain_total = gain_total + flip(gain_total, bit)
    bit = 1
    while bit < wt_count:
        gain_total = gain_total + flip(gain_total, bit, "wt", wt_count)
        bit *= 2
    for layer in reversed(range(layer_count)):
        share = shares[layer]
        if layer == 0:
            share["ff"] = spread_ff(sum_ff(share["ff"], (placed, attn_placed)))
        *ff_held, placed = place(
            place_ff_kernel, layer, where, share["ff"] + share["down"], ff_outs, ff_held, (flow_low,)
        )
        if layer == 0:
            totals = sum_rows(share["attn"], attn_cut, (placed, gain_total))
            share["attn"] = spread_rows(totals)
        *attn_held, attn_placed = place(
            place_attn_kernel, layer, where, share["attn"], attn_outs, attn_held, (flow_low,)
        )
    query_out, key_out, value_out, out_out = attn_held
    gate_out, up_out, down_out = ff_held
    token_grad = own_rows(flow)

    gain_share = lax.dynamic_slice(
        gain_total, (0, lax.axis_index("wt") * depth), (2 * layer_count, depth)
    )
    return (
        layer_out[None],
        token_grad[None],
        gain_share[:layer_count],
        query_out,
        key_out,
        value_out,
        out_out,
        gain_share[layer_count:],
        gate_out,
        up_out,
        down_out,
    )


def solution(mesh):
    weight = P(None, "wt", None)
    return jax.shard_map(
        per_device,
        mesh=mesh,
        in_specs=(
            P("wt", "ctx", None),
            P("wt", None),
            P("wt", "ctx", None),
            P(None, "wt"),
            weight,
            weight,
            weight,
            weight,
            P(None, "wt"),
            weight,
            weight,
            weight,
        ),
        out_specs=(
            P("wt", "ctx", None),
            P("wt", "ctx", None),
            P(None, "wt"),
            weight,
            weight,
            weight,
            weight,
            P(None, "wt"),
            weight,
            weight,
            weight,
        ),
        check_vma=False,
    )
```

```python
import functools
import math

import jax
import jax.numpy as jnp
from jax import lax
from jax.experimental import pallas as pl
from jax.experimental.pallas import tpu as pltpu
from jax.sharding import PartitionSpec as P

HEADS = 18
KV_HEADS = 6
HEAD_DIM = 64
HALF = 32
CONT = 256
SHARED = HEADS // KV_HEADS
PAIR_KV = KV_HEADS // 2
PAIR_HEADS = HEADS // 2
RUN = 2 * HALF + CONT
ROWS = 2 * RUN
PROMPT = 4 * HALF
TAIL = 2 * CONT

EPSILON = 1e-05
SCORE_SCALE = 0.125
BASE_TWO = SCORE_SCALE * math.log2(math.e)
MASKED = -1e30

BF16 = jnp.bfloat16
F32 = jnp.float32

PAIR, SIDE, ROW = 1, 2, 4


def dot_nn(left, right):
    return lax.dot_general(left, right, (((1,), (0,)), ((), ())), preferred_element_type=F32)


def dot_nt(left, right):
    return lax.dot_general(left, right, (((1,), (1,)), ((), ())), preferred_element_type=F32)


def dot_tn(left, right):
    return lax.dot_general(left, right, (((0,), (0,)), ((), ())), preferred_element_type=F32)


def dot_tt(left, right):
    return lax.dot_general(left, right, (((0,), (1,)), ((), ())), preferred_element_type=F32)


def turned(value):
    return jnp.transpose(value.astype(F32))


def shaped(shape, dtype):
    return jax.ShapeDtypeStruct(shape, dtype)


WHOLE = pl.BlockSpec(memory_space=pltpu.VMEM)
FAR = pl.BlockSpec(memory_space=pl.ANY)
SCALARS = pl.BlockSpec(memory_space=pltpu.SMEM)


def call(
    kernel, outs, ins, limit, out_specs=None, in_specs=None, after=(), far_in=0, far_out=0, **extra
):
    count, waited = len(ins), len(after)

    def body(*refs):
        kernel(*refs[:count], *refs[count + waited :])

    ins = [
        pltpu.with_memory_space_constraint(value, pltpu.HBM) if index < far_in else value
        for index, value in enumerate(ins)
    ]
    outs = [
        pltpu.HBM(out.shape, out.dtype) if index < far_out else out
        for index, out in enumerate(outs)
    ]
    return pl.pallas_call(
        body,
        out_shape=outs,
        in_specs=(in_specs or [WHOLE] * count) + [FAR] * waited,
        out_specs=out_specs or [WHOLE] * len(outs),
        compiler_params=pltpu.CompilerParams(vmem_limit_bytes=limit << 20),
        cost_estimate=pl.CostEstimate(flops=1, bytes_accessed=1, transcendentals=0),
        **extra,
    )(*ins, *after)


def add_norm_kernel(has_parts, *refs):
    if has_parts:
        held, mine, other, gain, total_ref, normed_ref = refs
        total = held[...] + (mine[...].astype(F32) + other[...].astype(F32))
        total_ref[...] = total
    else:
        held, gain, normed_ref = refs
        total = held[...]
    inverse = lax.rsqrt(jnp.mean(total * total, axis=-1, keepdims=True) + EPSILON)
    normed_ref[...] = (total * inverse * gain[...]).astype(BF16)


def add_norm(held, parts, gain, after=()):
    rows, width = held.shape
    step = 128
    block = pl.BlockSpec((step, width), lambda i: (i, 0))
    line = pl.BlockSpec((1, width), lambda i: (0, 0))
    ins = (held, *parts, gain)
    outs = ([shaped(held.shape, F32)] if parts else []) + [shaped(held.shape, BF16)]
    result = call(
        functools.partial(add_norm_kernel, bool(parts)),
        outs,
        ins,
        10,
        in_specs=[block] * (1 + len(parts)) + [line],
        out_specs=[block] * len(outs),
        grid=(rows // step,),
        after=after,
    )
    return result if parts else (held, result[0])


def norm_back_kernel(flow, mine, other, held, gain, flow_ref, low_ref, gain_ref):
    grad = mine[...].astype(F32) + other[...].astype(F32)
    value = held[...]
    inverse = lax.rsqrt(jnp.mean(value * value, axis=-1, keepdims=True) + EPSILON)
    plain = value * inverse
    scaled = grad * gain[...]
    tilt = jnp.mean(scaled * plain, axis=-1, keepdims=True)
    total = flow[...] + inverse * (scaled - plain * tilt)
    flow_ref[...] = total
    low_ref[...] = total.astype(BF16)

    @pl.when(pl.program_id(0) == 0)
    def _():
        gain_ref[...] = jnp.zeros_like(gain_ref)

    gain_ref[...] += jnp.sum(grad * plain, axis=0, keepdims=True)


def norm_back(flow, parts, held, gain, after=(), pinned=False):
    rows, width = held.shape
    step = 128
    block = pl.BlockSpec((step, width), lambda i: (i, 0))
    line = pl.BlockSpec((1, width), lambda i: (0, 0))
    return call(
        norm_back_kernel,
        [shaped(held.shape, F32), shaped(held.shape, BF16), shaped((1, width), F32)],
        (flow, *parts, held, gain),
        12,
        in_specs=[block] * 4 + [line],
        out_specs=[block, block, line],
        grid=(rows // step,),
        after=after,
        far_in=4 if pinned else 0,
    )


def add_kernel(mine, other, out):
    out[...] = (mine[...].astype(F32) + other[...].astype(F32)).astype(BF16)


def add_two_kernel(first_mine, first_other, second_mine, second_other, *refs):
    out = refs[-1]
    if len(refs) == 3:
        refs[1][...] = refs[0][...]
    first = first_mine[...].astype(F32) + first_other[...].astype(F32)
    second = second_mine[...].astype(F32) + second_other[...].astype(F32)
    axis = len(out.shape) - 1
    out[...] = jnp.concatenate([first.astype(BF16), second.astype(BF16)], axis=axis)


def add_two(first, second, after=(), passed=None):
    ins = (*first, *second)
    lead = first[0].shape[:-1]
    steps = 4

    def block(*shape):
        shape = (shape[0] // steps, *shape[1:])
        return pl.BlockSpec(shape, lambda i: (i,) + (0,) * (len(shape) - 1))

    columns = first[0].shape[-1] + second[0].shape[-1]
    extra = () if passed is None else (passed,)
    result = call(
        add_two_kernel,
        [shaped(part.shape, part.dtype) for part in extra] + [shaped((*lead, columns), BF16)],
        (*ins, *extra),
        12,
        in_specs=[block(*part.shape) for part in (*ins, *extra)],
        out_specs=[block(*part.shape) for part in extra] + [block(*lead, columns)],
        grid=(steps,),
        after=after,
        far_in=4,
    )
    return result if extra else result[0]


def split_sum_kernel(share, row_other, side_other, row_out, side_out):
    cut = row_out.shape[1]
    row_out[...] = (share[:, :cut].astype(F32) + row_other[...].astype(F32)).astype(BF16)
    side_out[...] = (share[:, cut:].astype(F32) + side_other[...].astype(F32)).astype(BF16)


def split_sum(share, row_other, side_other, after=()):
    return call(
        split_sum_kernel,
        [shaped(row_other.shape, BF16), shaped(side_other.shape, BF16)],
        (share, row_other, side_other),
        8,
        after=after,
    )


def order_kernel(ids_ref, row_mine, row_other, side_mine, side_other, out):
    side, row = ids_ref[4], ids_ref[3]
    half, cut = row_mine.shape
    for value, mine, other, cols in (
        (row, row_mine, row_other, slice(0, cut)),
        (side, side_mine, side_other, slice(cut, None)),
    ):
        for index in range(2):
            chosen = jnp.where(value == index, mine[...], other[...])
            out[index * half : (index + 1) * half, cols] = chosen


def order(ids, parts):
    half, cut = parts[0].shape
    return call(
        order_kernel,
        [shaped((2 * half, cut + parts[2].shape[1]), BF16)],
        (ids, *parts),
        8,
        in_specs=[SCALARS] + [WHOLE] * 4,
    )[0]


def cross_kernel(share, gate_other, up_other, gate_out, up_out):
    block = gate_out.shape[1] // 2
    for out, other, low in ((gate_out, gate_other, 0), (up_out, up_other, 2 * block)):
        for index in range(2):
            mine = share[:, low + index * block : low + (index + 1) * block]
            theirs = other[:, (1 - index) * block : (2 - index) * block]
            out[:, index * block : (index + 1) * block] = (
                mine.astype(F32) + theirs.astype(F32)
            ).astype(BF16)


def cross(share, gate_other, up_other, after=()):
    shape = (share.shape[0], share.shape[1] // 2)
    return call(
        cross_kernel,
        [shaped(shape, BF16)] * 2,
        (share, gate_other, up_other),
        8,
        after=after,
    )


def add(mine, other, after=(), steps=4):
    shape = mine.shape
    block = pl.BlockSpec(
        (shape[0] // steps, *shape[1:]), lambda i: (i,) + (0,) * (len(shape) - 1)
    )
    return call(
        add_kernel,
        [shaped(shape, BF16)],
        (mine, other),
        12,
        in_specs=[block, block],
        out_specs=[block],
        grid=(steps,),
        after=after,
    )[0]


KEY_HALF = PAIR_KV * HEAD_DIM
QUERY_HALF = PAIR_HEADS * HEAD_DIM
QKV = 2 * KEY_HALF + QUERY_HALF


def rope_kernel(qkv_ref, cos_ref, sin_ref, query_ref, kv_ref, kv_turned_ref):
    cosine, sine = cos_ref[...], sin_ref[...]
    half = HEAD_DIM // 2

    def head(source, target_ref, target):
        low = qkv_ref[source : source + half, :]
        high = qkv_ref[source + half : source + 2 * half, :]
        target_ref[target : target + half, :] = (low * cosine - high * sine).astype(BF16)
        target_ref[target + half : target + 2 * half, :] = (high * cosine + low * sine).astype(
            BF16
        )

    for index in range(PAIR_KV):
        head(index * HEAD_DIM, kv_turned_ref, index * HEAD_DIM)
    kv_turned_ref[KEY_HALF:, :] = qkv_ref[KEY_HALF : 2 * KEY_HALF, :].astype(BF16)
    kv_ref[...] = turned(kv_turned_ref[...]).astype(BF16)
    for index in range(PAIR_HEADS):
        head(2 * KEY_HALF + index * HEAD_DIM, query_ref, index * HEAD_DIM)


def rope(qkv, cosine, sine, after=()):
    return call(
        rope_kernel,
        [
            shaped((QUERY_HALF, ROWS), BF16),
            shaped((ROWS, 2 * KEY_HALF), BF16),
            shaped((2 * KEY_HALF, ROWS), BF16),
        ],
        (qkv, cosine, sine),
        14,
        after=after,
    )


def later_mask():
    key = lax.broadcasted_iota(jnp.int32, (CONT, CONT), 0)
    query = lax.broadcasted_iota(jnp.int32, (CONT, CONT), 1)
    return key <= query


def attend_kernel(
    query_ref, kv_ref, kv_turned_ref, shared_ref, key_pos_ref, row_pos_ref, out_ref, lse_ref
):
    shared_values = turned(shared_ref[:, KEY_HALF:]).astype(BF16)
    for kv_head in range(PAIR_KV):
        low = kv_head * HEAD_DIM
        keys = shared_ref[:, low : low + HEAD_DIM]
        values = shared_values[low : low + HEAD_DIM, :]

        def head(index, carry, kv_head=kv_head, low=low, keys=keys, values=values):
            number = kv_head * SHARED + index
            base = pl.multiple_of(number * HEAD_DIM, HEAD_DIM)
            allowed = key_pos_ref[...] <= row_pos_ref[...]
            query = query_ref[pl.ds(base, HEAD_DIM), TAIL:]
            scores = jnp.where(allowed, dot_nn(keys, query) * BASE_TWO, MASKED)
            top = jnp.max(scores, axis=0, keepdims=True)
            weight = jnp.exp2(scores - top)
            total = jnp.sum(weight, axis=0, keepdims=True)
            out = dot_nn(values, weight.astype(BF16)) / total
            out_ref[pl.ds(base, HEAD_DIM), TAIL:] = out.astype(BF16)
            lse_ref[number, :, TAIL:] = top + jnp.log2(total)
            for run in range(2):
                cols = slice(run * CONT, (run + 1) * CONT)
                query = query_ref[pl.ds(base, HEAD_DIM), cols]
                own_keys = kv_ref[cols, low : low + HEAD_DIM]
                own_values = kv_turned_ref[KEY_HALF + low : KEY_HALF + low + HEAD_DIM, cols]
                first = dot_nn(keys, query) * BASE_TWO
                second = jnp.where(later_mask(), dot_nn(own_keys, query) * BASE_TWO, MASKED)
                top = jnp.maximum(
                    jnp.max(first, axis=0, keepdims=True), jnp.max(second, axis=0, keepdims=True)
                )
                first = jnp.exp2(first - top)
                second = jnp.exp2(second - top)
                total = jnp.sum(first, axis=0, keepdims=True) + jnp.sum(
                    second, axis=0, keepdims=True
                )
                out = dot_nn(values, first.astype(BF16)) + dot_nn(
                    own_values, second.astype(BF16)
                )
                out_ref[pl.ds(base, HEAD_DIM), cols] = (out / total).astype(BF16)
                lse_ref[number, :, cols] = top + jnp.log2(total)
            return carry

        lax.fori_loop(0, SHARED, head, 0, unroll=True)


def attend(query, key_value, key_value_turned, shared, key_pos, row_pos, after=()):
    return call(
        attend_kernel,
        [shaped((QUERY_HALF, ROWS), BF16), shaped((PAIR_HEADS, 1, ROWS), F32)],
        (query, key_value, key_value_turned, shared, key_pos, row_pos),
        16 + shared.shape[0] // 64,
        after=after,
    )


def attend_back_kernel(
    query_ref,
    grad_ref,
    kv_ref,
    kv_turned_ref,
    shared_ref,
    key_pos_ref,
    row_pos_ref,
    lse_ref,
    cos_ref,
    sin_ref,
    query_grad_ref,
    own_grad_ref,
    shared_grad_ref,
    score_keep,
    weight_keep,
    own_score_keep,
    own_weight_keep,
):
    shared_turned = turned(shared_ref[:, :KEY_HALF]).astype(BF16)
    half = HEAD_DIM // 2
    for kv_head in range(PAIR_KV):
        low = kv_head * HEAD_DIM
        keys = shared_ref[:, low : low + HEAD_DIM]
        values = shared_ref[:, KEY_HALF + low : KEY_HALF + low + HEAD_DIM]
        keys_turned = shared_turned[low : low + HEAD_DIM, :]

        def head(index, carry, kv_head=kv_head, low=low, keys=keys, values=values, keys_turned=keys_turned):
            number = kv_head * SHARED + index
            base = pl.multiple_of(number * HEAD_DIM, HEAD_DIM)

            def put_query_grad(grad, cols):
                cosine, sine = cos_ref[:, cols], sin_ref[:, cols]
                first, second = grad[:half], grad[half:]
                query_grad_ref[pl.ds(base, half), cols] = (
                    (first * cosine + second * sine) * SCORE_SCALE
                ).astype(BF16)
                query_grad_ref[pl.ds(base + half, half), cols] = (
                    (second * cosine - first * sine) * SCORE_SCALE
                ).astype(BF16)

            cols = slice(TAIL, ROWS)
            query = query_ref[pl.ds(base, HEAD_DIM), cols]
            grad = grad_ref[pl.ds(base, HEAD_DIM), cols]
            lse = lse_ref[number, :, cols]
            allowed = key_pos_ref[...] <= row_pos_ref[...]
            scores = jnp.where(allowed, dot_nn(keys, query) * BASE_TWO, MASKED)
            weight = jnp.exp2(scores - lse)
            weight_keep[index, :, cols] = weight.astype(BF16)
            flow = weight * dot_nn(values, grad)
            delta = jnp.sum(flow, axis=0, keepdims=True)
            flow = (flow - weight * delta).astype(BF16)
            score_keep[index, :, cols] = flow
            put_query_grad(dot_nn(keys_turned, flow), cols)
            for run in range(2):
                cols = slice(run * CONT, (run + 1) * CONT)
                query = query_ref[pl.ds(base, HEAD_DIM), cols]
                grad = grad_ref[pl.ds(base, HEAD_DIM), cols]
                lse = lse_ref[number, :, cols]
                own_keys = kv_ref[cols, low : low + HEAD_DIM]
                own_values = kv_ref[cols, KEY_HALF + low : KEY_HALF + low + HEAD_DIM]
                own_turned = kv_turned_ref[low : low + HEAD_DIM, cols]
                first = jnp.exp2(dot_nn(keys, query) * BASE_TWO - lse)
                second = jnp.where(later_mask(), dot_nn(own_keys, query) * BASE_TWO, MASKED)
                second = jnp.exp2(second - lse)
                weight_keep[index, :, cols] = first.astype(BF16)
                own_weight_keep[index, :, cols] = second.astype(BF16)
                first_flow = first * dot_nn(values, grad)
                second_flow = second * dot_nn(own_values, grad)
                delta = jnp.sum(first_flow, axis=0, keepdims=True) + jnp.sum(
                    second_flow, axis=0, keepdims=True
                )
                first_flow = (first_flow - first * delta).astype(BF16)
                second_flow = (second_flow - second * delta).astype(BF16)
                score_keep[index, :, cols] = first_flow
                own_score_keep[index, :, cols] = second_flow
                put_query_grad(
                    dot_nn(keys_turned, first_flow) + dot_nn(own_turned, second_flow), cols
                )
            return carry

        lax.fori_loop(0, SHARED, head, 0, unroll=True)
        key_sum, value_sum = 0.0, 0.0
        own_key_sum, own_value_sum = [0.0, 0.0], [0.0, 0.0]
        for index in range(SHARED):
            base = (kv_head * SHARED + index) * HEAD_DIM
            query = query_ref[base : base + HEAD_DIM, :]
            grad = grad_ref[base : base + HEAD_DIM, :]
            key_sum = key_sum + dot_nt(score_keep[index], query)
            value_sum = value_sum + dot_nt(weight_keep[index], grad)
            for run in range(2):
                cols = slice(run * CONT, (run + 1) * CONT)
                own_key_sum[run] = own_key_sum[run] + dot_nt(
                    own_score_keep[index, :, cols], query[:, cols]
                )
                own_value_sum[run] = own_value_sum[run] + dot_nt(
                    own_weight_keep[index, :, cols], grad[:, cols]
                )
        shared_grad_ref[:, low : low + HEAD_DIM] = key_sum * SCORE_SCALE
        shared_grad_ref[:, KEY_HALF + low : KEY_HALF + low + HEAD_DIM] = value_sum
        for run in range(2):
            cols = slice(run * CONT, (run + 1) * CONT)
            own_grad_ref[cols, low : low + HEAD_DIM] = own_key_sum[run] * SCORE_SCALE
            own_grad_ref[cols, KEY_HALF + low : KEY_HALF + low + HEAD_DIM] = own_value_sum[run]


def attend_back(
    query, grad, key_value, key_value_turned, shared, key_pos, row_pos, lse, cosine, sine, after=()
):
    count = shared.shape[0]
    return call(
        attend_back_kernel,
        [
            shaped((QUERY_HALF, ROWS), BF16),
            shaped((TAIL, 2 * KEY_HALF), F32),
            shaped((count, 2 * KEY_HALF), F32),
        ],
        (query, grad, key_value, key_value_turned, shared, key_pos, row_pos, lse, cosine, sine),
        22 + count // 64,
        scratch_shapes=[
            pltpu.VMEM((SHARED, count, ROWS), BF16),
            pltpu.VMEM((SHARED, count, ROWS), BF16),
            pltpu.VMEM((SHARED, CONT, TAIL), BF16),
            pltpu.VMEM((SHARED, CONT, TAIL), BF16),
        ],
        after=after,
    )


def merge_kernel(query_grad_ref, own_ref, prompt_ref, cos_ref, sin_ref, out_ref):
    cosine, sine = cos_ref[...], sin_ref[...]
    half = HEAD_DIM // 2
    both = turned(jnp.concatenate([own_ref[...], prompt_ref[...]], axis=0))
    pieces = []
    for index in range(PAIR_KV):
        low = both[index * HEAD_DIM : index * HEAD_DIM + half]
        high = both[index * HEAD_DIM + half : (index + 1) * HEAD_DIM]
        pieces += [low * cosine + high * sine, high * cosine - low * sine]
    both = jnp.concatenate(pieces + [both[KEY_HALF:]], axis=0)
    out_ref[:, : 2 * KEY_HALF] = jnp.transpose(both).astype(BF16)
    out_ref[:, 2 * KEY_HALF :] = turned(query_grad_ref[...]).astype(BF16)


def merge(query_grad, own_grad, prompt_grad, cosine, sine, after=()):
    return call(
        merge_kernel,
        [shaped((ROWS, QKV), BF16)],
        (query_grad, own_grad, prompt_grad, cosine, sine),
        16,
        after=after,
    )[0]


def mlp_kernel(layer, ids_ref, normed_ref, *refs):
    own = refs[0]
    from_row, from_side, from_across = refs[1:3], refs[3:5], refs[5:9]
    gate_ref, up_ref, down_shard = (ref.at[layer] for ref in refs[9:12])
    weight_ref, down_ref, slope_ref, scale_ref, unit_ref, out_ref = refs[12:18]
    held, sems, down_sem, keep_sem = refs[18:]
    rows, depth = normed_ref.shape
    block = held.shape[2] // 2
    shard = depth // 4
    lines = block // 4
    wide = depth // 3
    quarter, plane, pair = ids_ref[0], ids_ref[1], ids_ref[2]
    slots = line_slots(plane)

    def copy(source, target, sem):
        pltpu.make_async_copy(source, target, sem).start()

    def at(start, size):
        return pl.ds(pl.multiple_of(start, 16), size)

    def pieces(part):
        if part == 0:
            return [(own.at[owner], 0, shard, owner) for owner in (plane, *slots)]
        if part < 3:
            pair_of_slots, last = (from_row, from_side)[part - 1]
            arrived = (pair_of_slots.at[0], pair_of_slots.at[1], last.at[0])
            return [(arrived[slot], 0, shard, slots[slot]) for slot in range(3)]
        half = shard // 2
        return [
            (from_across[0], 0, shard, slots[0]),
            (from_across[1], 0, shard, slots[1]),
            (from_across[2], 0, half, slots[2]),
            (from_across[3], half, shard, slots[2]),
        ]

    for part in range(4):
        for source, low, high, owner in pieces(part):
            copy(
                source.at[:, : 2 * block],
                held.at[part, at(shard * owner + low, high - low)],
                sems.at[part],
            )
        if part == 0:
            continue
        col = pl.ds(pl.multiple_of((2 * (quarter ^ part) + pair) * block, block), block)
        for index, ref in enumerate((gate_ref, up_ref)):
            copy(
                ref.at[:, col],
                held.at[part, at(shard * plane, shard), pl.ds(index * block, block)],
                sems.at[part],
            )
    taken = pl.ds(2 * block, wide)

    def down_copies(source, low, high, place, piece):
        for column in range(3):
            first, last = max(low, lines * column), min(high, lines * (column + 1))
            if first < last:
                copy(
                    source.at[at(first - low, last - first), taken],
                    down_ref.at[
                        at(
                            block * place + lines * (quarter ^ piece) + first - lines * column,
                            last - first,
                        ),
                        pl.ds(wide * column, wide),
                    ],
                    down_sem,
                )

    for part in range(4):
        for source, low, high, owner in pieces(part):
            down_copies(source, low, high, quarter ^ owner, part)
        if part == 0:
            continue
        copy(
            down_shard.at[at(block * pair + lines * (quarter ^ part), lines)],
            down_ref.at[at(block * (quarter ^ plane) + lines * (quarter ^ part), lines)],
            down_sem,
        )

    step = rows // 2
    kept = []
    for part in range(4):
        pltpu.make_async_copy(held.at[part], held.at[part], sems.at[part]).wait()
        kept.append(pltpu.make_async_copy(held.at[part], weight_ref.at[part], keep_sem.at[part]))
        kept[-1].start()

        def tile(index, carry, part=part):
            some = pl.ds(pl.multiple_of(index * step, step), step)
            normed = normed_ref[some, :]
            gate = dot_nn(normed, held[part, :, :block])
            up = dot_nn(normed, held[part, :, block:])
            sigmoid = 1.0 / (1.0 + jnp.exp(-gate))
            scale = gate * sigmoid
            cols = slice(part * block, (part + 1) * block)
            slope_ref[some, cols] = (up * sigmoid * (1.0 + gate * (1.0 - sigmoid))).astype(BF16)
            scale_ref[some, cols] = scale.astype(BF16)
            unit_ref[some, cols] = (scale * up).astype(BF16)
            return carry

        lax.fori_loop(0, 2, tile, 0, unroll=True)
    pltpu.make_async_copy(down_ref, down_ref, down_sem).wait()

    def finish(index, carry):
        some = pl.ds(pl.multiple_of(index * step, step), step)
        out_ref[some, :] = dot_nn(unit_ref[some, :], down_ref[...]).astype(BF16)
        return carry

    lax.fori_loop(0, 2, finish, 0, unroll=True)
    for part in kept:
        part.wait()


def mlp(layer, ids, normed, pieces, weights, block, after=(), far_out=0):
    rows, depth = normed.shape
    units = 4 * block
    ins = (ids, normed, *pieces, *weights)
    return call(
        functools.partial(mlp_kernel, layer),
        [
            shaped((4, depth, 2 * block), BF16),
            shaped((units, depth), BF16),
            shaped((rows, units), BF16),
            shaped((rows, units), BF16),
            shaped((rows, units), BF16),
            shaped((rows, depth), BF16),
        ],
        ins,
        32,
        in_specs=[SCALARS, WHOLE] + [FAR] * (len(ins) - 2),
        out_specs=[FAR] + [WHOLE] * 5,
        scratch_shapes=[
            pltpu.VMEM((4, depth, 2 * block), BF16),
            pltpu.SemaphoreType.DMA((4,)),
            pltpu.SemaphoreType.DMA,
            pltpu.SemaphoreType.DMA((4,)),
        ],
        after=after,
        far_out=far_out,
    )


def pack_kernel(layer, ids_ref, gate_ref, up_ref, down_ref, out, sem):
    quarter, pair = ids_ref[0], ids_ref[2]
    depth, columns = out.shape
    wide = columns // 3
    lines = depth // 3
    col = pl.ds(pl.multiple_of((2 * quarter + pair) * wide, wide), wide)
    for index, ref in enumerate((gate_ref, up_ref)):
        target = out.at[:, pl.ds(index * wide, wide)]
        pltpu.make_async_copy(ref.at[layer, :, col], target, sem).start()
    start = pl.multiple_of((4 * pair + quarter) * lines, lines)
    for index in range(3):
        pltpu.make_async_copy(
            down_ref.at[layer, pl.ds(start, lines), pl.ds(index * wide, wide)],
            out.at[pl.ds(index * lines, lines), pl.ds(2 * wide, wide)],
            sem,
        ).start()
    pltpu.make_async_copy(out, out, sem).wait()


def pack(layer, ids, weights, after=()):
    _, depth, units = weights[0].shape
    return call(
        functools.partial(pack_kernel, layer),
        [shaped((depth, 3 * units // 8), BF16)],
        (ids, *weights),
        16,
        in_specs=[SCALARS] + [FAR] * 3,
        scratch_shapes=[pltpu.SemaphoreType.DMA],
        after=after,
    )[0]


def deal(total, row, side, cut, place, row_keep, row_send, side_keep, side_send):
    half = total.shape[0] // 2
    for index in range(2):
        part = total[index * half : (index + 1) * half]
        for value, keep, send, cols in (
            (row, row_keep, row_send, slice(0, cut)),
            (side, side_keep, side_send, slice(cut, None)),
        ):

            @pl.when(value == index)
            def _(part=part, keep=keep, cols=cols):
                keep[place] = part[:, cols]

            @pl.when(value != index)
            def _(part=part, send=send, cols=cols):
                send[place] = part[:, cols]


def dealt(blocks, half, columns, cut):
    return [
        shaped((blocks, half, size), BF16) for size in (cut, cut, columns - cut, columns - cut)
    ]


def down_grad_kernel(cut, ids_ref, unit_ref, flow_ref, *outs):
    quarter, side, row = ids_ref[0], ids_ref[4], ids_ref[3]
    block = unit_ref.shape[1] // 4
    for place in range(4):
        total = dot_tn(unit_ref[:, place * block : (place + 1) * block], flow_ref[...])
        deal(total.astype(BF16), row, side, cut, quarter ^ place, *outs)


def down_grad(ids, unit, flow, cut, after=()):
    rows, units = unit.shape
    width = flow.shape[1]
    return call(
        functools.partial(down_grad_kernel, cut),
        dealt(4, units // 8, width, cut),
        (ids, unit, flow),
        16,
        in_specs=[SCALARS, WHOLE, WHOLE],
        after=after,
    )


def mlp_back_kernel(
    flow_ref,
    normed_ref,
    slope_ref,
    scale_ref,
    down_ref,
    weight_ref,
    gate_keep,
    gate_send,
    up_keep,
    up_send,
    out_ref,
    held,
    total,
    unit_grad,
    sems,
):
    rows, depth = normed_ref.shape
    block = held.shape[2] // 2
    order = (3, 2, 1, 0)
    copies = {
        part: pltpu.make_async_copy(weight_ref.at[part], held.at[part], sems.at[part])
        for part in order
    }
    for part in order:
        copies[part].start()
    step = rows // 2
    for part in order:
        cols = slice(part * block, (part + 1) * block)

        def tile(index, carry, cols=cols):
            at = pl.ds(pl.multiple_of(index * step, step), step)
            grad = dot_nt(flow_ref[at, :], down_ref[cols, :])
            unit_grad[at, :block] = (grad * slope_ref[at, cols].astype(F32)).astype(BF16)
            unit_grad[at, block:] = (grad * scale_ref[at, cols].astype(F32)).astype(BF16)
            return carry

        lax.fori_loop(0, 2, tile, 0, unroll=True)
        both = dot_tn(normed_ref[...], unit_grad[...]).astype(BF16)
        target = gate_send if part >= 2 else gate_keep
        target[:, (part % 2) * block : (part % 2 + 1) * block] = both[:, :block]
        target = up_send if part % 2 else up_keep
        target[:, (part // 2) * block : (part // 2 + 1) * block] = both[:, block:]
        copies[part].wait()

        def gather(index, carry, part=part):
            at = pl.ds(pl.multiple_of(index * step, step), step)
            value = dot_nt(unit_grad[at, :], held[part])
            if part == order[0]:
                total[at, :] = value
            elif part == order[-1]:
                out_ref[at, :] = (total[at, :] + value).astype(BF16)
            else:
                total[at, :] += value
            return carry

        lax.fori_loop(0, 2, gather, 0, unroll=True)


def mlp_back(flow, normed, slope, scale, down, weights, after=()):
    rows, depth = normed.shape
    block = down.shape[0] // 4
    return call(
        mlp_back_kernel,
        [shaped((depth, 2 * block), BF16)] * 4 + [shaped((rows, depth), BF16)],
        (flow, normed, slope, scale, down, weights),
        40,
        in_specs=[WHOLE] * 5 + [FAR],
        scratch_shapes=[
            pltpu.VMEM((4, depth, 2 * block), BF16),
            pltpu.VMEM((rows, depth), F32),
            pltpu.VMEM((rows, 2 * block), BF16),
            pltpu.SemaphoreType.DMA((4,)),
        ],
        after=after,
        far_out=4,
    )


def join_kernel(ids_ref, local, mine, other, out, sem):
    plane, row = ids_ref[1], ids_ref[3]
    half = local.shape[0] // 2

    def copy(source, start):
        target = out.at[pl.ds(pl.multiple_of(start, 16), source.shape[0])]
        pltpu.make_async_copy(source, target, sem).start()

    copy(local, 2 * half * plane)
    for slot, owner in enumerate(line_slots(plane)):
        copy(mine.at[owner, pl.ds(0, half)], half * (2 * owner + row))
        copy(other.at[slot], half * (2 * owner + 1 - row))
    pltpu.make_async_copy(out, out, sem).wait()


def join(ids, local, mine, other, after=()):
    shape = (4 * local.shape[0], local.shape[1])
    return call(
        join_kernel,
        [shaped(shape, BF16)],
        (ids, local, mine, other),
        16,
        in_specs=[SCALARS] + [FAR] * 3,
        scratch_shapes=[pltpu.SemaphoreType.DMA],
        after=after,
    )[0]


def others_kernel(first, ids_ref, gathered, out, sem):
    count, rows, _ = out.shape
    for slot, owner in enumerate(line_slots(ids_ref[1])[first : first + count]):
        pltpu.make_async_copy(gathered.at[owner, pl.ds(0, rows)], out.at[slot], sem).start()
    pltpu.make_async_copy(out, out, sem).wait()


def others(ids, gathered, rows, first, last, after=()):
    return call(
        functools.partial(others_kernel, first),
        [shaped((last - first, rows, gathered.shape[2]), BF16)],
        (ids, gathered),
        16,
        in_specs=[SCALARS, FAR],
        scratch_shapes=[pltpu.SemaphoreType.DMA],
        after=after,
    )[0]


def line_slots(plane):
    return [plane ^ step for step in (1, 2, 3)]


def attn_grad_kernel(cut, ids_ref, normed, grad, attended, flow, *outs):
    side, row = ids_ref[4], ids_ref[3]
    blocks, half, _ = outs[0].shape
    out_cols = flow.shape[1] // 2
    out = dot_nn(attended[...], flow[...]).astype(BF16)
    for block in range(blocks):
        low, col = 2 * (block // 2) * half, (block % 2) * out_cols
        total = jnp.concatenate(
            [
                dot_tn(normed[:, 2 * block * half : 2 * (block + 1) * half], grad[...]).astype(
                    BF16
                ),
                out[low : low + 2 * half, col : col + out_cols],
            ],
            axis=1,
        )
        deal(total, row, side, cut, block, *outs)


def attn_grad(ids, normed, grad, attended, flow, cut, after=()):
    columns = grad.shape[1] + flow.shape[1] // 2
    return call(
        functools.partial(attn_grad_kernel, cut),
        dealt(4, normed.shape[1] // 8, columns, cut),
        (ids, normed, grad, attended, flow),
        20,
        in_specs=[SCALARS] + [WHOLE] * 4,
        after=after,
    )


def attn_sum_kernel(pair_ref, row_mine, row_other, side_mine, side_other, keep_ref, send_ref):
    pair = pair_ref[0]
    total = jnp.concatenate(
        [
            (mine[...].astype(F32) + other[...].astype(F32)).astype(BF16)
            for mine, other in ((row_mine, row_other), (side_mine, side_other))
        ],
        axis=2,
    )
    keep_ref[:, :, :QKV] = total[:, :, :QKV]
    for plane in range(4):
        for owner in range(2):

            @pl.when(pair == owner)
            def _(plane=plane, owner=owner):
                if plane // 2 == owner:
                    keep_ref[plane, :, QKV:] = total[2 * (plane % 2) + owner, :, QKV:]
                else:
                    send_ref[plane % 2] = total[2 * (plane % 2) + 1 - owner, :, QKV:]
                    keep_ref[plane, :, QKV:] = jnp.zeros_like(keep_ref[plane, :, QKV:])


def attn_sum(pair, parts, after=()):
    blocks, half, first = parts[0].shape
    columns = first + parts[2].shape[2]
    return call(
        attn_sum_kernel,
        [
            shaped((blocks, half, columns), BF16),
            shaped((blocks // 2, half, columns - QKV), BF16),
        ],
        (pair, *parts),
        16,
        in_specs=[SCALARS] + [WHOLE] * 4,
        after=after,
    )


def attn_join_kernel(pair_ref, mine, other, out):
    pair = pair_ref[0]
    out[:, :, :QKV] = mine[:, :, :QKV]
    for plane in range(4):
        for owner in range(2):

            @pl.when(pair == owner)
            def _(plane=plane, owner=owner):
                if plane // 2 == owner:
                    out[plane, :, QKV:] = mine[plane, :, QKV:]
                else:
                    out[plane, :, QKV:] = other[plane % 2]


def attn_join(pair, mine, other, after=()):
    return call(
        attn_join_kernel,
        [shaped(mine.shape, BF16)],
        (pair, mine, other),
        12,
        in_specs=[SCALARS, WHOLE, WHOLE],
        after=after,
    )[0]


def place_ff_kernel(where_ref, *refs):
    gates, ups, downs = refs[0:4], refs[4:8], refs[8:10]
    gate_out, up_out, down_out = refs[10:]
    pair, quarter = where_ref[0], where_ref[1]
    block = gates[0].shape[1] // 2
    for out, pieces, spread, inner in ((gate_out, gates, 2, 1), (up_out, ups, 1, 2)):
        for number, ref in enumerate(pieces):
            owner = pair ^ (number // 2)
            for index in range(2):
                plane = quarter ^ ((number % 2) * spread + index * inner)
                col = pl.multiple_of((2 * plane + owner) * block, block)
                out[0, :, pl.ds(col, block)] = ref[
                    :, index * block : (index + 1) * block
                ].astype(F32)
    down_rows = downs[0].shape[0]
    for where_from, owner in ((downs[0], pair), (downs[1], 1 - pair)):
        down_out[0, pl.ds(pl.multiple_of(owner * down_rows, down_rows), down_rows), :] = (
            where_from[...].astype(F32)
        )


def place_attn_kernel(where_ref, attn_mine, attn_other, *refs):
    query_out, key_out, value_out, out_out = refs
    pair = where_ref[0]
    first = jnp.where(pair == 0, attn_mine[...], attn_other[...]).astype(F32)
    second = jnp.where(pair == 0, attn_other[...], attn_mine[...]).astype(F32)
    low = 0
    for out, cols in (
        (key_out, KEY_HALF),
        (value_out, KEY_HALF),
        (query_out, QUERY_HALF),
        (out_out, first.shape[1] - QKV),
    ):
        out[0] = jnp.concatenate([first[:, low : low + cols], second[:, low : low + cols]], axis=1)
        low += cols


def place_kernel(kernel, fresh, parts, outs, *refs):
    here = refs[: 1 + parts]
    there = refs[1 + parts :] if fresh else refs[1 + parts + outs :]
    kernel(*here, *there[:outs])
    there[outs][...] = jnp.zeros_like(there[outs])


def place(kernel, layer, where, parts, outs, held, after=()):
    ins = (where, *parts, *(held or ()))
    specs = [SCALARS] + [WHOLE] * len(parts) + [FAR] * len(held or ())

    def layer_block(out):
        return pl.BlockSpec((1, *out.shape[1:]), lambda _: (layer, 0, 0))

    aliases = {} if held is None else {1 + len(parts) + i: i for i in range(len(outs))}
    return call(
        functools.partial(place_kernel, kernel, held is None, len(parts), len(outs)),
        [*outs, shaped((8, 128), F32)],
        ins,
        48,
        in_specs=specs,
        out_specs=[layer_block(out) for out in outs]
        + [pl.BlockSpec((8, 128), lambda _: (0, 0))],
        input_output_aliases=aliases,
        grid=(1,),
        after=after,
    )


def positions(deal_row, ctx_count):
    row_ids = jnp.arange(RUN, dtype=jnp.int32)
    block_ids = deal_row[..., None]
    lower_block = block_ids * HALF + row_ids
    upper_block = (2 * ctx_count - 1 - block_ids) * HALF + row_ids - HALF
    continued = 2 * HALF * ctx_count + row_ids - 2 * HALF
    return jnp.where(
        row_ids < HALF, lower_block, jnp.where(row_ids < 2 * HALF, upper_block, continued)
    )


def per_device(
    tokens,
    assign,
    cotangent,
    attn_gain,
    w_query,
    w_key,
    w_value,
    w_out,
    mlp_gain,
    w_gate,
    w_up,
    w_down,
):
    ctx_count = lax.axis_size("ctx")
    wt_count = lax.axis_size("wt")
    ctx_index = lax.axis_index("ctx")
    pair = ctx_index % 2
    side = (ctx_index // SIDE) % 2
    row = (ctx_index // ROW) % 2
    quarter = 2 * side + row
    chip = ctx_index // 2
    chip_count = ctx_count // 2
    outer_bits = [bit for bit in (8, 16, 32, 64, 128) if bit < ctx_count]

    layer_count, depth = attn_gain.shape[0], w_query.shape[1]
    width = w_out.shape[2]
    half_width = width // 2
    ff_block = w_down.shape[1] // 2
    ff_piece = ff_block // 4
    half_depth = depth // 2

    def flip(value, bit, axis="ctx", count=None):
        count = ctx_count if count is None else count
        return lax.ppermute(value, axis, [(i, i ^ bit) for i in range(count)])

    def ordered(bit_value, mine, other):
        first = jnp.where(bit_value == 0, mine, other)
        second = jnp.where(bit_value == 0, other, mine)
        return first, second

    def pair_rows(own):
        first, second = ordered(pair, own, flip(own, PAIR))
        cut = 2 * HALF
        return jnp.concatenate([first[cut:], second[cut:], first[:cut], second[:cut]], axis=0)

    def own_rows(both):
        return jnp.concatenate(
            [
                lax.dynamic_slice(both, (TAIL + 2 * HALF * pair, 0), (2 * HALF, width)),
                lax.dynamic_slice(both, (CONT * pair, 0), (CONT, width)),
            ],
            axis=0,
        )

    every_pos = positions(assign[0], ctx_count).reshape(chip_count, 2, RUN)
    key_bits = [ROW, SIDE] + outer_bits
    steps = [0]
    for bit in key_bits:
        steps += [step ^ (bit // 2) for step in steps]
    wanted = chip ^ jnp.array(steps, dtype=jnp.int32)
    picked = wanted[:, None] == jnp.arange(chip_count, dtype=jnp.int32)[None, :]
    prompt_pos = jnp.sum(
        jnp.where(picked[:, :, None, None], every_pos[None, :, :, : 2 * HALF], 0), axis=1
    )
    key_pos = prompt_pos.reshape(-1, 1)
    row_pos = prompt_pos[0].reshape(1, -1)
    cont_pos = every_pos[0, 0, 2 * HALF :]
    own_pos = jnp.concatenate([cont_pos, cont_pos, row_pos[0]])
    half_dim = HEAD_DIM // 2
    frequency = jnp.exp(jnp.arange(half_dim, dtype=F32) * (-jnp.log(10000.0) / half_dim))
    phase = frequency[:, None] * own_pos.astype(F32)[None, :]
    cosine, sine = jnp.cos(phase), jnp.sin(phase)

    gain_line = jnp.concatenate([attn_gain, mlp_gain]).reshape(1, -1)
    columns = QKV + half_width
    plane = lax.axis_index("wt")
    ids = jnp.stack([quarter, plane, pair, row, side])
    ff_weights = (w_gate, w_up, w_down)

    def attn_local(layer):
        return jnp.concatenate(
            [
                lax.dynamic_slice(weight[layer], (0, cols * pair), (depth, cols))
                for weight, cols in (
                    (w_key, KEY_HALF),
                    (w_value, KEY_HALF),
                    (w_query, QUERY_HALF),
                    (w_out, half_width),
                )
            ],
            axis=1,
        )

    def attn_gather(layer):
        local = attn_local(layer)
        piece = lax.dynamic_slice(local, (half_depth * row, 0), (half_depth, columns))
        if layer == 0:
            line = jnp.pad(gain_line, ((0, 15), (0, columns - gain_line.shape[1])))
            piece = jnp.concatenate([piece, line], axis=0)
        return local, lax.all_gather(piece, "wt", axis=0, tiled=False)

    def attn_weights(local, mine, other, after):
        both = join(ids, local, mine, other, after)
        keep = lax.dynamic_slice(both, (QUERY_HALF * pair, QKV), (QUERY_HALF, half_width))
        send = lax.dynamic_slice(both, (QUERY_HALF * (1 - pair), QKV), (QUERY_HALF, half_width))
        out_w = jnp.concatenate(ordered(pair, keep, flip(send, PAIR)), axis=1)
        return both[:, :QKV], out_w

    def mlp_gather(layer):
        piece = pack(layer, ids, ff_weights)
        return lax.all_gather(piece, "wt", axis=0, tiled=False)

    def mlp_spread(line, ahead, bit):
        first, last = line
        by_row, by_side = ahead or (flip(first, ROW), flip(first, SIDE))
        last_by_row, last_by_side = flip(last, ROW), flip(last, SIDE)
        across = (
            flip(by_row[0], SIDE),
            flip(by_row[1], SIDE) if bit == SIDE else flip(by_side[1], ROW),
            flip(last_by_row[0, :half_depth], SIDE),
            flip(last_by_side[0, half_depth:], ROW),
        )
        return by_row, last_by_row, by_side, last_by_side, *across

    where = jnp.stack([pair, quarter])

    residual = pair_rows(tokens[0]).astype(F32)
    parts = ()
    saved_layers = []
    attn_sets, ff_sets = [], []
    for layer in range(layer_count):
        attn_sets.append(attn_gather(layer))
        ff_sets.append(mlp_gather(layer))
    lines = attn_sets[0][1][:, half_depth, : gain_line.shape[1]].astype(F32)
    gains = (
        lines.reshape(wt_count, 2 * layer_count, depth)
        .transpose(1, 0, 2)
        .reshape(2 * layer_count, 1, wt_count * depth)
    )
    attn_other = flip(others(ids, attn_sets[0][1], half_depth, 0, 3), ROW)
    for layer in range(layer_count):
        last = layer + 1 == layer_count
        local, mine = attn_sets[layer]
        qkv_w, out_w = attn_weights(local, mine, attn_other, ())
        gain_attn, gain_mlp = gains[layer], gains[layer_count + layer]
        residual, normed_attn = add_norm(residual, parts, gain_attn)
        ahead = tuple(flip(early, bit) for bit in (ROW, SIDE)) if layer else ()
        query, key_value, key_value_turned = rope(
            dot_tt(qkv_w, normed_attn), cosine, sine, ahead
        )
        shared = key_value[TAIL:]
        for bit in key_bits:
            shared = jnp.concatenate([shared, flip(shared, bit)], axis=0)
        first = early if layer else others(ids, ff_sets[layer], depth, 0, 2, (shared,))
        line = (first, others(ids, ff_sets[layer], depth, 2, 3, (shared,)))
        spread = mlp_spread(line, ahead, ROW if layer else SIDE)
        attended, lse = attend(
            query, key_value, key_value_turned, shared, key_pos, row_pos, line
        )
        part = dot_tn(attended, out_w).astype(BF16)
        residual_mid, normed_mlp = add_norm(residual, (part, flip(part, PAIR)), gain_mlp)
        late = ()
        if layer + 1 < layer_count:
            next_attn = attn_sets[layer + 1][1]
            attn_other = flip(others(ids, next_attn, half_depth, 0, 3, (attended,)), ROW)
            late = (attn_other,)
        ff_w, down_w, slope, scale, unit, part = mlp(
            layer,
            ids,
            normed_mlp,
            (ff_sets[layer], *spread),
            ff_weights,
            ff_block,
            late,
            0 if layer + 1 == layer_count else 5,
        )
        parts = (part, flip(part, PAIR))
        if layer + 1 < layer_count:
            early = others(ids, ff_sets[layer + 1], depth, 0, 2, (part,))
        saved_layers.append(
            (
                qkv_w,
                out_w,
                ff_w,
                down_w,
                gain_attn,
                gain_mlp,
                residual,
                normed_attn,
                query,
                key_value,
                key_value_turned,
                shared,
                lse,
                attended,
                residual_mid,
                normed_mlp,
                slope,
                scale,
                unit,
            )
        )
        residual = residual_mid
    residual = residual + (parts[0].astype(F32) + parts[1].astype(F32))
    layer_out = own_rows(residual)

    def outer_sum(total):
        for bit in outer_bits:
            total = add(total, flip(total, bit), steps=1)
        return total

    def sum_ff(share, after=()):
        cut = 2 * ff_block
        totals = cross(share, flip(share[:, :cut], ROW), flip(share[:, cut:], SIDE), after)
        return [outer_sum(total) for total in totals]

    def spread_ff(totals):
        gate, up = totals
        gates, ups = [gate, flip(gate, SIDE)], [up, flip(up, ROW)]
        for group in (gates, ups):
            group += [flip(part, PAIR) for part in group]
        return gates + ups

    def sum_rows(share, cut, after=()):
        totals = split_sum(
            share, flip(share[:, :cut], SIDE), flip(share[:, cut:], ROW), after
        )
        return [outer_sum(total) for total in totals]

    def spread_rows(totals):
        by_row, by_side = totals
        joined = order(ids, (by_row, flip(by_row, ROW), by_side, flip(by_side, SIDE)))
        return [joined, flip(joined, PAIR)]

    down_cut, attn_cut = 640, 768

    def scatter(total):
        return lax.psum_scatter(total, "wt", scatter_dimension=0, tiled=total.ndim == 2)

    flow = pair_rows(cotangent[0])
    flow, flow_low = flow.astype(F32), flow
    gain_grads = [None] * (2 * layer_count)
    ff_outs, attn_outs = (
        [shaped((layer_count, *weight.shape[1:]), F32) for weight in group]
        for group in ((w_gate, w_up, w_down), (w_query, w_key, w_value, w_out))
    )
    ff_held = attn_held = None
    shares = {}
    for layer in reversed(range(layer_count)):
        (
            qkv_w,
            out_w,
            ff_w,
            down_w,
            gain_attn,
            gain_mlp,
            residual,
            normed_attn,
            query,
            key_value,
            key_value_turned,
            shared,
            lse,
            attended,
            residual_mid,
            normed_mlp,
            slope,
            scale,
            unit,
        ) = saved_layers[layer]
        older = shares.get(layer + 1)
        row_keep, row_send, side_keep, side_send = down_grad(ids, unit, flow_low, down_cut)
        down_parts = (row_keep, flip(row_send, ROW)), (side_keep, flip(side_send, SIDE))
        done = (row_keep,) if older is None else (row_keep, attn_all)
        gate_keep, gate_send, up_keep, up_send, part = mlp_back(
            flow_low, normed_mlp, slope, scale, down_w, ff_w, after=done
        )
        gate_got, up_got = flip(gate_send, SIDE), flip(up_send, ROW)
        done = () if older is None else (older["ff"],)
        part, down_sum = add_two(*down_parts, done, part)
        done = (down_sum,)
        flow, flow_low, gain_grads[layer_count + layer] = norm_back(
            flow, (part, flip(part, PAIR)), residual_mid, gain_mlp, after=done, pinned=True
        )
        attended_grad = dot_nt(out_w, flow_low).astype(BF16)
        query_grad, own_grad, shared_grad = attend_back(
            query,
            attended_grad,
            key_value,
            key_value_turned,
            shared,
            key_pos,
            row_pos,
            lse,
            cosine,
            sine,
        )
        for bit in reversed(key_bits):
            half = shared_grad.shape[0] // 2
            arrived = flip(shared_grad[half:].astype(BF16), bit)
            shared_grad = shared_grad[:half] + arrived.astype(F32)
            if bit == key_bits[-1]:
                started = shared_grad
        shares[layer] = {"down": scatter(down_sum)}
        done = (started, shares[layer]["down"])
        if older is not None:
            done = (*done, older["attn"])
        ff_sum = add_two((gate_keep, gate_got), (up_keep, up_got), done)
        shares[layer]["ff"] = scatter(ff_sum)
        down_totals = sum_rows(shares[layer]["down"], down_cut, (ff_sum,))
        done = (ff_sum, down_totals[0])
        if older is not None:
            ff_totals = sum_ff(older["ff"], (ff_sum,))
            attn_totals = sum_rows(older["attn"], attn_cut, (ff_sum,))
            done = (*done, ff_totals[0], attn_totals[0])
        grad_qkv = merge(query_grad, own_grad, shared_grad, cosine, sine, done)
        part = dot_nt(grad_qkv, qkv_w).astype(BF16)
        shares[layer]["down"] = spread_rows(down_totals)
        done = (shares[layer]["down"][0],)
        if older is not None:
            older["ff"] = spread_ff(ff_totals)
            older["attn"] = spread_rows(attn_totals)
            done = (*done, older["ff"][1], older["ff"][5], older["attn"][0])
        row_keep, row_send, side_keep, side_send = attn_grad(
            ids, normed_attn, grad_qkv, attended, flow_low, attn_cut, done
        )
        if older is None:
            done = (layer_out,)
        else:
            *ff_held, placed = place(
                place_ff_kernel,
                layer + 1,
                where,
                older["ff"] + older["down"],
                ff_outs,
                ff_held,
                (row_keep,),
            )
            *attn_held, attn_placed = place(
                place_attn_kernel, layer + 1, where, older["attn"], attn_outs, attn_held, (row_keep,)
            )
            done = (placed, attn_placed)
        attn_mine, send = attn_sum(
            pair[None],
            (row_keep, flip(row_send, ROW), side_keep, flip(side_send, SIDE)),
            done,
        )
        done = (attn_mine,)
        flow, flow_low, gain_grads[layer] = norm_back(
            flow, (part, flip(part, PAIR)), residual, gain_attn, after=done
        )
        attn_all = attn_join(pair[None], attn_mine, flip(send, PAIR))
        shares[layer]["attn"] = scatter(attn_all)
    ff_totals = sum_ff(shares[0]["ff"], (attn_all,))
    gain_total = jnp.concatenate(gain_grads, axis=0)
    for bit in [SIDE, ROW] + outer_bits:
        gain_total = gain_total + flip(gain_total, bit)
    bit = 1
    while bit < wt_count:
        gain_total = gain_total + flip(gain_total, bit, "wt", wt_count)
        bit *= 2
    ff = spread_ff(ff_totals)
    *ff_held, placed = place(
        place_ff_kernel, 0, where, ff + shares[0]["down"], ff_outs, ff_held, (gain_total,)
    )
    attn_totals = sum_rows(shares[0]["attn"], attn_cut, (placed,))
    *attn_held, _ = place(
        place_attn_kernel, 0, where, spread_rows(attn_totals), attn_outs, attn_held
    )
    query_out, key_out, value_out, out_out = attn_held
    gate_out, up_out, down_out = ff_held
    token_grad = own_rows(flow)

    gain_share = lax.dynamic_slice(
        gain_total, (0, lax.axis_index("wt") * depth), (2 * layer_count, depth)
    )
    return (
        layer_out[None],
        token_grad[None],
        gain_share[:layer_count],
        query_out,
        key_out,
        value_out,
        out_out,
        gain_share[layer_count:],
        gate_out,
        up_out,
        down_out,
    )


def solution(mesh):
    weight = P(None, "wt", None)
    return jax.shard_map(
        per_device,
        mesh=mesh,
        in_specs=(
            P("wt", "ctx", None),
            P("wt", None),
            P("wt", "ctx", None),
            P(None, "wt"),
            weight,
            weight,
            weight,
            weight,
            P(None, "wt"),
            weight,
            weight,
            weight,
        ),
        out_specs=(
            P("wt", "ctx", None),
            P("wt", "ctx", None),
            P(None, "wt"),
            weight,
            weight,
            weight,
            weight,
            P(None, "wt"),
            weight,
            weight,
            weight,
        ),
        check_vma=False,
    )
```

```python
import functools
import math

import jax
import jax.numpy as jnp
from jax import lax
from jax.experimental import pallas as pl
from jax.experimental.pallas import tpu as pltpu
from jax.sharding import PartitionSpec as P

HEADS = 18
KV_HEADS = 6
HEAD_DIM = 64
HALF = 32
CONT = 256
SHARED = HEADS // KV_HEADS
PAIR_KV = KV_HEADS // 2
PAIR_HEADS = HEADS // 2
RUN = 2 * HALF + CONT
ROWS = 2 * RUN
PROMPT = 4 * HALF
TAIL = 2 * CONT

EPSILON = 1e-05
SCORE_SCALE = 0.125
BASE_TWO = SCORE_SCALE * math.log2(math.e)
MASKED = -1e30

BF16 = jnp.bfloat16
F32 = jnp.float32

PAIR, SIDE, ROW = 1, 2, 4


def dot_nn(left, right):
    return lax.dot_general(left, right, (((1,), (0,)), ((), ())), preferred_element_type=F32)


def dot_nt(left, right):
    return lax.dot_general(left, right, (((1,), (1,)), ((), ())), preferred_element_type=F32)


def dot_tn(left, right):
    return lax.dot_general(left, right, (((0,), (0,)), ((), ())), preferred_element_type=F32)


def dot_tt(left, right):
    return lax.dot_general(left, right, (((0,), (1,)), ((), ())), preferred_element_type=F32)


def turned(value):
    return jnp.transpose(value.astype(F32))


def shaped(shape, dtype):
    return jax.ShapeDtypeStruct(shape, dtype)


WHOLE = pl.BlockSpec(memory_space=pltpu.VMEM)
FAR = pl.BlockSpec(memory_space=pl.ANY)
SCALARS = pl.BlockSpec(memory_space=pltpu.SMEM)


def call(
    kernel, outs, ins, limit, out_specs=None, in_specs=None, after=(), far_in=0, far_out=0, **extra
):
    count, waited = len(ins), len(after)

    def body(*refs):
        kernel(*refs[:count], *refs[count + waited :])

    ins = [
        pltpu.with_memory_space_constraint(value, pltpu.HBM) if index < far_in else value
        for index, value in enumerate(ins)
    ]
    outs = [
        pltpu.HBM(out.shape, out.dtype) if index < far_out else out
        for index, out in enumerate(outs)
    ]
    return pl.pallas_call(
        body,
        out_shape=outs,
        in_specs=(in_specs or [WHOLE] * count) + [FAR] * waited,
        out_specs=out_specs or [WHOLE] * len(outs),
        compiler_params=pltpu.CompilerParams(vmem_limit_bytes=limit << 20),
        cost_estimate=pl.CostEstimate(flops=1, bytes_accessed=1, transcendentals=0),
        **extra,
    )(*ins, *after)


def add_norm_kernel(has_parts, *refs):
    if has_parts:
        held, mine, other, gain, total_ref, normed_ref = refs
        total = held[...] + (mine[...].astype(F32) + other[...].astype(F32))
        total_ref[...] = total
    else:
        held, gain, normed_ref = refs
        total = held[...]
    inverse = lax.rsqrt(jnp.mean(total * total, axis=-1, keepdims=True) + EPSILON)
    normed_ref[...] = (total * inverse * gain[...]).astype(BF16)


def add_norm(held, parts, gain, after=()):
    rows, width = held.shape
    step = 128
    block = pl.BlockSpec((step, width), lambda i: (i, 0))
    line = pl.BlockSpec((1, width), lambda i: (0, 0))
    ins = (held, *parts, gain)
    outs = ([shaped(held.shape, F32)] if parts else []) + [shaped(held.shape, BF16)]
    result = call(
        functools.partial(add_norm_kernel, bool(parts)),
        outs,
        ins,
        10,
        in_specs=[block] * (1 + len(parts)) + [line],
        out_specs=[block] * len(outs),
        grid=(rows // step,),
        after=after,
    )
    return result if parts else (held, result[0])


def norm_back_kernel(flow, mine, other, held, gain, flow_ref, low_ref, gain_ref):
    grad = mine[...].astype(F32) + other[...].astype(F32)
    value = held[...]
    inverse = lax.rsqrt(jnp.mean(value * value, axis=-1, keepdims=True) + EPSILON)
    plain = value * inverse
    scaled = grad * gain[...]
    tilt = jnp.mean(scaled * plain, axis=-1, keepdims=True)
    total = flow[...] + inverse * (scaled - plain * tilt)
    flow_ref[...] = total
    low_ref[...] = total.astype(BF16)

    @pl.when(pl.program_id(0) == 0)
    def _():
        gain_ref[...] = jnp.zeros_like(gain_ref)

    gain_ref[...] += jnp.sum(grad * plain, axis=0, keepdims=True)


def norm_back(flow, parts, held, gain, after=(), pinned=False):
    rows, width = held.shape
    step = 128
    block = pl.BlockSpec((step, width), lambda i: (i, 0))
    line = pl.BlockSpec((1, width), lambda i: (0, 0))
    return call(
        norm_back_kernel,
        [shaped(held.shape, F32), shaped(held.shape, BF16), shaped((1, width), F32)],
        (flow, *parts, held, gain),
        12,
        in_specs=[block] * 4 + [line],
        out_specs=[block, block, line],
        grid=(rows // step,),
        after=after,
        far_in=4 if pinned else 0,
    )


def add_kernel(mine, other, out):
    out[...] = (mine[...].astype(F32) + other[...].astype(F32)).astype(BF16)


def add_two_kernel(first_mine, first_other, second_mine, second_other, *refs):
    out = refs[-1]
    if len(refs) == 3:
        refs[1][...] = refs[0][...]
    first = first_mine[...].astype(F32) + first_other[...].astype(F32)
    second = second_mine[...].astype(F32) + second_other[...].astype(F32)
    axis = len(out.shape) - 1
    out[...] = jnp.concatenate([first.astype(BF16), second.astype(BF16)], axis=axis)


def add_two(first, second, after=(), passed=None):
    ins = (*first, *second)
    lead = first[0].shape[:-1]
    steps = 4

    def block(*shape):
        shape = (shape[0] // steps, *shape[1:])
        return pl.BlockSpec(shape, lambda i: (i,) + (0,) * (len(shape) - 1))

    columns = first[0].shape[-1] + second[0].shape[-1]
    extra = () if passed is None else (passed,)
    result = call(
        add_two_kernel,
        [shaped(part.shape, part.dtype) for part in extra] + [shaped((*lead, columns), BF16)],
        (*ins, *extra),
        12,
        in_specs=[block(*part.shape) for part in (*ins, *extra)],
        out_specs=[block(*part.shape) for part in extra] + [block(*lead, columns)],
        grid=(steps,),
        after=after,
        far_in=4,
    )
    return result if extra else result[0]


def split_sum_kernel(share, row_other, side_other, row_out, side_out):
    cut = row_out.shape[1]
    row_out[...] = (share[:, :cut].astype(F32) + row_other[...].astype(F32)).astype(BF16)
    side_out[...] = (share[:, cut:].astype(F32) + side_other[...].astype(F32)).astype(BF16)


def split_sum(share, row_other, side_other, after=()):
    return call(
        split_sum_kernel,
        [shaped(row_other.shape, BF16), shaped(side_other.shape, BF16)],
        (share, row_other, side_other),
        8,
        after=after,
    )


def order_kernel(ids_ref, row_mine, row_other, side_mine, side_other, out):
    side, row = ids_ref[4], ids_ref[3]
    half, cut = row_mine.shape
    for value, mine, other, cols in (
        (row, row_mine, row_other, slice(0, cut)),
        (side, side_mine, side_other, slice(cut, None)),
    ):
        for index in range(2):
            chosen = jnp.where(value == index, mine[...], other[...])
            out[index * half : (index + 1) * half, cols] = chosen


def order(ids, parts):
    half, cut = parts[0].shape
    return call(
        order_kernel,
        [shaped((2 * half, cut + parts[2].shape[1]), BF16)],
        (ids, *parts),
        8,
        in_specs=[SCALARS] + [WHOLE] * 4,
    )[0]


def cross_kernel(share, gate_other, up_other, gate_out, up_out):
    block = gate_out.shape[1] // 2
    for out, other, low in ((gate_out, gate_other, 0), (up_out, up_other, 2 * block)):
        for index in range(2):
            mine = share[:, low + index * block : low + (index + 1) * block]
            theirs = other[:, (1 - index) * block : (2 - index) * block]
            out[:, index * block : (index + 1) * block] = (
                mine.astype(F32) + theirs.astype(F32)
            ).astype(BF16)


def cross(share, gate_other, up_other, after=()):
    shape = (share.shape[0], share.shape[1] // 2)
    return call(
        cross_kernel,
        [shaped(shape, BF16)] * 2,
        (share, gate_other, up_other),
        8,
        after=after,
    )


def add(mine, other, after=(), steps=4):
    shape = mine.shape
    block = pl.BlockSpec(
        (shape[0] // steps, *shape[1:]), lambda i: (i,) + (0,) * (len(shape) - 1)
    )
    return call(
        add_kernel,
        [shaped(shape, BF16)],
        (mine, other),
        12,
        in_specs=[block, block],
        out_specs=[block],
        grid=(steps,),
        after=after,
    )[0]


KEY_HALF = PAIR_KV * HEAD_DIM
QUERY_HALF = PAIR_HEADS * HEAD_DIM
QKV = 2 * KEY_HALF + QUERY_HALF


def rope_kernel(qkv_ref, cos_ref, sin_ref, query_ref, kv_ref, kv_turned_ref):
    cosine, sine = cos_ref[...], sin_ref[...]
    half = HEAD_DIM // 2

    def head(source, target_ref, target):
        low = qkv_ref[source : source + half, :]
        high = qkv_ref[source + half : source + 2 * half, :]
        target_ref[target : target + half, :] = (low * cosine - high * sine).astype(BF16)
        target_ref[target + half : target + 2 * half, :] = (high * cosine + low * sine).astype(
            BF16
        )

    for index in range(PAIR_KV):
        head(index * HEAD_DIM, kv_turned_ref, index * HEAD_DIM)
    kv_turned_ref[KEY_HALF:, :] = qkv_ref[KEY_HALF : 2 * KEY_HALF, :].astype(BF16)
    kv_ref[...] = turned(kv_turned_ref[...]).astype(BF16)
    for index in range(PAIR_HEADS):
        head(2 * KEY_HALF + index * HEAD_DIM, query_ref, index * HEAD_DIM)


def rope(qkv, cosine, sine, after=()):
    return call(
        rope_kernel,
        [
            shaped((QUERY_HALF, ROWS), BF16),
            shaped((ROWS, 2 * KEY_HALF), BF16),
            shaped((2 * KEY_HALF, ROWS), BF16),
        ],
        (qkv, cosine, sine),
        14,
        after=after,
    )


def later_mask():
    key = lax.broadcasted_iota(jnp.int32, (CONT, CONT), 0)
    query = lax.broadcasted_iota(jnp.int32, (CONT, CONT), 1)
    return key <= query


def attend_kernel(
    query_ref, kv_ref, kv_turned_ref, shared_ref, key_pos_ref, row_pos_ref, out_ref, lse_ref
):
    shared_values = turned(shared_ref[:, KEY_HALF:]).astype(BF16)
    for kv_head in range(PAIR_KV):
        low = kv_head * HEAD_DIM
        keys = shared_ref[:, low : low + HEAD_DIM]
        values = shared_values[low : low + HEAD_DIM, :]

        def head(index, carry, kv_head=kv_head, low=low, keys=keys, values=values):
            number = kv_head * SHARED + index
            base = pl.multiple_of(number * HEAD_DIM, HEAD_DIM)
            allowed = key_pos_ref[...] <= row_pos_ref[...]
            query = query_ref[pl.ds(base, HEAD_DIM), TAIL:]
            scores = jnp.where(allowed, dot_nn(keys, query) * BASE_TWO, MASKED)
            top = jnp.max(scores, axis=0, keepdims=True)
            weight = jnp.exp2(scores - top)
            total = jnp.sum(weight, axis=0, keepdims=True)
            out = dot_nn(values, weight.astype(BF16)) / total
            out_ref[pl.ds(base, HEAD_DIM), TAIL:] = out.astype(BF16)
            lse_ref[number, :, TAIL:] = top + jnp.log2(total)
            for run in range(2):
                cols = slice(run * CONT, (run + 1) * CONT)
                query = query_ref[pl.ds(base, HEAD_DIM), cols]
                own_keys = kv_ref[cols, low : low + HEAD_DIM]
                own_values = kv_turned_ref[KEY_HALF + low : KEY_HALF + low + HEAD_DIM, cols]
                first = dot_nn(keys, query) * BASE_TWO
                second = jnp.where(later_mask(), dot_nn(own_keys, query) * BASE_TWO, MASKED)
                top = jnp.maximum(
                    jnp.max(first, axis=0, keepdims=True), jnp.max(second, axis=0, keepdims=True)
                )
                first = jnp.exp2(first - top)
                second = jnp.exp2(second - top)
                total = jnp.sum(first, axis=0, keepdims=True) + jnp.sum(
                    second, axis=0, keepdims=True
                )
                out = dot_nn(values, first.astype(BF16)) + dot_nn(
                    own_values, second.astype(BF16)
                )
                out_ref[pl.ds(base, HEAD_DIM), cols] = (out / total).astype(BF16)
                lse_ref[number, :, cols] = top + jnp.log2(total)
            return carry

        lax.fori_loop(0, SHARED, head, 0, unroll=True)


def attend(query, key_value, key_value_turned, shared, key_pos, row_pos, after=()):
    return call(
        attend_kernel,
        [shaped((QUERY_HALF, ROWS), BF16), shaped((PAIR_HEADS, 1, ROWS), F32)],
        (query, key_value, key_value_turned, shared, key_pos, row_pos),
        16 + shared.shape[0] // 64,
        after=after,
    )


def attend_back_kernel(
    query_ref,
    grad_ref,
    kv_ref,
    kv_turned_ref,
    shared_ref,
    key_pos_ref,
    row_pos_ref,
    lse_ref,
    cos_ref,
    sin_ref,
    query_grad_ref,
    own_grad_ref,
    shared_grad_ref,
    score_keep,
    weight_keep,
    own_score_keep,
    own_weight_keep,
):
    shared_turned = turned(shared_ref[:, :KEY_HALF]).astype(BF16)
    half = HEAD_DIM // 2
    for kv_head in range(PAIR_KV):
        low = kv_head * HEAD_DIM
        keys = shared_ref[:, low : low + HEAD_DIM]
        values = shared_ref[:, KEY_HALF + low : KEY_HALF + low + HEAD_DIM]
        keys_turned = shared_turned[low : low + HEAD_DIM, :]

        def head(index, carry, kv_head=kv_head, low=low, keys=keys, values=values, keys_turned=keys_turned):
            number = kv_head * SHARED + index
            base = pl.multiple_of(number * HEAD_DIM, HEAD_DIM)

            def put_query_grad(grad, cols):
                cosine, sine = cos_ref[:, cols], sin_ref[:, cols]
                first, second = grad[:half], grad[half:]
                query_grad_ref[pl.ds(base, half), cols] = (
                    (first * cosine + second * sine) * SCORE_SCALE
                ).astype(BF16)
                query_grad_ref[pl.ds(base + half, half), cols] = (
                    (second * cosine - first * sine) * SCORE_SCALE
                ).astype(BF16)

            cols = slice(TAIL, ROWS)
            query = query_ref[pl.ds(base, HEAD_DIM), cols]
            grad = grad_ref[pl.ds(base, HEAD_DIM), cols]
            lse = lse_ref[number, :, cols]
            allowed = key_pos_ref[...] <= row_pos_ref[...]
            scores = jnp.where(allowed, dot_nn(keys, query) * BASE_TWO, MASKED)
            weight = jnp.exp2(scores - lse)
            weight_keep[index, :, cols] = weight.astype(BF16)
            flow = weight * dot_nn(values, grad)
            delta = jnp.sum(flow, axis=0, keepdims=True)
            flow = (flow - weight * delta).astype(BF16)
            score_keep[index, :, cols] = flow
            put_query_grad(dot_nn(keys_turned, flow), cols)
            for run in range(2):
                cols = slice(run * CONT, (run + 1) * CONT)
                query = query_ref[pl.ds(base, HEAD_DIM), cols]
                grad = grad_ref[pl.ds(base, HEAD_DIM), cols]
                lse = lse_ref[number, :, cols]
                own_keys = kv_ref[cols, low : low + HEAD_DIM]
                own_values = kv_ref[cols, KEY_HALF + low : KEY_HALF + low + HEAD_DIM]
                own_turned = kv_turned_ref[low : low + HEAD_DIM, cols]
                first = jnp.exp2(dot_nn(keys, query) * BASE_TWO - lse)
                second = jnp.where(later_mask(), dot_nn(own_keys, query) * BASE_TWO, MASKED)
                second = jnp.exp2(second - lse)
                weight_keep[index, :, cols] = first.astype(BF16)
                own_weight_keep[index, :, cols] = second.astype(BF16)
                first_flow = first * dot_nn(values, grad)
                second_flow = second * dot_nn(own_values, grad)
                delta = jnp.sum(first_flow, axis=0, keepdims=True) + jnp.sum(
                    second_flow, axis=0, keepdims=True
                )
                first_flow = (first_flow - first * delta).astype(BF16)
                second_flow = (second_flow - second * delta).astype(BF16)
                score_keep[index, :, cols] = first_flow
                own_score_keep[index, :, cols] = second_flow
                put_query_grad(
                    dot_nn(keys_turned, first_flow) + dot_nn(own_turned, second_flow), cols
                )
            return carry

        lax.fori_loop(0, SHARED, head, 0, unroll=True)
        key_sum, value_sum = 0.0, 0.0
        own_key_sum, own_value_sum = [0.0, 0.0], [0.0, 0.0]
        for index in range(SHARED):
            base = (kv_head * SHARED + index) * HEAD_DIM
            query = query_ref[base : base + HEAD_DIM, :]
            grad = grad_ref[base : base + HEAD_DIM, :]
            key_sum = key_sum + dot_nt(score_keep[index], query)
            value_sum = value_sum + dot_nt(weight_keep[index], grad)
            for run in range(2):
                cols = slice(run * CONT, (run + 1) * CONT)
                own_key_sum[run] = own_key_sum[run] + dot_nt(
                    own_score_keep[index, :, cols], query[:, cols]
                )
                own_value_sum[run] = own_value_sum[run] + dot_nt(
                    own_weight_keep[index, :, cols], grad[:, cols]
                )
        shared_grad_ref[:, low : low + HEAD_DIM] = key_sum * SCORE_SCALE
        shared_grad_ref[:, KEY_HALF + low : KEY_HALF + low + HEAD_DIM] = value_sum
        for run in range(2):
            cols = slice(run * CONT, (run + 1) * CONT)
            own_grad_ref[cols, low : low + HEAD_DIM] = own_key_sum[run] * SCORE_SCALE
            own_grad_ref[cols, KEY_HALF + low : KEY_HALF + low + HEAD_DIM] = own_value_sum[run]


def attend_back(
    query, grad, key_value, key_value_turned, shared, key_pos, row_pos, lse, cosine, sine, after=()
):
    count = shared.shape[0]
    return call(
        attend_back_kernel,
        [
            shaped((QUERY_HALF, ROWS), BF16),
            shaped((TAIL, 2 * KEY_HALF), F32),
            shaped((count, 2 * KEY_HALF), F32),
        ],
        (query, grad, key_value, key_value_turned, shared, key_pos, row_pos, lse, cosine, sine),
        22 + count // 64,
        scratch_shapes=[
            pltpu.VMEM((SHARED, count, ROWS), BF16),
            pltpu.VMEM((SHARED, count, ROWS), BF16),
            pltpu.VMEM((SHARED, CONT, TAIL), BF16),
            pltpu.VMEM((SHARED, CONT, TAIL), BF16),
        ],
        after=after,
    )


def merge_kernel(query_grad_ref, own_ref, prompt_ref, cos_ref, sin_ref, out_ref):
    cosine, sine = cos_ref[...], sin_ref[...]
    half = HEAD_DIM // 2
    both = turned(jnp.concatenate([own_ref[...], prompt_ref[...]], axis=0))
    pieces = []
    for index in range(PAIR_KV):
        low = both[index * HEAD_DIM : index * HEAD_DIM + half]
        high = both[index * HEAD_DIM + half : (index + 1) * HEAD_DIM]
        pieces += [low * cosine + high * sine, high * cosine - low * sine]
    both = jnp.concatenate(pieces + [both[KEY_HALF:]], axis=0)
    out_ref[:, : 2 * KEY_HALF] = jnp.transpose(both).astype(BF16)
    out_ref[:, 2 * KEY_HALF :] = turned(query_grad_ref[...]).astype(BF16)


def merge(query_grad, own_grad, prompt_grad, cosine, sine, after=()):
    return call(
        merge_kernel,
        [shaped((ROWS, QKV), BF16)],
        (query_grad, own_grad, prompt_grad, cosine, sine),
        16,
        after=after,
    )[0]


def mlp_kernel(layer, ids_ref, normed_ref, *refs):
    own = refs[0]
    from_row, from_side, from_across = refs[1:3], refs[3:5], refs[5:9]
    gate_ref, up_ref, down_shard = (ref.at[layer] for ref in refs[9:12])
    weight_ref, down_ref, slope_ref, scale_ref, unit_ref, out_ref = refs[12:18]
    held, sems, down_sem, keep_sem = refs[18:]
    rows, depth = normed_ref.shape
    block = held.shape[2] // 2
    shard = depth // 4
    lines = block // 4
    wide = depth // 3
    quarter, plane, pair = ids_ref[0], ids_ref[1], ids_ref[2]
    slots = line_slots(plane)

    def copy(source, target, sem):
        pltpu.make_async_copy(source, target, sem).start()

    def at(start, size):
        return pl.ds(pl.multiple_of(start, 16), size)

    def pieces(part):
        if part == 0:
            return [(own.at[owner], 0, shard, owner) for owner in (plane, *slots)]
        if part < 3:
            pair_of_slots, last = (from_row, from_side)[part - 1]
            arrived = (pair_of_slots.at[0], pair_of_slots.at[1], last.at[0])
            return [(arrived[slot], 0, shard, slots[slot]) for slot in range(3)]
        half = shard // 2
        return [
            (from_across[0], 0, shard, slots[0]),
            (from_across[1], 0, shard, slots[1]),
            (from_across[2], 0, half, slots[2]),
            (from_across[3], half, shard, slots[2]),
        ]

    for part in range(4):
        for source, low, high, owner in pieces(part):
            copy(
                source.at[:, : 2 * block],
                held.at[part, at(shard * owner + low, high - low)],
                sems.at[part],
            )
        if part == 0:
            continue
        col = pl.ds(pl.multiple_of((2 * (quarter ^ part) + pair) * block, block), block)
        for index, ref in enumerate((gate_ref, up_ref)):
            copy(
                ref.at[:, col],
                held.at[part, at(shard * plane, shard), pl.ds(index * block, block)],
                sems.at[part],
            )
    taken = pl.ds(2 * block, wide)

    def down_copies(source, low, high, place, piece):
        for column in range(3):
            first, last = max(low, lines * column), min(high, lines * (column + 1))
            if first < last:
                copy(
                    source.at[at(first - low, last - first), taken],
                    down_ref.at[
                        at(
                            block * place + lines * (quarter ^ piece) + first - lines * column,
                            last - first,
                        ),
                        pl.ds(wide * column, wide),
                    ],
                    down_sem,
                )

    for part in range(4):
        for source, low, high, owner in pieces(part):
            down_copies(source, low, high, quarter ^ owner, part)
        if part == 0:
            continue
        copy(
            down_shard.at[at(block * pair + lines * (quarter ^ part), lines)],
            down_ref.at[at(block * (quarter ^ plane) + lines * (quarter ^ part), lines)],
            down_sem,
        )

    step = rows // 2
    kept = []
    for part in range(4):
        pltpu.make_async_copy(held.at[part], held.at[part], sems.at[part]).wait()
        kept.append(pltpu.make_async_copy(held.at[part], weight_ref.at[part], keep_sem.at[part]))
        kept[-1].start()

        def tile(index, carry, part=part):
            some = pl.ds(pl.multiple_of(index * step, step), step)
            normed = normed_ref[some, :]
            gate = dot_nn(normed, held[part, :, :block])
            up = dot_nn(normed, held[part, :, block:])
            sigmoid = 1.0 / (1.0 + jnp.exp(-gate))
            scale = gate * sigmoid
            cols = slice(part * block, (part + 1) * block)
            slope_ref[some, cols] = (up * sigmoid * (1.0 + gate * (1.0 - sigmoid))).astype(BF16)
            scale_ref[some, cols] = scale.astype(BF16)
            unit_ref[some, cols] = (scale * up).astype(BF16)
            return carry

        lax.fori_loop(0, 2, tile, 0, unroll=True)
    pltpu.make_async_copy(down_ref, down_ref, down_sem).wait()

    def finish(index, carry):
        some = pl.ds(pl.multiple_of(index * step, step), step)
        out_ref[some, :] = dot_nn(unit_ref[some, :], down_ref[...]).astype(BF16)
        return carry

    lax.fori_loop(0, 2, finish, 0, unroll=True)
    for part in kept:
        part.wait()


def mlp(layer, ids, normed, pieces, weights, block, after=(), far_out=0):
    rows, depth = normed.shape
    units = 4 * block
    ins = (ids, normed, *pieces, *weights)
    return call(
        functools.partial(mlp_kernel, layer),
        [
            shaped((4, depth, 2 * block), BF16),
            shaped((units, depth), BF16),
            shaped((rows, units), BF16),
            shaped((rows, units), BF16),
            shaped((rows, units), BF16),
            shaped((rows, depth), BF16),
        ],
        ins,
        32,
        in_specs=[SCALARS, WHOLE] + [FAR] * (len(ins) - 2),
        out_specs=[FAR] + [WHOLE] * 5,
        scratch_shapes=[
            pltpu.VMEM((4, depth, 2 * block), BF16),
            pltpu.SemaphoreType.DMA((4,)),
            pltpu.SemaphoreType.DMA,
            pltpu.SemaphoreType.DMA((4,)),
        ],
        after=after,
        far_out=far_out,
    )


def pack_kernel(layer, ids_ref, gate_ref, up_ref, down_ref, out, sem):
    quarter, pair = ids_ref[0], ids_ref[2]
    depth, columns = out.shape
    wide = columns // 3
    lines = depth // 3
    col = pl.ds(pl.multiple_of((2 * quarter + pair) * wide, wide), wide)
    for index, ref in enumerate((gate_ref, up_ref)):
        target = out.at[:, pl.ds(index * wide, wide)]
        pltpu.make_async_copy(ref.at[layer, :, col], target, sem).start()
    start = pl.multiple_of((4 * pair + quarter) * lines, lines)
    for index in range(3):
        pltpu.make_async_copy(
            down_ref.at[layer, pl.ds(start, lines), pl.ds(index * wide, wide)],
            out.at[pl.ds(index * lines, lines), pl.ds(2 * wide, wide)],
            sem,
        ).start()
    pltpu.make_async_copy(out, out, sem).wait()


def pack(layer, ids, weights, after=()):
    _, depth, units = weights[0].shape
    return call(
        functools.partial(pack_kernel, layer),
        [shaped((depth, 3 * units // 8), BF16)],
        (ids, *weights),
        16,
        in_specs=[SCALARS] + [FAR] * 3,
        scratch_shapes=[pltpu.SemaphoreType.DMA],
        after=after,
    )[0]


def deal(total, row, side, cut, place, row_keep, row_send, side_keep, side_send):
    half = total.shape[0] // 2
    for index in range(2):
        part = total[index * half : (index + 1) * half]
        for value, keep, send, cols in (
            (row, row_keep, row_send, slice(0, cut)),
            (side, side_keep, side_send, slice(cut, None)),
        ):

            @pl.when(value == index)
            def _(part=part, keep=keep, cols=cols):
                keep[place] = part[:, cols]

            @pl.when(value != index)
            def _(part=part, send=send, cols=cols):
                send[place] = part[:, cols]


def dealt(blocks, half, columns, cut):
    return [
        shaped((blocks, half, size), BF16) for size in (cut, cut, columns - cut, columns - cut)
    ]


def down_grad_kernel(cut, ids_ref, unit_ref, flow_ref, *outs):
    quarter, side, row = ids_ref[0], ids_ref[4], ids_ref[3]
    block = unit_ref.shape[1] // 4
    for place in range(4):
        total = dot_tn(unit_ref[:, place * block : (place + 1) * block], flow_ref[...])
        deal(total.astype(BF16), row, side, cut, quarter ^ place, *outs)


def down_grad(ids, unit, flow, cut, after=()):
    rows, units = unit.shape
    width = flow.shape[1]
    return call(
        functools.partial(down_grad_kernel, cut),
        dealt(4, units // 8, width, cut),
        (ids, unit, flow),
        16,
        in_specs=[SCALARS, WHOLE, WHOLE],
        after=after,
    )


def mlp_back_kernel(
    flow_ref,
    normed_ref,
    slope_ref,
    scale_ref,
    down_ref,
    weight_ref,
    gate_keep,
    gate_send,
    up_keep,
    up_send,
    out_ref,
    held,
    total,
    unit_grad,
    sems,
):
    rows, depth = normed_ref.shape
    block = held.shape[2] // 2
    order = (3, 2, 1, 0)
    copies = {
        part: pltpu.make_async_copy(weight_ref.at[part], held.at[part], sems.at[part])
        for part in order
    }
    for part in order:
        copies[part].start()
    step = rows // 2
    for part in order:
        cols = slice(part * block, (part + 1) * block)

        def tile(index, carry, cols=cols):
            at = pl.ds(pl.multiple_of(index * step, step), step)
            grad = dot_nt(flow_ref[at, :], down_ref[cols, :])
            unit_grad[at, :block] = (grad * slope_ref[at, cols].astype(F32)).astype(BF16)
            unit_grad[at, block:] = (grad * scale_ref[at, cols].astype(F32)).astype(BF16)
            return carry

        lax.fori_loop(0, 2, tile, 0, unroll=True)
        both = dot_tn(normed_ref[...], unit_grad[...]).astype(BF16)
        target = gate_send if part >= 2 else gate_keep
        target[:, (part % 2) * block : (part % 2 + 1) * block] = both[:, :block]
        target = up_send if part % 2 else up_keep
        target[:, (part // 2) * block : (part // 2 + 1) * block] = both[:, block:]
        copies[part].wait()

        def gather(index, carry, part=part):
            at = pl.ds(pl.multiple_of(index * step, step), step)
            value = dot_nt(unit_grad[at, :], held[part])
            if part == order[0]:
                total[at, :] = value
            elif part == order[-1]:
                out_ref[at, :] = (total[at, :] + value).astype(BF16)
            else:
                total[at, :] += value
            return carry

        lax.fori_loop(0, 2, gather, 0, unroll=True)


def mlp_back(flow, normed, slope, scale, down, weights, after=()):
    rows, depth = normed.shape
    block = down.shape[0] // 4
    return call(
        mlp_back_kernel,
        [shaped((depth, 2 * block), BF16)] * 4 + [shaped((rows, depth), BF16)],
        (flow, normed, slope, scale, down, weights),
        40,
        in_specs=[WHOLE] * 5 + [FAR],
        scratch_shapes=[
            pltpu.VMEM((4, depth, 2 * block), BF16),
            pltpu.VMEM((rows, depth), F32),
            pltpu.VMEM((rows, 2 * block), BF16),
            pltpu.SemaphoreType.DMA((4,)),
        ],
        after=after,
        far_out=4,
    )


def local_kernel(ids_ref, gain_ref, key_ref, value_ref, query_ref, out_ref, local, piece):
    row, pair = ids_ref[3], ids_ref[2]
    half = local.shape[0] // 2
    low = 0
    for ref in (key_ref, value_ref, query_ref, out_ref):
        cols = ref.shape[2] // 2
        for index in range(2):

            @pl.when(pair == index)
            def _(ref=ref, low=low, cols=cols, index=index):
                local[:, low : low + cols] = ref[0, :, index * cols : (index + 1) * cols]

        low += cols
    for index in range(2):

        @pl.when(row == index)
        def _(index=index):
            piece[:half, :] = local[index * half : (index + 1) * half, :]

    if piece.shape[0] > half:
        piece[half:, :] = jnp.broadcast_to(gain_ref[...], (piece.shape[0] - half, low))


def local_weights(layer, ids, gains, weights):
    depth = weights[0].shape[1]
    columns = sum(weight.shape[2] for weight in weights) // 2
    rows = depth // 2 + (0 if layer else 16)
    return call(
        local_kernel,
        [shaped((depth, columns), BF16), shaped((rows, columns), BF16)],
        (ids, gains, *weights),
        16,
        in_specs=[SCALARS, pl.BlockSpec(gains.shape, lambda _: (0, 0))]
        + [
            pl.BlockSpec((1, *weight.shape[1:]), lambda _: (layer, 0, 0)) for weight in weights
        ],
        out_specs=[
            pl.BlockSpec((depth, columns), lambda _: (0, 0)),
            pl.BlockSpec((rows, columns), lambda _: (0, 0)),
        ],
        grid=(1,),
    )


def join_kernel(ids_ref, local, mine, other, out, sem):
    plane, row = ids_ref[1], ids_ref[3]
    half = local.shape[0] // 2

    def copy(source, start):
        target = out.at[pl.ds(pl.multiple_of(start, 16), source.shape[0])]
        pltpu.make_async_copy(source, target, sem).start()

    copy(local, 2 * half * plane)
    for slot, owner in enumerate(line_slots(plane)):
        copy(mine.at[owner, pl.ds(0, half)], half * (2 * owner + row))
        copy(other.at[slot], half * (2 * owner + 1 - row))
    pltpu.make_async_copy(out, out, sem).wait()


def join(ids, local, mine, other, after=()):
    shape = (4 * local.shape[0], local.shape[1])
    return call(
        join_kernel,
        [shaped(shape, BF16)],
        (ids, local, mine, other),
        16,
        in_specs=[SCALARS] + [FAR] * 3,
        scratch_shapes=[pltpu.SemaphoreType.DMA],
        after=after,
    )[0]


def others_kernel(first, ids_ref, gathered, out, sem):
    count, rows, _ = out.shape
    for slot, owner in enumerate(line_slots(ids_ref[1])[first : first + count]):
        pltpu.make_async_copy(gathered.at[owner, pl.ds(0, rows)], out.at[slot], sem).start()
    pltpu.make_async_copy(out, out, sem).wait()


def others(ids, gathered, rows, first, last, after=()):
    return call(
        functools.partial(others_kernel, first),
        [shaped((last - first, rows, gathered.shape[2]), BF16)],
        (ids, gathered),
        16,
        in_specs=[SCALARS, FAR],
        scratch_shapes=[pltpu.SemaphoreType.DMA],
        after=after,
    )[0]


def line_slots(plane):
    return [plane ^ step for step in (1, 2, 3)]


def attn_grad_kernel(cut, ids_ref, normed, grad, attended, flow, *outs):
    side, row = ids_ref[4], ids_ref[3]
    blocks, half, _ = outs[0].shape
    out_cols = flow.shape[1] // 2
    out = dot_nn(attended[...], flow[...]).astype(BF16)
    for block in range(blocks):
        low, col = 2 * (block // 2) * half, (block % 2) * out_cols
        total = jnp.concatenate(
            [
                dot_tn(normed[:, 2 * block * half : 2 * (block + 1) * half], grad[...]).astype(
                    BF16
                ),
                out[low : low + 2 * half, col : col + out_cols],
            ],
            axis=1,
        )
        deal(total, row, side, cut, block, *outs)


def attn_grad(ids, normed, grad, attended, flow, cut, after=()):
    columns = grad.shape[1] + flow.shape[1] // 2
    return call(
        functools.partial(attn_grad_kernel, cut),
        dealt(4, normed.shape[1] // 8, columns, cut),
        (ids, normed, grad, attended, flow),
        20,
        in_specs=[SCALARS] + [WHOLE] * 4,
        after=after,
    )


def attn_sum_kernel(pair_ref, row_mine, row_other, side_mine, side_other, keep_ref, send_ref):
    pair = pair_ref[0]
    total = jnp.concatenate(
        [
            (mine[...].astype(F32) + other[...].astype(F32)).astype(BF16)
            for mine, other in ((row_mine, row_other), (side_mine, side_other))
        ],
        axis=2,
    )
    keep_ref[:, :, :QKV] = total[:, :, :QKV]
    for plane in range(4):
        for owner in range(2):

            @pl.when(pair == owner)
            def _(plane=plane, owner=owner):
                if plane // 2 == owner:
                    keep_ref[plane, :, QKV:] = total[2 * (plane % 2) + owner, :, QKV:]
                else:
                    send_ref[plane % 2] = total[2 * (plane % 2) + 1 - owner, :, QKV:]
                    keep_ref[plane, :, QKV:] = jnp.zeros_like(keep_ref[plane, :, QKV:])


def attn_sum(pair, parts, after=()):
    blocks, half, first = parts[0].shape
    columns = first + parts[2].shape[2]
    return call(
        attn_sum_kernel,
        [
            shaped((blocks, half, columns), BF16),
            shaped((blocks // 2, half, columns - QKV), BF16),
        ],
        (pair, *parts),
        16,
        in_specs=[SCALARS] + [WHOLE] * 4,
        after=after,
    )


def attn_join_kernel(pair_ref, mine, other, out):
    pair = pair_ref[0]
    out[:, :, :QKV] = mine[:, :, :QKV]
    for plane in range(4):
        for owner in range(2):

            @pl.when(pair == owner)
            def _(plane=plane, owner=owner):
                if plane // 2 == owner:
                    out[plane, :, QKV:] = mine[plane, :, QKV:]
                else:
                    out[plane, :, QKV:] = other[plane % 2]


def attn_join(pair, mine, other, after=()):
    return call(
        attn_join_kernel,
        [shaped(mine.shape, BF16)],
        (pair, mine, other),
        12,
        in_specs=[SCALARS, WHOLE, WHOLE],
        after=after,
    )[0]


def place_ff_kernel(where_ref, *refs):
    gates, ups, downs = refs[0:4], refs[4:8], refs[8:10]
    gate_out, up_out, down_out = refs[10:]
    pair, quarter = where_ref[0], where_ref[1]
    block = gates[0].shape[1] // 2
    for out, pieces, spread, inner in ((gate_out, gates, 2, 1), (up_out, ups, 1, 2)):
        for number, ref in enumerate(pieces):
            owner = pair ^ (number // 2)
            for index in range(2):
                plane = quarter ^ ((number % 2) * spread + index * inner)
                col = pl.multiple_of((2 * plane + owner) * block, block)
                out[0, :, pl.ds(col, block)] = ref[
                    :, index * block : (index + 1) * block
                ].astype(F32)
    down_rows = downs[0].shape[0]
    for where_from, owner in ((downs[0], pair), (downs[1], 1 - pair)):
        down_out[0, pl.ds(pl.multiple_of(owner * down_rows, down_rows), down_rows), :] = (
            where_from[...].astype(F32)
        )


def place_attn_kernel(where_ref, attn_mine, attn_other, *refs):
    query_out, key_out, value_out, out_out = refs
    pair = where_ref[0]
    first = jnp.where(pair == 0, attn_mine[...], attn_other[...]).astype(F32)
    second = jnp.where(pair == 0, attn_other[...], attn_mine[...]).astype(F32)
    low = 0
    for out, cols in (
        (key_out, KEY_HALF),
        (value_out, KEY_HALF),
        (query_out, QUERY_HALF),
        (out_out, first.shape[1] - QKV),
    ):
        out[0] = jnp.concatenate([first[:, low : low + cols], second[:, low : low + cols]], axis=1)
        low += cols


def place_kernel(kernel, fresh, parts, outs, *refs):
    here = refs[: 1 + parts]
    there = refs[1 + parts :] if fresh else refs[1 + parts + outs :]
    kernel(*here, *there[:outs])
    there[outs][...] = jnp.zeros_like(there[outs])


def place(kernel, layer, where, parts, outs, held, after=()):
    ins = (where, *parts, *(held or ()))
    specs = [SCALARS] + [WHOLE] * len(parts) + [FAR] * len(held or ())

    def layer_block(out):
        return pl.BlockSpec((1, *out.shape[1:]), lambda _: (layer, 0, 0))

    aliases = {} if held is None else {1 + len(parts) + i: i for i in range(len(outs))}
    return call(
        functools.partial(place_kernel, kernel, held is None, len(parts), len(outs)),
        [*outs, shaped((8, 128), F32)],
        ins,
        48,
        in_specs=specs,
        out_specs=[layer_block(out) for out in outs]
        + [pl.BlockSpec((8, 128), lambda _: (0, 0))],
        input_output_aliases=aliases,
        grid=(1,),
        after=after,
    )


def positions(deal_row, ctx_count):
    row_ids = jnp.arange(RUN, dtype=jnp.int32)
    block_ids = deal_row[..., None]
    lower_block = block_ids * HALF + row_ids
    upper_block = (2 * ctx_count - 1 - block_ids) * HALF + row_ids - HALF
    continued = 2 * HALF * ctx_count + row_ids - 2 * HALF
    return jnp.where(
        row_ids < HALF, lower_block, jnp.where(row_ids < 2 * HALF, upper_block, continued)
    )


def per_device(
    tokens,
    assign,
    cotangent,
    attn_gain,
    w_query,
    w_key,
    w_value,
    w_out,
    mlp_gain,
    w_gate,
    w_up,
    w_down,
):
    ctx_count = lax.axis_size("ctx")
    wt_count = lax.axis_size("wt")
    ctx_index = lax.axis_index("ctx")
    pair = ctx_index % 2
    side = (ctx_index // SIDE) % 2
    row = (ctx_index // ROW) % 2
    quarter = 2 * side + row
    chip = ctx_index // 2
    chip_count = ctx_count // 2
    outer_bits = [bit for bit in (8, 16, 32, 64, 128) if bit < ctx_count]

    layer_count, depth = attn_gain.shape[0], w_query.shape[1]
    width = w_out.shape[2]
    half_width = width // 2
    ff_block = w_down.shape[1] // 2
    ff_piece = ff_block // 4
    half_depth = depth // 2

    def flip(value, bit, axis="ctx", count=None):
        count = ctx_count if count is None else count
        return lax.ppermute(value, axis, [(i, i ^ bit) for i in range(count)])

    def ordered(bit_value, mine, other):
        first = jnp.where(bit_value == 0, mine, other)
        second = jnp.where(bit_value == 0, other, mine)
        return first, second

    def pair_rows(own):
        first, second = ordered(pair, own, flip(own, PAIR))
        cut = 2 * HALF
        return jnp.concatenate([first[cut:], second[cut:], first[:cut], second[:cut]], axis=0)

    def own_rows(both):
        return jnp.concatenate(
            [
                lax.dynamic_slice(both, (TAIL + 2 * HALF * pair, 0), (2 * HALF, width)),
                lax.dynamic_slice(both, (CONT * pair, 0), (CONT, width)),
            ],
            axis=0,
        )

    every_pos = positions(assign[0], ctx_count).reshape(chip_count, 2, RUN)
    key_bits = [ROW, SIDE] + outer_bits
    steps = [0]
    for bit in key_bits:
        steps += [step ^ (bit // 2) for step in steps]
    wanted = chip ^ jnp.array(steps, dtype=jnp.int32)
    picked = wanted[:, None] == jnp.arange(chip_count, dtype=jnp.int32)[None, :]
    prompt_pos = jnp.sum(
        jnp.where(picked[:, :, None, None], every_pos[None, :, :, : 2 * HALF], 0), axis=1
    )
    key_pos = prompt_pos.reshape(-1, 1)
    row_pos = prompt_pos[0].reshape(1, -1)
    cont_pos = every_pos[0, 0, 2 * HALF :]
    own_pos = jnp.concatenate([cont_pos, cont_pos, row_pos[0]])
    half_dim = HEAD_DIM // 2
    frequency = jnp.exp(jnp.arange(half_dim, dtype=F32) * (-jnp.log(10000.0) / half_dim))
    phase = frequency[:, None] * own_pos.astype(F32)[None, :]
    cosine, sine = jnp.cos(phase), jnp.sin(phase)

    gain_line = jnp.concatenate([attn_gain, mlp_gain]).reshape(1, -1)
    columns = QKV + half_width
    plane = lax.axis_index("wt")
    ids = jnp.stack([quarter, plane, pair, row, side])
    ff_weights = (w_gate, w_up, w_down)

    gain_row = jnp.pad(gain_line, ((0, 0), (0, columns - gain_line.shape[1])))

    def attn_gather(layer):
        local, piece = local_weights(layer, ids, gain_row, (w_key, w_value, w_query, w_out))
        return local, lax.all_gather(piece, "wt", axis=0, tiled=False)

    def attn_weights(local, mine, other, after):
        both = join(ids, local, mine, other, after)
        keep = lax.dynamic_slice(both, (QUERY_HALF * pair, QKV), (QUERY_HALF, half_width))
        send = lax.dynamic_slice(both, (QUERY_HALF * (1 - pair), QKV), (QUERY_HALF, half_width))
        out_w = jnp.concatenate(ordered(pair, keep, flip(send, PAIR)), axis=1)
        return both[:, :QKV], out_w

    def mlp_gather(layer):
        piece = pack(layer, ids, ff_weights)
        return lax.all_gather(piece, "wt", axis=0, tiled=False)

    def mlp_spread(line, ahead, bit):
        first, last = line
        by_row, by_side = ahead or (flip(first, ROW), flip(first, SIDE))
        last_by_row, last_by_side = flip(last, ROW), flip(last, SIDE)
        across = (
            flip(by_row[0], SIDE),
            flip(by_row[1], SIDE) if bit == SIDE else flip(by_side[1], ROW),
            flip(last_by_row[0, :half_depth], SIDE),
            flip(last_by_side[0, half_depth:], ROW),
        )
        return by_row, last_by_row, by_side, last_by_side, *across

    where = jnp.stack([pair, quarter])

    residual = pair_rows(tokens[0]).astype(F32)
    parts = ()
    saved_layers = []
    attn_sets, ff_sets = [], []
    for layer in range(layer_count):
        attn_sets.append(attn_gather(layer))
        ff_sets.append(mlp_gather(layer))
    lines = attn_sets[0][1][:, half_depth, : gain_line.shape[1]].astype(F32)
    gains = (
        lines.reshape(wt_count, 2 * layer_count, depth)
        .transpose(1, 0, 2)
        .reshape(2 * layer_count, 1, wt_count * depth)
    )
    attn_other = flip(others(ids, attn_sets[0][1], half_depth, 0, 3), ROW)
    for layer in range(layer_count):
        last = layer + 1 == layer_count
        local, mine = attn_sets[layer]
        qkv_w, out_w = attn_weights(local, mine, attn_other, ())
        gain_attn, gain_mlp = gains[layer], gains[layer_count + layer]
        residual, normed_attn = add_norm(residual, parts, gain_attn)
        ahead = tuple(flip(early, bit) for bit in (ROW, SIDE)) if layer else ()
        query, key_value, key_value_turned = rope(
            dot_tt(qkv_w, normed_attn), cosine, sine, ahead
        )
        shared = key_value[TAIL:]
        for bit in key_bits:
            shared = jnp.concatenate([shared, flip(shared, bit)], axis=0)
        first = early if layer else others(ids, ff_sets[layer], depth, 0, 2, (shared,))
        line = (first, others(ids, ff_sets[layer], depth, 2, 3, (shared,)))
        spread = mlp_spread(line, ahead, ROW if layer else SIDE)
        attended, lse = attend(
            query, key_value, key_value_turned, shared, key_pos, row_pos, line
        )
        part = dot_tn(attended, out_w).astype(BF16)
        residual_mid, normed_mlp = add_norm(residual, (part, flip(part, PAIR)), gain_mlp)
        late = ()
        if layer + 1 < layer_count:
            next_attn = attn_sets[layer + 1][1]
            attn_other = flip(others(ids, next_attn, half_depth, 0, 3, (attended,)), ROW)
            late = (attn_other,)
        ff_w, down_w, slope, scale, unit, part = mlp(
            layer,
            ids,
            normed_mlp,
            (ff_sets[layer], *spread),
            ff_weights,
            ff_block,
            late,
            0 if layer + 1 == layer_count else 5,
        )
        parts = (part, flip(part, PAIR))
        if layer + 1 < layer_count:
            early = others(ids, ff_sets[layer + 1], depth, 0, 2, (part,))
        saved_layers.append(
            (
                qkv_w,
                out_w,
                ff_w,
                down_w,
                gain_attn,
                gain_mlp,
                residual,
                normed_attn,
                query,
                key_value,
                key_value_turned,
                shared,
                lse,
                attended,
                residual_mid,
                normed_mlp,
                slope,
                scale,
                unit,
            )
        )
        residual = residual_mid
    residual = residual + (parts[0].astype(F32) + parts[1].astype(F32))
    layer_out = own_rows(residual)

    def outer_sum(total):
        for bit in outer_bits:
            total = add(total, flip(total, bit), steps=1)
        return total

    def sum_ff(share, after=()):
        cut = 2 * ff_block
        totals = cross(share, flip(share[:, :cut], ROW), flip(share[:, cut:], SIDE), after)
        return [outer_sum(total) for total in totals]

    def spread_ff(totals):
        gate, up = totals
        gates, ups = [gate, flip(gate, SIDE)], [up, flip(up, ROW)]
        for group in (gates, ups):
            group += [flip(part, PAIR) for part in group]
        return gates + ups

    def sum_rows(share, cut, after=()):
        totals = split_sum(
            share, flip(share[:, :cut], SIDE), flip(share[:, cut:], ROW), after
        )
        return [outer_sum(total) for total in totals]

    def spread_rows(totals):
        by_row, by_side = totals
        joined = order(ids, (by_row, flip(by_row, ROW), by_side, flip(by_side, SIDE)))
        return [joined, flip(joined, PAIR)]

    down_cut, attn_cut = 640, 768

    def scatter(total):
        return lax.psum_scatter(total, "wt", scatter_dimension=0, tiled=total.ndim == 2)

    flow = pair_rows(cotangent[0])
    flow, flow_low = flow.astype(F32), flow
    gain_grads = [None] * (2 * layer_count)
    ff_outs, attn_outs = (
        [shaped((layer_count, *weight.shape[1:]), F32) for weight in group]
        for group in ((w_gate, w_up, w_down), (w_query, w_key, w_value, w_out))
    )
    ff_held = attn_held = None
    shares = {}
    for layer in reversed(range(layer_count)):
        (
            qkv_w,
            out_w,
            ff_w,
            down_w,
            gain_attn,
            gain_mlp,
            residual,
            normed_attn,
            query,
            key_value,
            key_value_turned,
            shared,
            lse,
            attended,
            residual_mid,
            normed_mlp,
            slope,
            scale,
            unit,
        ) = saved_layers[layer]
        older = shares.get(layer + 1)
        row_keep, row_send, side_keep, side_send = down_grad(ids, unit, flow_low, down_cut)
        down_parts = (row_keep, flip(row_send, ROW)), (side_keep, flip(side_send, SIDE))
        done = (row_keep,) if older is None else (row_keep, attn_all)
        gate_keep, gate_send, up_keep, up_send, part = mlp_back(
            flow_low, normed_mlp, slope, scale, down_w, ff_w, after=done
        )
        gate_got, up_got = flip(gate_send, SIDE), flip(up_send, ROW)
        done = () if older is None else (older["ff"],)
        part, down_sum = add_two(*down_parts, done, part)
        done = (down_sum,)
        flow, flow_low, gain_grads[layer_count + layer] = norm_back(
            flow, (part, flip(part, PAIR)), residual_mid, gain_mlp, after=done, pinned=True
        )
        attended_grad = dot_nt(out_w, flow_low).astype(BF16)
        query_grad, own_grad, shared_grad = attend_back(
            query,
            attended_grad,
            key_value,
            key_value_turned,
            shared,
            key_pos,
            row_pos,
            lse,
            cosine,
            sine,
        )
        for bit in reversed(key_bits):
            half = shared_grad.shape[0] // 2
            arrived = flip(shared_grad[half:].astype(BF16), bit)
            shared_grad = shared_grad[:half] + arrived.astype(F32)
            if bit == key_bits[-1]:
                started = shared_grad
        shares[layer] = {"down": scatter(down_sum)}
        done = (started, shares[layer]["down"])
        if older is not None:
            done = (*done, older["attn"])
        ff_sum = add_two((gate_keep, gate_got), (up_keep, up_got), done)
        shares[layer]["ff"] = scatter(ff_sum)
        down_totals = sum_rows(shares[layer]["down"], down_cut, (ff_sum,))
        done = (ff_sum, down_totals[0])
        if older is not None:
            ff_totals = sum_ff(older["ff"], (ff_sum,))
            attn_totals = sum_rows(older["attn"], attn_cut, (ff_sum,))
            done = (*done, ff_totals[0], attn_totals[0])
        grad_qkv = merge(query_grad, own_grad, shared_grad, cosine, sine, done)
        part = dot_nt(grad_qkv, qkv_w).astype(BF16)
        shares[layer]["down"] = spread_rows(down_totals)
        done = (shares[layer]["down"][0],)
        if older is not None:
            older["ff"] = spread_ff(ff_totals)
            older["attn"] = spread_rows(attn_totals)
            done = (*done, older["ff"][1], older["ff"][5], older["attn"][0])
        row_keep, row_send, side_keep, side_send = attn_grad(
            ids, normed_attn, grad_qkv, attended, flow_low, attn_cut, done
        )
        if older is None:
            done = (layer_out,)
        else:
            *ff_held, placed = place(
                place_ff_kernel,
                layer + 1,
                where,
                older["ff"] + older["down"],
                ff_outs,
                ff_held,
                (row_keep,),
            )
            *attn_held, attn_placed = place(
                place_attn_kernel, layer + 1, where, older["attn"], attn_outs, attn_held, (row_keep,)
            )
            done = (placed, attn_placed)
        attn_mine, send = attn_sum(
            pair[None],
            (row_keep, flip(row_send, ROW), side_keep, flip(side_send, SIDE)),
            done,
        )
        done = (attn_mine,)
        flow, flow_low, gain_grads[layer] = norm_back(
            flow, (part, flip(part, PAIR)), residual, gain_attn, after=done
        )
        attn_all = attn_join(pair[None], attn_mine, flip(send, PAIR))
        shares[layer]["attn"] = scatter(attn_all)
    ff_totals = sum_ff(shares[0]["ff"], (attn_all,))
    gain_total = jnp.concatenate(gain_grads, axis=0)
    for bit in [SIDE, ROW] + outer_bits:
        gain_total = gain_total + flip(gain_total, bit)
    bit = 1
    while bit < wt_count:
        gain_total = gain_total + flip(gain_total, bit, "wt", wt_count)
        bit *= 2
    ff = spread_ff(ff_totals)
    *ff_held, placed = place(
        place_ff_kernel, 0, where, ff + shares[0]["down"], ff_outs, ff_held, (gain_total,)
    )
    attn_totals = sum_rows(shares[0]["attn"], attn_cut, (placed,))
    *attn_held, _ = place(
        place_attn_kernel, 0, where, spread_rows(attn_totals), attn_outs, attn_held
    )
    query_out, key_out, value_out, out_out = attn_held
    gate_out, up_out, down_out = ff_held
    token_grad = own_rows(flow)

    gain_share = lax.dynamic_slice(
        gain_total, (0, lax.axis_index("wt") * depth), (2 * layer_count, depth)
    )
    return (
        layer_out[None],
        token_grad[None],
        gain_share[:layer_count],
        query_out,
        key_out,
        value_out,
        out_out,
        gain_share[layer_count:],
        gate_out,
        up_out,
        down_out,
    )


def solution(mesh):
    weight = P(None, "wt", None)
    return jax.shard_map(
        per_device,
        mesh=mesh,
        in_specs=(
            P("wt", "ctx", None),
            P("wt", None),
            P("wt", "ctx", None),
            P(None, "wt"),
            weight,
            weight,
            weight,
            weight,
            P(None, "wt"),
            weight,
            weight,
            weight,
        ),
        out_specs=(
            P("wt", "ctx", None),
            P("wt", "ctx", None),
            P(None, "wt"),
            weight,
            weight,
            weight,
            weight,
            P(None, "wt"),
            weight,
            weight,
            weight,
        ),
        check_vma=False,
    )
```
